256 devices in a mesh: dp: 8 (over z), expert: 32 (over x, y, core).
Axes of the slice: x: 4, y: 4, z: 8, core: 2. Of those that a mesh axis runs over, the one named last changes fastest.
Arguments:
- tokens: bfloat16 [32768, 2048], P(('dp', 'expert')), parts along dimension 0, may hold values from -6 to 6
- expert_ids: int32 [32768, 8], P(('dp', 'expert')), parts along dimension 0, may hold values from 0 to 31, all different within a row; in each aligned block of 128 rows (0 to 127, 128 to 255, ...) at most 40 rows name the same one
- gate_weights: float32 [32768, 8], P(('dp', 'expert')), parts along dimension 0, may hold values from 0.1 to 1
- w_gate: bfloat16 [32, 2048, 768], P('expert'), may hold values from -0.125 to 0.125
- w_up: bfloat16 [32, 2048, 768], P('expert'), may hold values from -0.125 to 0.125
- w_down: bfloat16 [32, 768, 2048], P('expert'), may hold values from -0.21875 to 0.21875
Outputs:
- mixed: bfloat16 [32768, 2048], P(('dp', 'expert')), parts along dimension 0
The draws below stay inside these ranges and needn't reach their ends.
There are 8 independent parts, one for each index of `dp`. The reference program is written for one: setup_inputs(seed, part) draws one part's arguments, and reference() takes and returns one part's arrays. A program takes and returns all parts, laid end to end along the dimension named above; an argument that names none is the same for every part. Nothing has to cross between parts.
Inputs may be any that keep to these rules, and one draw needn't show every extreme that they name: `expert_ids`: each row names 8 different experts. In each aligned block of 128 rows (the rows of one device) no expert is named by more than 40 rows, a bound that some block reaches.
All inputs are finite; a program needn't handle non-finite values.
Results may differ from the reference program's by a relative error of at most 0.0058.
Values may be sent and summed in bfloat16 or wider, within the bound.
No kernel may reach another device: no remote copies, remote signals or barrier semaphores. Data moves between devices by JAX's collectives and lax.ppermute only.
A program may use at most 64 MiB of HBM per device.

```python
import math
import jax
import jax.numpy as jnp
import numpy as np
from jax import lax

D = 2048
FF = 768
TOP = 8
TOK_DEV = 128
EXPERTS = 32
CAP = 40
TOKENS = 4096
N_EXPERT = 32


def block_scale(own_key, extent, split, low, largest):
    def one(dim, shards_of):
        draws = jax.random.uniform(jax.random.fold_in(jax.random.fold_in(own_key, 6), dim), (shards_of,), jnp.float32, low / len(split), largest / len(split))
        return jnp.repeat(jnp.exp(draws), extent[dim] // shards_of).reshape((-1,) + (1,) * (len(extent) - dim - 1))

    loudness = one(*split[0])
    for cut in split[1:]:
        loudness = loudness * one(*cut)
    return loudness


def shared_out(key, own, number, rows, count, top, bound, slope):
    order = jax.random.permutation(key, count)
    heavy_load, usual = portions_of(count, rows * top, bound, slope, True), portions_of(count, rows * top, bound, slope, False)
    places = jnp.arange(count)

    def named(sizes, offset_by):
        used = int((sizes > 0).sum())
        fixed = max(1, used // 4)
        passed = fixed + (places - fixed + offset_by * (used - fixed)) % max(1, count - fixed)
        return jnp.zeros((count,), jnp.int32).at[order[jnp.where(places < fixed, places, passed)]].set(jnp.asarray(sizes, jnp.int32))

    sizes = jnp.where(number % 4 == 0, named(heavy_load, number // 4), named(usual, number - number // 4 - 1))
    mixed = jax.random.permutation(jax.random.fold_in(own, 3), count)
    source_of, sink = mixed[0:count // 2 * 2:2], mixed[1:count // 2 * 2:2]
    margin = jnp.minimum(sizes[source_of] - 1, bound - sizes[sink]) // 2
    margin = jnp.where((source_of == order[0]) | (sink == order[0]) | (sizes[sink] == 0), 0, jnp.maximum(margin, 0))
    passed = jax.random.randint(jax.random.fold_in(own, 4), (count // 2,), 0, 1 << 20) % (margin + 1)
    sizes = sizes.at[source_of].add(-passed).at[sink].add(passed)
    items = jnp.searchsorted(jnp.cumsum(sizes), jnp.arange(rows * top), side="right").astype(jnp.int32)
    table = items.reshape(top, rows).T
    table = table[jax.random.permutation(jax.random.fold_in(own, 1), rows)]
    offset_by = jax.random.randint(jax.random.fold_in(own, 2), (rows, 1), 0, top)
    return jnp.take_along_axis(table, (jnp.arange(top)[None, :] + offset_by) % top, axis=1)


def portions_of(amount, total, reach, lean, full):
    portions = [(1 << 20) // math.isqrt(grade ** lean) + 1 for grade in range(1, amount + 1)]
    largest = reach if full else min(reach, max(-(-total // amount), total * portions[0] // sum(portions)))
    least = 1 if total - largest >= amount - 1 else 0
    given, rest = [largest] + [least] * (amount - 1), total - largest - least * (amount - 1)
    while rest > 0:
        free = [i for i in range(1, amount) if given[i] < largest] or [i for i in range(1, amount) if given[i] < reach]
        mass, budget = sum([portions[i] for i in free]), rest
        for i in free:
            more = min(reach - given[i], max(1, budget * portions[i] // mass), rest)
            given[i] = given[i] + more
            rest = rest - more
    return np.array(given)


def scatter_about(key, shape, width, reach, pieces=(), kind=jnp.bfloat16):
    gain = block_scale(key, shape, pieces, -0.22, 0.18) if pieces else 1.0
    entries = jax.random.normal(key, shape, jnp.float32) * width * gain
    return jnp.minimum(jnp.maximum(entries, -reach), reach).astype(kind)


def setup_inputs(seed: int = 0, part: int = 0) -> dict:
    splits = jax.random.split(jax.random.key(seed), 7)
    part_splits = jax.random.split(jax.random.fold_in(splits[6], part), 7)
    tokens = scatter_about(part_splits[0], (TOKENS, D), 1.0, 6.0, ((0, 32),))
    expert_ids_keys = jax.random.split(jax.random.fold_in(part_splits[1], 1), TOKENS // TOK_DEV)
    expert_ids_turns = jax.random.permutation(jax.random.fold_in(part_splits[1], 3), TOKENS // TOK_DEV)
    expert_ids = jax.vmap(lambda own, number: shared_out(jax.random.fold_in(part_splits[1], 2), own, number, TOK_DEV, EXPERTS, TOP, CAP, 2))(expert_ids_keys, expert_ids_turns).reshape((TOKENS, TOP))
    gate_weights = jnp.clip(jnp.exp(math.log(1.0) - 2.3025851 * jax.random.uniform(part_splits[2], (TOKENS, TOP), jnp.float32) ** block_scale(part_splits[2], (TOKENS, TOP), ((0, 32),), -0.2, 0.2)), 0.1, 1.0)
    w_gate = scatter_about(splits[3], (EXPERTS, D, FF), D ** -0.5, 0.125, ((0, 32),))
    w_up = scatter_about(splits[4], (EXPERTS, D, FF), D ** -0.5, 0.125, ((0, 32),))
    w_down = scatter_about(splits[5], (EXPERTS, FF, D), FF ** -0.5, 0.21875, ((0, 32),))
    return {"tokens": tokens, "expert_ids": expert_ids, "gate_weights": gate_weights, "w_gate": w_gate, "w_up": w_up, "w_down": w_down}


def reference(tokens, expert_ids, gate_weights, w_gate, w_up, w_down):
    sources = N_EXPERT
    per_block = TOK_DEV * TOP
    flat_ids = expert_ids.reshape(sources, per_block).astype(jnp.int32)
    choose = (flat_ids[:, :, None] == jnp.arange(EXPERTS, dtype=jnp.int32)[None, None, :]).astype(jnp.int32)
    ranks = jnp.cumsum(choose, axis=1) - choose
    slot_ids = jnp.sum(ranks * choose, axis=2).astype(jnp.int32)
    source_ids = jnp.broadcast_to(jnp.arange(sources, dtype=jnp.int32)[:, None], (sources, per_block))
    token_rows = jnp.repeat(tokens.reshape(sources, TOK_DEV, D), TOP, axis=1)
    dispatch = jnp.zeros((EXPERTS, sources, CAP, D), jnp.bfloat16)
    dispatch = dispatch.at[flat_ids, source_ids, slot_ids].set(token_rows)

    def expert_apply(packed):
        held, gate_mat, up_mat, down_mat = packed
        lines = held.reshape(sources * CAP, D)
        gate_part = jnp.dot(lines, gate_mat, preferred_element_type=jnp.float32)
        up_part = jnp.dot(lines, up_mat, preferred_element_type=jnp.float32)
        hidden = (jax.nn.silu(gate_part) * up_part).astype(jnp.bfloat16)
        answer = jnp.dot(hidden, down_mat, preferred_element_type=jnp.float32).astype(jnp.bfloat16)
        return answer.reshape(sources, CAP, D)

    answers = lax.map(expert_apply, (dispatch, w_gate, w_up, w_down))
    picked = answers[flat_ids, source_ids, slot_ids]
    weighted = picked.astype(jnp.float32) * gate_weights.reshape(sources, per_block)[:, :, None]
    mixed = jnp.sum(weighted.reshape(TOKENS, TOP, D), axis=1)
    return mixed.astype(jnp.bfloat16)
```

```python
import functools

import jax
import jax.numpy as jnp
from jax import lax
from jax.experimental import pallas as pl
from jax.experimental.pallas import tpu as pltpu
from jax.sharding import PartitionSpec as P

NX, NY, NC = 4, 4, 2
EXPERTS = NX * NY * NC
CAP = 40
META = 16
KF = 8


def index_of(x, y, c):
    return ((x % NX) * NY + (y % NY)) * NC + c


def spread_pairs(j):
    pairs = []
    for x in range(NX):
        for y in range(NY):
            pairs.append((index_of(x, y, 0), index_of(x + j, y, 0)))
            pairs.append((index_of(x, y, 1), index_of(x, y + j, 1)))
    return pairs


def deliver_pairs(k, f):
    pairs = []
    for x in range(NX):
        for y in range(NY):
            pairs.append((index_of(x, y, 0), index_of(x, y + k, f)))
            pairs.append((index_of(x, y, 1), index_of(x + k, y, 1 - f)))
    return pairs


def back(pairs):
    return [(b, a) for a, b in pairs]


def prep_kernel(tok_ref, ids_ref, gw_ref, out_ref):
    tok, top = ids_ref.shape
    lanes = 128
    ids = ids_ref[...]
    gw = gw_ref[...]
    lane = lax.broadcasted_iota(jnp.int32, (tok, lanes), 1)
    chosen = jnp.zeros((tok, lanes), jnp.float32)
    weight = jnp.zeros((tok, lanes), jnp.float32)
    for k in range(top):
        hit = ids[:, k : k + 1] == lane
        chosen = jnp.where(hit, 1.0, chosen)
        weight = jnp.where(hit, gw[:, k : k + 1], weight)
    row = lax.broadcasted_iota(jnp.int32, (tok, tok), 0)
    col = lax.broadcasted_iota(jnp.int32, (tok, tok), 1)
    earlier = jnp.where(col < row, 1.0, 0.0).astype(jnp.bfloat16)
    count = jnp.dot(earlier, chosen.astype(jnp.bfloat16), preferred_element_type=jnp.float32)
    slot = jnp.where(chosen > 0.5, count, -1.0)
    slot_t = slot.T
    weight_t = weight.T
    half = EXPERTS // 2
    meta = jnp.concatenate(
        [slot_t[:half], slot_t[half:EXPERTS], weight_t[:half], weight_t[half:EXPERTS]], axis=1
    ).astype(jnp.bfloat16)
    out_ref[:tok, :] = tok_ref[...]
    out_ref[tok:, : 4 * tok] = meta
    out_ref[tok:, 4 * tok :] = jnp.zeros((META, out_ref.shape[1] - 4 * tok), jnp.bfloat16)


def prep(tokens, ids, gw):
    tok, width = tokens.shape
    return pl.pallas_call(
        prep_kernel,
        out_shape=jax.ShapeDtypeStruct((tok + META, width), jnp.bfloat16),
        cost_estimate=pl.CostEstimate(flops=2 * tok**3, bytes_accessed=4 * tok * width, transcendentals=0),
        name="prep",
    )(tokens, ids, gw)


def select(q, meta, at, tok):
    half = EXPERTS // 2
    return jnp.dot(
        q[:, :half], meta[:, at : at + tok], preferred_element_type=jnp.float32
    ) + jnp.dot(q[:, half:], meta[:, at + tok : at + 2 * tok], preferred_element_type=jnp.float32)


def pack_kernel(q_ref, m0, m1, m2, m3, b0, b1, b2, b3, *outs):
    tok = b0.shape[0]
    q = q_ref[...]
    r = lax.broadcasted_iota(jnp.int32, (2 * CAP, 2 * tok), 0)
    t = lax.broadcasted_iota(jnp.int32, (2 * CAP, 2 * tok), 1)
    second = r >= CAP
    target = jnp.where(second, r - CAP, r)
    target = jnp.where(second == (t >= tok), target, -5).astype(jnp.float32)
    for p, (ma, mb, ba, bb) in enumerate(((m0, m1, b0, b1), (m2, m3, b2, b3))):
        slots = jnp.concatenate([select(q, m[...], 0, tok) for m in (ma, mb)], axis=1)
        rows = [
            jnp.where(slots[n : n + 1, :] == target, 1.0, 0.0).astype(jnp.bfloat16) for n in range(KF)
        ]
        pick = jnp.concatenate(rows, axis=0)
        block = jnp.concatenate([ba[...], bb[...]], axis=0)
        got = jnp.dot(pick, block, preferred_element_type=jnp.float32).astype(jnp.bfloat16)
        for n in range(KF):
            outs[n][2 * CAP * p : 2 * CAP * (p + 1), :] = got[2 * CAP * n : 2 * CAP * (n + 1), :]


def pack(q, blocks):
    rows, width = blocks[0].shape
    tok = rows - META
    cols = 512
    metas = pl.BlockSpec((META, 4 * tok), lambda i: (tok // META, 0))
    body = pl.BlockSpec((tok, cols), lambda i: (0, i))
    return pl.pallas_call(
        pack_kernel,
        grid=(width // cols,),
        in_specs=[pl.BlockSpec(q.shape, lambda i: (0, 0))] + [metas] * 4 + [body] * 4,
        out_specs=[pl.BlockSpec((4 * CAP, cols), lambda i: (0, i))] * KF,
        out_shape=[jax.ShapeDtypeStruct((4 * CAP, width), jnp.bfloat16)] * KF,
        cost_estimate=pl.CostEstimate(
            flops=2 * 2 * 640 * 256 * width, bytes_accessed=1800 * width * 2, transcendentals=0
        ),
        name="pack",
    )(q, *blocks, *blocks)


def combine_kernel(q_ref, m0, m1, m2, m3, *refs):
    backs, (own, o1, o2, o3) = refs[:KF], refs[KF:]
    tok = own.shape[0]
    q = q_ref[...]
    span = 2 * CAP * KF
    lane = lax.broadcasted_iota(jnp.int32, (2 * tok, span), 1)
    part = jnp.zeros((2 * tok, span), jnp.int32)
    for n in range(1, KF):
        part = jnp.where(lane >= 2 * CAP * n, 2 * CAP * n, part)
    r = lane - part
    t = lax.broadcasted_iota(jnp.int32, (2 * tok, span), 0)
    second = r >= CAP
    target = jnp.where(second, r - CAP, r)
    target = jnp.where(second == (t >= tok), target, -5).astype(jnp.float32)
    er = lax.broadcasted_iota(jnp.int32, (16, span), 0)
    el = lax.broadcasted_iota(jnp.int32, (16, span), 1)
    ep = jnp.zeros((16, span), jnp.int32)
    for n in range(1, KF):
        ep = jnp.where(el >= 2 * CAP * n, n, ep)
    expand = jnp.where(er == ep, 1.0, 0.0).astype(jnp.bfloat16)

    def widen(v):
        return lax.dot_general(
            v.astype(jnp.bfloat16), expand, (((0,), (0,)), ((), ())), preferred_element_type=jnp.float32
        )

    for p, (ma, mb, oa, ob) in enumerate(((m0, m1, own, o1), (m2, m3, o2, o3))):
        slots = jnp.concatenate([select(q, m[...], 0, tok) for m in (ma, mb)], axis=1)
        weights = jnp.concatenate([select(q, m[...], 2 * tok, tok) for m in (ma, mb)], axis=1)
        mix = jnp.where(widen(slots) == target, widen(weights), 0.0).astype(jnp.bfloat16)
        rows = jnp.concatenate([b[2 * CAP * p : 2 * CAP * (p + 1), :] for b in backs], axis=0)
        got = jnp.dot(mix, rows, preferred_element_type=jnp.float32)
        oa[...] = got[:tok].astype(oa.dtype)
        ob[...] = got[tok:].astype(ob.dtype)


def combine(q, blocks, backs):
    rows, width = blocks[0].shape
    tok = rows - META
    cols = 512
    metas = pl.BlockSpec((META, 4 * tok), lambda i: (tok // META, 0))
    out = pl.BlockSpec((tok, cols), lambda i: (0, i))
    return pl.pallas_call(
        combine_kernel,
        grid=(width // cols,),
        in_specs=[pl.BlockSpec(q.shape, lambda i: (0, 0))]
        + [metas] * 4
        + [pl.BlockSpec((4 * CAP, cols), lambda i: (0, i))] * KF,
        out_specs=[out] * 4,
        out_shape=[jax.ShapeDtypeStruct((tok, width), jnp.float32)]
        + [jax.ShapeDtypeStruct((tok, width), jnp.bfloat16)] * 3,
        cost_estimate=pl.CostEstimate(
            flops=2 * 2 * 640 * 256 * width, bytes_accessed=1800 * width * 2, transcendentals=0
        ),
        name="combine",
    )(q, *blocks, *backs)


def expert_kernel(count, *refs):
    slabs, (wg, wu, wd), outs, total = refs[:count], refs[count : count + 3], refs[count + 3 : -1], refs[-1]
    step = pl.program_id(0)
    lines = jnp.concatenate([s[...] for s in slabs], axis=0)
    gate = jnp.dot(lines, wg[...], preferred_element_type=jnp.float32)
    up = jnp.dot(lines, wu[...], preferred_element_type=jnp.float32)
    hidden = (gate / (1.0 + jnp.exp(-gate)) * up).astype(jnp.bfloat16)
    add = jnp.dot(hidden, wd[...], preferred_element_type=jnp.float32)

    @pl.when(step == 0)
    def _():
        total[...] = add

    @pl.when(step > 0)
    def _():
        total[...] += add

    @pl.when(step == pl.num_programs(0) - 1)
    def _():
        rows = slabs[0].shape[0]
        for n, o in enumerate(outs):
            o[...] = total[n * rows : (n + 1) * rows, :].astype(jnp.bfloat16)


def expert(slabs, w_gate, w_up, w_down):
    count = len(slabs)
    rows, width = slabs[0].shape
    ff = w_gate.shape[-1]
    tile = 256
    whole = pl.BlockSpec((rows, width), lambda i: (0, 0))
    into = pl.BlockSpec((None, width, tile), lambda i: (0, 0, i))
    down = pl.BlockSpec((None, tile, width), lambda i: (0, i, 0))
    return pl.pallas_call(
        functools.partial(expert_kernel, count),
        grid=(ff // tile,),
        in_specs=[whole] * count + [into, into, down],
        out_specs=[whole] * count,
        out_shape=[jax.ShapeDtypeStruct((rows, width), jnp.bfloat16)] * count,
        scratch_shapes=[pltpu.VMEM((count * rows, width), jnp.float32)],
        compiler_params=pltpu.CompilerParams(vmem_limit_bytes=48 * 1024 * 1024),
        cost_estimate=pl.CostEstimate(
            flops=6 * count * rows * width * ff,
            bytes_accessed=6 * width * ff + 4 * count * rows * width,
            transcendentals=count * rows * ff,
        ),
        name="expert",
    )(*slabs, w_gate, w_up, w_down)


def per_device(tokens, expert_ids, gate_weights, w_gate, w_up, w_down):
    me = lax.axis_index("expert")
    x, y, c = me // (NY * NC), (me // NC) % NY, me % NC
    n = jnp.arange(16, dtype=jnp.int32)
    k, f = n // NC, n % NC
    along_y = x * (NY * NC) + ((y + k) % NY) * NC + (c ^ f)
    along_x = ((x + k) % NX) * (NY * NC) + y * NC + (c ^ f)
    mine = jnp.where(n < KF, jnp.where(c == 0, along_y, along_x), -1)
    q = (mine[:, None] == jnp.arange(EXPERTS, dtype=jnp.int32)[None, :]).astype(jnp.bfloat16)

    send = lambda v, pairs: lax.ppermute(v, "expert", pairs)
    home = prep(tokens, expert_ids, gate_weights)
    blocks = [home] + [send(home, spread_pairs(j)) for j in (1, 2, 3)]
    packed = pack(q, blocks)
    arrived = {}
    for k in (1, 3, 2, 0):
        for f in (0, 1):
            slab = packed[NC * k + f]
            arrived[k, f] = slab if (k, f) == (0, 0) else send(slab, deliver_pairs(k, f))
    answers = {}
    for group in (((0, 0), (0, 1)), ((1, 0), (1, 1), (3, 0), (3, 1)), ((2, 0), (2, 1))):
        done = expert([arrived[g] for g in group], w_gate, w_up, w_down)
        answers.update(zip(group, done))
    backs = []
    for k in range(4):
        for f in (0, 1):
            slab = answers[k, f]
            backs.append(slab if (k, f) == (0, 0) else send(slab, back(deliver_pairs(k, f))))
    parts = combine(q, blocks, backs)
    mixed = parts[0]
    for j in (1, 2, 3):
        mixed = mixed + send(parts[j], back(spread_pairs(j))).astype(jnp.float32)
    return mixed.astype(jnp.bfloat16)


def solution(mesh):
    return jax.shard_map(
        per_device,
        mesh=mesh,
        in_specs=(
            P(("dp", "expert"), None),
            P(("dp", "expert"), None),
            P(("dp", "expert"), None),
            P("expert", None, None),
            P("expert", None, None),
            P("expert", None, None),
        ),
        out_specs=P(("dp", "expert"), None),
        check_vma=False,
    )
```

```python
import functools

import jax
import jax.numpy as jnp
from jax import lax
from jax.experimental import pallas as pl
from jax.experimental.pallas import tpu as pltpu
from jax.sharding import PartitionSpec as P

NX, NY, NC = 4, 4, 2
EXPERTS = NX * NY * NC
CAP = 40
KF = 8


def index_of(x, y, c):
    return ((x % NX) * NY + (y % NY)) * NC + c


def spread_pairs(j):
    pairs = []
    for x in range(NX):
        for y in range(NY):
            pairs.append((index_of(x, y, 0), index_of(x + j, y, 0)))
            pairs.append((index_of(x, y, 1), index_of(x, y + j, 1)))
    return pairs


def deliver_pairs(k, f):
    pairs = []
    for x in range(NX):
        for y in range(NY):
            pairs.append((index_of(x, y, 0), index_of(x, y + k, f)))
            pairs.append((index_of(x, y, 1), index_of(x + k, y, 1 - f)))
    return pairs


def back(pairs):
    return [(b, a) for a, b in pairs]


def prep_kernel(ids_ref, gw_ref, out_ref):
    top, tok = ids_ref.shape
    ids = ids_ref[...]
    gw = gw_ref[...]
    name = lax.broadcasted_iota(jnp.int32, (EXPERTS, tok), 0)
    chosen = jnp.zeros((EXPERTS, tok), jnp.float32)
    weight = jnp.zeros((EXPERTS, tok), jnp.float32)
    for k in range(top):
        hit = ids[k : k + 1, :] == name
        chosen = jnp.where(hit, 1.0, chosen)
        weight = jnp.where(hit, gw[k : k + 1, :], weight)
    row = lax.broadcasted_iota(jnp.int32, (tok, tok), 0)
    col = lax.broadcasted_iota(jnp.int32, (tok, tok), 1)
    earlier = jnp.where(row < col, 1.0, 0.0).astype(jnp.bfloat16)
    count = jnp.dot(chosen.astype(jnp.bfloat16), earlier, preferred_element_type=jnp.float32)
    slot = jnp.where(chosen > 0.5, count, -1.0)
    half = EXPERTS // 2
    out_ref[...] = jnp.concatenate(
        [slot[:half], slot[half:], weight[:half], weight[half:]], axis=1
    ).astype(jnp.bfloat16)


def prep(ids, gw):
    tok = ids.shape[1]
    return pl.pallas_call(
        prep_kernel,
        out_shape=jax.ShapeDtypeStruct((EXPERTS // 2, 4 * tok), jnp.bfloat16),
        cost_estimate=pl.CostEstimate(flops=2 * EXPERTS * tok**2, bytes_accessed=32 * tok * 4, transcendentals=0),
        name="prep",
    )(ids, gw)


def select(q, meta, at, tok):
    half = EXPERTS // 2
    return jnp.dot(
        q[:, :half], meta[:, at : at + tok], preferred_element_type=jnp.float32
    ) + jnp.dot(q[:, half:], meta[:, at + tok : at + 2 * tok], preferred_element_type=jnp.float32)


def pack_kernel(which, q_ref, *refs):
    metas, blocks, outs = refs[:4], refs[4:8], refs[-len(which) :]
    tok, width = blocks[0].shape
    q = q_ref[...]
    r = lax.broadcasted_iota(jnp.int32, (2 * CAP, 2 * tok), 0)
    t = lax.broadcasted_iota(jnp.int32, (2 * CAP, 2 * tok), 1)
    second = r >= CAP
    target = jnp.where(second, r - CAP, r)
    target = jnp.where(second == (t >= tok), target, -5).astype(jnp.float32)
    cols = 512
    for p in range(2):
        slots = jnp.concatenate([select(q, m[...], 0, tok) for m in metas[2 * p : 2 * p + 2]], axis=1)
        pick = jnp.concatenate(
            [jnp.where(slots[n : n + 1, :] == target, 1.0, 0.0).astype(jnp.bfloat16) for n in which], axis=0
        )
        for at in range(0, width, cols):
            block = jnp.concatenate([b[:, at : at + cols] for b in blocks[2 * p : 2 * p + 2]], axis=0)
            got = jnp.dot(pick, block, preferred_element_type=jnp.float32).astype(jnp.bfloat16)
            for n, o in enumerate(outs):
                o[2 * CAP * p : 2 * CAP * (p + 1), at : at + cols] = got[2 * CAP * n : 2 * CAP * (n + 1), :]


def pack(which, q, metas, blocks, after=()):
    tok, width = blocks[0].shape
    count = len(which)
    vmem = pl.BlockSpec(memory_space=pltpu.VMEM)
    return pl.pallas_call(
        functools.partial(pack_kernel, which),
        in_specs=[vmem] * 9 + [pl.BlockSpec(memory_space=pl.ANY)] * len(after),
        out_specs=[vmem] * count,
        out_shape=[jax.ShapeDtypeStruct((4 * CAP, width), jnp.bfloat16)] * count,
        compiler_params=pltpu.CompilerParams(vmem_limit_bytes=24 * 1024 * 1024),
        cost_estimate=pl.CostEstimate(
            flops=2 * 4 * CAP * count * 2 * tok * width,
            bytes_accessed=2 * (4 * tok + 4 * CAP * count) * width,
            transcendentals=0,
        ),
        name="pack",
    )(q, *metas, *blocks, *after)


def combine_kernel(q_ref, *refs):
    metas, backs, outs = refs[:4], refs[4 : 4 + KF], refs[4 + KF :]
    tok, width = outs[0].shape
    q = q_ref[...]
    span = 2 * CAP * KF
    lane = lax.broadcasted_iota(jnp.int32, (2 * tok, span), 1)
    part = jnp.zeros((2 * tok, span), jnp.int32)
    er = lax.broadcasted_iota(jnp.int32, (16, span), 0)
    el = lax.broadcasted_iota(jnp.int32, (16, span), 1)
    ep = jnp.zeros((16, span), jnp.int32)
    for n in range(1, KF):
        part = jnp.where(lane >= 2 * CAP * n, 2 * CAP * n, part)
        ep = jnp.where(el >= 2 * CAP * n, n, ep)
    r = lane - part
    t = lax.broadcasted_iota(jnp.int32, (2 * tok, span), 0)
    second = r >= CAP
    target = jnp.where(second, r - CAP, r)
    target = jnp.where(second == (t >= tok), target, -5).astype(jnp.float32)
    expand = jnp.where(er == ep, 1.0, 0.0).astype(jnp.bfloat16)

    def widen(v):
        return lax.dot_general(
            v.astype(jnp.bfloat16), expand, (((0,), (0,)), ((), ())), preferred_element_type=jnp.float32
        )

    cols = 512
    for p in range(2):
        pair = metas[2 * p : 2 * p + 2]
        slots = jnp.concatenate([select(q, m[...], 0, tok) for m in pair], axis=1)
        weights = jnp.concatenate([select(q, m[...], 2 * tok, tok) for m in pair], axis=1)
        mix = jnp.where(widen(slots) == target, widen(weights), 0.0).astype(jnp.bfloat16)
        for at in range(0, width, cols):
            rows = jnp.concatenate(
                [b[2 * CAP * p : 2 * CAP * (p + 1), at : at + cols] for b in backs], axis=0
            )
            got = jnp.dot(mix, rows, preferred_element_type=jnp.float32)
            for n, o in enumerate(outs[2 * p : 2 * p + 2]):
                o[:, at : at + cols] = got[n * tok : (n + 1) * tok].astype(o.dtype)


def combine(q, metas, backs):
    tok = metas[0].shape[1] // 4
    width = backs[0].shape[1]
    vmem = pl.BlockSpec(memory_space=pltpu.VMEM)
    return pl.pallas_call(
        combine_kernel,
        in_specs=[vmem] * (5 + KF),
        out_specs=[vmem] * 4,
        out_shape=[jax.ShapeDtypeStruct((tok, width), jnp.float32)]
        + [jax.ShapeDtypeStruct((tok, width), jnp.bfloat16)] * 3,
        compiler_params=pltpu.CompilerParams(vmem_limit_bytes=24 * 1024 * 1024),
        cost_estimate=pl.CostEstimate(
            flops=2 * 2 * 2 * CAP * KF * 2 * tok * width,
            bytes_accessed=2 * (5 * tok + 4 * CAP * KF) * width,
            transcendentals=0,
        ),
        name="combine",
    )(q, *metas, *backs)


def expert_kernel(count, *refs):
    slabs, (wg, wu, wd), outs = refs[:count], refs[count : count + 3], refs[count + 3 :]
    rows, width = slabs[0].shape
    ff = wg.shape[-1]
    lines = jnp.concatenate([s[...] for s in slabs], axis=0)
    hidden = []
    for at in range(0, ff, 256):
        gate = jnp.dot(lines, wg[0, :, at : at + 256], preferred_element_type=jnp.float32)
        up = jnp.dot(lines, wu[0, :, at : at + 256], preferred_element_type=jnp.float32)
        hidden.append((gate / (1.0 + jnp.exp(-gate)) * up).astype(jnp.bfloat16))
    hidden = jnp.concatenate(hidden, axis=1)
    for at in range(0, width, 512):
        got = jnp.dot(hidden, wd[0, :, at : at + 512], preferred_element_type=jnp.float32)
        for n, o in enumerate(outs):
            o[:, at : at + 512] = got[n * rows : (n + 1) * rows].astype(jnp.bfloat16)


def expert(slabs, weights):
    count = len(slabs)
    rows, width = slabs[0].shape
    ff = weights[0].shape[-1]
    vmem = pl.BlockSpec(memory_space=pltpu.VMEM)
    return pl.pallas_call(
        functools.partial(expert_kernel, count),
        in_specs=[vmem] * (count + 3),
        out_specs=[vmem] * count,
        out_shape=[jax.ShapeDtypeStruct((rows, width), jnp.bfloat16)] * count,
        compiler_params=pltpu.CompilerParams(vmem_limit_bytes=24 * 1024 * 1024),
        cost_estimate=pl.CostEstimate(
            flops=6 * count * rows * width * ff,
            bytes_accessed=4 * count * rows * width,
            transcendentals=count * rows * ff,
        ),
        name="expert",
    )(*slabs, *[pltpu.with_memory_space_constraint(w, pltpu.VMEM) for w in weights])


def per_device(tokens, expert_ids, gate_weights, w_gate, w_up, w_down):
    me = lax.axis_index("expert")
    x, y, c = me // (NY * NC), (me // NC) % NY, me % NC
    n = jnp.arange(16, dtype=jnp.int32)
    k, f = n // NC, n % NC
    along_y = x * (NY * NC) + ((y + k) % NY) * NC + (c ^ f)
    along_x = ((x + k) % NX) * (NY * NC) + y * NC + (c ^ f)
    mine = jnp.where(n < KF, jnp.where(c == 0, along_y, along_x), -1)
    q = (mine[:, None] == jnp.arange(EXPERTS, dtype=jnp.int32)[None, :]).astype(jnp.bfloat16)

    send = lambda v, pairs: lax.ppermute(v, "expert", pairs)
    blocks = [tokens] + [send(tokens, spread_pairs(j)) for j in (1, 2, 3)]
    meta = prep(expert_ids.T, gate_weights.T)
    metas = [meta] + [send(meta, spread_pairs(j)) for j in (1, 2, 3)]
    weights = (w_gate, w_up, w_down)

    arrived = {}

    def deliver(keys, after=()):
        slabs = pack([NC * k + f for k, f in keys], q, metas, blocks, after)
        for (k, f), slab in zip(keys, slabs):
            arrived[k, f] = slab if (k, f) == (0, 0) else send(slab, deliver_pairs(k, f))

    backs = {}

    def work(keys):
        done = expert([arrived[g] for g in keys], weights)
        for (k, f), slab in zip(keys, done):
            backs[k, f] = slab if (k, f) == (0, 0) else send(slab, back(deliver_pairs(k, f)))
        return done[0]

    near = [(1, 0), (1, 1), (3, 0), (3, 1)]
    deliver(near + [(0, 0), (0, 1)])
    first = work([(0, 0), (0, 1)])
    deliver([(2, 0), (2, 1)], (first,))
    work(near[:2])
    work(near[2:])
    work([(2, 0), (2, 1)])
    parts = combine(q, metas, [backs[k, f] for k in range(4) for f in (0, 1)])
    mixed = parts[0]
    for j in (1, 2, 3):
        mixed = mixed + send(parts[j], back(spread_pairs(j))).astype(jnp.float32)
    return mixed.astype(jnp.bfloat16)


def solution(mesh):
    return jax.shard_map(
        per_device,
        mesh=mesh,
        in_specs=(
            P(("dp", "expert"), None),
            P(("dp", "expert"), None),
            P(("dp", "expert"), None),
            P("expert", None, None),
            P("expert", None, None),
            P("expert", None, None),
        ),
        out_specs=P(("dp", "expert"), None),
        check_vma=False,
    )
```

```python
import functools

import jax
import jax.numpy as jnp
from jax import lax
from jax.experimental import pallas as pl
from jax.experimental.pallas import tpu as pltpu
from jax.sharding import PartitionSpec as P

NX, NY, NC = 4, 4, 2
EXPERTS = NX * NY * NC
CAP = 40
KF = 8


def index_of(x, y, c):
    return ((x % NX) * NY + (y % NY)) * NC + c


def spread_pairs(j):
    pairs = []
    for x in range(NX):
        for y in range(NY):
            pairs.append((index_of(x, y, 0), index_of(x + j, y, 0)))
            pairs.append((index_of(x, y, 1), index_of(x, y + j, 1)))
    return pairs


def deliver_pairs(k):
    pairs = []
    for x in range(NX):
        for y in range(NY):
            pairs.append((index_of(x, y, 0), index_of(x, y + k, 0)))
            pairs.append((index_of(x, y, 1), index_of(x + k, y, 1)))
    return pairs


def spread_groups():
    return [[index_of(x, y, 0) for x in range(NX)] for y in range(NY)] + [
        [index_of(x, y, 1) for y in range(NY)] for x in range(NX)
    ]


def swap_pairs():
    return [(i, i ^ 1) for i in range(EXPERTS)]


def back(pairs):
    return [(b, a) for a, b in pairs]


def prep_kernel(ids_ref, gw_ref, tok_ref, out_ref, own_ref, sem):
    copy = pltpu.make_async_copy(tok_ref, own_ref, sem)
    copy.start()
    top, tok = ids_ref.shape
    ids = ids_ref[...]
    gw = gw_ref[...]
    name = lax.broadcasted_iota(jnp.int32, (EXPERTS, tok), 0)
    chosen = jnp.zeros((EXPERTS, tok), jnp.float32)
    weight = jnp.zeros((EXPERTS, tok), jnp.float32)
    for k in range(top):
        hit = ids[k : k + 1, :] == name
        chosen = jnp.where(hit, 1.0, chosen)
        weight = jnp.where(hit, gw[k : k + 1, :], weight)
    row = lax.broadcasted_iota(jnp.int32, (tok, tok), 0)
    col = lax.broadcasted_iota(jnp.int32, (tok, tok), 1)
    earlier = jnp.where(row < col, 1.0, 0.0).astype(jnp.bfloat16)
    count = jnp.dot(chosen.astype(jnp.bfloat16), earlier, preferred_element_type=jnp.float32)
    slot = jnp.where(chosen > 0.5, count, -1.0)
    half = EXPERTS // 2
    out_ref[...] = jnp.concatenate(
        [slot[:half], slot[half:], weight[:half], weight[half:]], axis=1
    ).astype(jnp.bfloat16)
    copy.wait()


def prep(ids, gw, tokens):
    tok = ids.shape[1]
    vmem = pl.BlockSpec(memory_space=pltpu.VMEM)
    return pl.pallas_call(
        prep_kernel,
        in_specs=[vmem, vmem, pl.BlockSpec(memory_space=pl.ANY)],
        out_specs=[vmem, vmem],
        out_shape=[
            jax.ShapeDtypeStruct((EXPERTS // 2, 4 * tok), jnp.bfloat16),
            pltpu.VMEM(tokens.shape, tokens.dtype),
        ],
        scratch_shapes=[pltpu.SemaphoreType.DMA],
        compiler_params=pltpu.CompilerParams(vmem_limit_bytes=4 * 1024 * 1024),
        cost_estimate=pl.CostEstimate(flops=2 * EXPERTS * tok**2, bytes_accessed=32 * tok * 4, transcendentals=0),
        name="prep",
    )(ids, gw, pltpu.with_memory_space_constraint(tokens, pltpu.HBM))


def select(q, meta, at, tok):
    half = EXPERTS // 2
    return jnp.dot(
        q[:, :half], meta[:, at : at + tok], preferred_element_type=jnp.float32
    ) + jnp.dot(q[:, half:], meta[:, at + tok : at + 2 * tok], preferred_element_type=jnp.float32)


def table(pos_ref, metas_ref, j):
    return metas_ref[lax.rem(pos_ref[0] + 4 - j, 4)]


def pack_kernel(which, pos_ref, q_ref, metas_ref, *refs):
    blocks, outs = refs[:4], refs[-len(which) :]
    tok, width = blocks[0].shape
    q = q_ref[...]
    span = 2 * CAP
    r = lax.broadcasted_iota(jnp.int32, (span, 2 * tok), 0)
    t = lax.broadcasted_iota(jnp.int32, (span, 2 * tok), 1)
    second = r >= CAP
    target = jnp.where(second, r - CAP, r)
    target = jnp.where(second == (t >= tok), target, -5).astype(jnp.float32)
    cols = 512
    for p in range(2):
        metas = [table(pos_ref, metas_ref, j) for j in (2 * p, 2 * p + 1)]
        slots = jnp.concatenate([select(q, m, 0, tok) for m in metas], axis=1)
        pick = jnp.concatenate(
            [
                jnp.where(slots[NC * k + f : NC * k + f + 1, :] == target, 1.0, 0.0).astype(jnp.bfloat16)
                for k in which
                for f in range(NC)
            ],
            axis=0,
        )
        for at in range(0, width, cols):
            block = jnp.concatenate([b[:, at : at + cols] for b in blocks[2 * p : 2 * p + 2]], axis=0)
            got = jnp.dot(pick, block, preferred_element_type=jnp.float32).astype(jnp.bfloat16)
            for n, o in enumerate(outs):
                for f in range(NC):
                    to, of = span * (2 * f + p), span * (NC * n + f)
                    o[to : to + span, at : at + cols] = got[of : of + span, :]


def pack(which, pos, q, metas, blocks, after=()):
    tok, width = blocks[0].shape
    count = len(which)
    rows = NC * 4 * CAP
    vmem = pl.BlockSpec(memory_space=pltpu.VMEM)
    return pl.pallas_call(
        functools.partial(pack_kernel, which),
        in_specs=[pl.BlockSpec(memory_space=pltpu.SMEM)] + [vmem] * 6 + [pl.BlockSpec(memory_space=pl.ANY)] * len(after),
        out_specs=[vmem] * count,
        out_shape=[jax.ShapeDtypeStruct((rows, width), jnp.bfloat16)] * count,
        compiler_params=pltpu.CompilerParams(vmem_limit_bytes=16 * 1024 * 1024),
        cost_estimate=pl.CostEstimate(
            flops=2 * rows * count * 2 * tok * width,
            bytes_accessed=2 * (4 * tok + rows * count) * width,
            transcendentals=0,
        ),
        name="pack",
    )(pos, q, metas, *blocks, *after)


def combine_kernel(pos_ref, q_ref, metas_ref, *refs):
    backs, outs = refs[:4], refs[4:]
    tok, width = outs[0].shape
    q = q_ref[...]
    half = 2 * CAP
    span = half * KF
    lane = lax.broadcasted_iota(jnp.int32, (2 * tok, span), 1)
    part = jnp.zeros((2 * tok, span), jnp.int32)
    er = lax.broadcasted_iota(jnp.int32, (16, span), 0)
    el = lax.broadcasted_iota(jnp.int32, (16, span), 1)
    ep = jnp.zeros((16, span), jnp.int32)
    for n in range(1, KF):
        part = jnp.where(lane >= half * n, half * n, part)
        ep = jnp.where(el >= half * n, n, ep)
    r = lane - part
    t = lax.broadcasted_iota(jnp.int32, (2 * tok, span), 0)
    second = r >= CAP
    target = jnp.where(second, r - CAP, r)
    target = jnp.where(second == (t >= tok), target, -5).astype(jnp.float32)
    expand = jnp.where(er == ep, 1.0, 0.0).astype(jnp.bfloat16)

    def widen(v):
        return lax.dot_general(
            v.astype(jnp.bfloat16), expand, (((0,), (0,)), ((), ())), preferred_element_type=jnp.float32
        )

    cols = 512
    for p in range(2):
        metas = [table(pos_ref, metas_ref, j) for j in (2 * p, 2 * p + 1)]
        slots = jnp.concatenate([select(q, m, 0, tok) for m in metas], axis=1)
        weights = jnp.concatenate([select(q, m, 2 * tok, tok) for m in metas], axis=1)
        mix = jnp.where(widen(slots) == target, widen(weights), 0.0).astype(jnp.bfloat16)
        for at in range(0, width, cols):
            rows = jnp.concatenate(
                [b[half * (2 * f + p) : half * (2 * f + p + 1), at : at + cols] for b in backs for f in range(NC)],
                axis=0,
            )
            got = jnp.dot(mix, rows, preferred_element_type=jnp.float32)
            for n, o in enumerate(outs[2 * p : 2 * p + 2]):
                o[:, at : at + cols] = got[n * tok : (n + 1) * tok].astype(o.dtype)


def combine(pos, q, metas, backs, tok):
    rows, width = backs[0].shape
    vmem = pl.BlockSpec(memory_space=pltpu.VMEM)
    return pl.pallas_call(
        combine_kernel,
        in_specs=[pl.BlockSpec(memory_space=pltpu.SMEM)] + [vmem] * 6,
        out_specs=[vmem] * 4,
        out_shape=[jax.ShapeDtypeStruct((tok, width), jnp.float32)]
        + [jax.ShapeDtypeStruct((tok, width), jnp.bfloat16)] * 3,
        compiler_params=pltpu.CompilerParams(vmem_limit_bytes=16 * 1024 * 1024),
        cost_estimate=pl.CostEstimate(
            flops=2 * 4 * rows * 2 * tok * width,
            bytes_accessed=2 * (5 * tok + 4 * rows) * width,
            transcendentals=0,
        ),
        name="combine",
    )(pos, q, metas, *backs)


def expert_kernel(count, *refs):
    slabs, weights, outs = refs[:count], refs[count : count + 6], refs[count + 6 :]
    width = slabs[0].shape[1]
    rows = slabs[0].shape[0] // NC
    for f in range(NC):
        wg, wu, wd = weights[3 * f : 3 * f + 3]
        ff = wg.shape[-1]
        lines = jnp.concatenate([s[f * rows : (f + 1) * rows, :] for s in slabs], axis=0)
        hidden = []
        for at in range(0, ff, 256):
            gate = jnp.dot(lines, wg[0, :, at : at + 256], preferred_element_type=jnp.float32)
            up = jnp.dot(lines, wu[0, :, at : at + 256], preferred_element_type=jnp.float32)
            hidden.append((gate / (1.0 + jnp.exp(-gate)) * up).astype(jnp.bfloat16))
        hidden = jnp.concatenate(hidden, axis=1)
        for at in range(0, width, 512):
            got = jnp.dot(hidden, wd[0, :, at : at + 512], preferred_element_type=jnp.float32)
            for n, o in enumerate(outs):
                o[f * rows : (f + 1) * rows, at : at + 512] = got[n * rows : (n + 1) * rows].astype(jnp.bfloat16)


def expert(slabs, weights):
    count = len(slabs)
    rows, width = slabs[0].shape
    ff = weights[0].shape[-1]
    vmem = pl.BlockSpec(memory_space=pltpu.VMEM)
    return pl.pallas_call(
        functools.partial(expert_kernel, count),
        in_specs=[vmem] * (count + 6),
        out_specs=[vmem] * count,
        out_shape=[jax.ShapeDtypeStruct((rows, width), jnp.bfloat16)] * count,
        compiler_params=pltpu.CompilerParams(vmem_limit_bytes=16 * 1024 * 1024),
        cost_estimate=pl.CostEstimate(
            flops=6 * count * rows * width * ff,
            bytes_accessed=4 * count * rows * width,
            transcendentals=count * rows * ff,
        ),
        name="expert",
    )(*slabs, *[pltpu.with_memory_space_constraint(w, pltpu.VMEM) for w in weights])


def hold_kernel(*refs):
    ins, outs, sems = refs[:3], refs[3:6], refs[6]
    copies = [pltpu.make_async_copy(a, b, sems.at[n]) for n, (a, b) in enumerate(zip(ins, outs))]
    for copy in copies:
        copy.start()
    for copy in copies:
        copy.wait()


def hold(*weights):
    return pl.pallas_call(
        hold_kernel,
        in_specs=[pl.BlockSpec(memory_space=pl.ANY)] * 3,
        out_specs=[pl.BlockSpec(memory_space=pltpu.VMEM)] * 3,
        out_shape=[pltpu.VMEM(w.shape, w.dtype) for w in weights],
        scratch_shapes=[pltpu.SemaphoreType.DMA((3,))],
        compiler_params=pltpu.CompilerParams(vmem_limit_bytes=4 * 1024 * 1024),
        cost_estimate=pl.CostEstimate(flops=0, bytes_accessed=4 * weights[0].size * 3, transcendentals=0),
        name="hold",
    )(*[pltpu.with_memory_space_constraint(w, pltpu.HBM) for w in weights])


def per_device(tokens, expert_ids, gate_weights, w_gate, w_up, w_down):
    me = lax.axis_index("expert")
    x, y, c = me // (NY * NC), (me // NC) % NY, me % NC
    n = jnp.arange(16, dtype=jnp.int32)
    k, f = n // NC, n % NC
    along_y = x * (NY * NC) + ((y + k) % NY) * NC + (c ^ f)
    along_x = ((x + k) % NX) * (NY * NC) + y * NC + (c ^ f)
    mine = jnp.where(n < KF, jnp.where(c == 0, along_y, along_x), -1)
    q = (mine[:, None] == jnp.arange(EXPERTS, dtype=jnp.int32)[None, :]).astype(jnp.bfloat16)
    pos = jnp.where(c == 0, x, y).reshape(1).astype(jnp.int32)

    send = lambda v, pairs: lax.ppermute(v, "expert", pairs)
    moved = [send(tokens, spread_pairs(j)) for j in (1, 2, 3)]
    meta, own = prep(expert_ids.T, gate_weights.T, tokens)
    blocks = [own] + moved
    metas = lax.all_gather(meta, "expert", axis=0, axis_index_groups=spread_groups())
    first = lax.optimization_barrier((w_gate, w_up, metas))[:2]
    weights = list(hold(w_gate, w_up, w_down)) + [send(w, swap_pairs()) for w in first]

    slabs = dict(zip((1, 3, 0), pack((1, 3, 0), pos, q, metas, blocks)))
    last = lax.optimization_barrier((w_down, slabs[0]))[0]
    weights.append(send(last, swap_pairs()))
    arrived = {k: send(slabs[k], deliver_pairs(k)) for k in (1, 3)}
    backs = {}
    (backs[0],) = expert([slabs[0]], weights)
    (far,) = pack((2,), pos, q, metas, blocks, (backs[0],))
    arrived[2] = send(far, deliver_pairs(2))
    for ks in ((1, 3), (2,)):
        for k, slab in zip(ks, expert([arrived[k] for k in ks], weights)):
            backs[k] = send(slab, back(deliver_pairs(k)))
    parts = combine(pos, q, metas, [backs[k] for k in range(4)], tokens.shape[0])
    mixed = parts[0]
    for j in (1, 2, 3):
        mixed = mixed + send(parts[j], back(spread_pairs(j))).astype(jnp.float32)
    return mixed.astype(jnp.bfloat16)


def solution(mesh):
    return jax.shard_map(
        per_device,
        mesh=mesh,
        in_specs=(
            P(("dp", "expert"), None),
            P(("dp", "expert"), None),
            P(("dp", "expert"), None),
            P("expert", None, None),
            P("expert", None, None),
            P("expert", None, None),
        ),
        out_specs=P(("dp", "expert"), None),
        check_vma=False,
    )
```

```python
import functools

import jax
import jax.numpy as jnp
from jax import lax
from jax.experimental import pallas as pl
from jax.experimental.pallas import tpu as pltpu
from jax.sharding import PartitionSpec as P

NX, NY, NC = 4, 4, 2
EXPERTS = NX * NY * NC
CAP = 40
META = 16
KF = 8


def index_of(x, y, c):
    return ((x % NX) * NY + (y % NY)) * NC + c


def spread_pairs(j):
    pairs = []
    for x in range(NX):
        for y in range(NY):
            pairs.append((index_of(x, y, 0), index_of(x + j, y, 0)))
            pairs.append((index_of(x, y, 1), index_of(x, y + j, 1)))
    return pairs


def deliver_pairs(k):
    pairs = []
    for x in range(NX):
        for y in range(NY):
            pairs.append((index_of(x, y, 0), index_of(x, y + k, 0)))
            pairs.append((index_of(x, y, 1), index_of(x + k, y, 1)))
    return pairs


def swap_pairs():
    return [(i, i ^ 1) for i in range(EXPERTS)]


def back(pairs):
    return [(b, a) for a, b in pairs]


def prep_kernel(ids_hbm, gw_hbm, tok_hbm, out_ref, load_ref, ids_ref, gw_ref, sems):
    top, tok = ids_ref.shape
    copies = [
        pltpu.make_async_copy(ids_hbm, ids_ref, sems.at[0]),
        pltpu.make_async_copy(gw_hbm, gw_ref, sems.at[1]),
        pltpu.make_async_copy(tok_hbm, load_ref.at[pl.ds(0, tok)], sems.at[2]),
    ]
    for copy in copies:
        copy.start()
    row = lax.broadcasted_iota(jnp.int32, (tok, tok), 0)
    col = lax.broadcasted_iota(jnp.int32, (tok, tok), 1)
    earlier = jnp.where(row < col, 1.0, 0.0).astype(jnp.bfloat16)
    name = lax.broadcasted_iota(jnp.int32, (EXPERTS, tok), 0)
    chosen = jnp.zeros((EXPERTS, tok), jnp.float32)
    weight = jnp.zeros((EXPERTS, tok), jnp.float32)
    copies[0].wait()
    copies[1].wait()
    ids = ids_ref[...]
    gw = gw_ref[...]
    for k in range(top):
        hit = ids[k : k + 1, :] == name
        chosen = jnp.where(hit, 1.0, chosen)
        weight = jnp.where(hit, gw[k : k + 1, :], weight)
    count = jnp.dot(chosen.astype(jnp.bfloat16), earlier, preferred_element_type=jnp.float32)
    slot = jnp.where(chosen > 0.5, count, -1.0)
    half = EXPERTS // 2
    meta = jnp.concatenate([slot[:half], slot[half:], weight[:half], weight[half:]], axis=1)
    meta = meta.astype(jnp.bfloat16)
    out_ref[...] = meta
    load_ref[tok:, : 4 * tok] = meta
    load_ref[tok:, 4 * tok :] = jnp.zeros((META, load_ref.shape[1] - 4 * tok), jnp.bfloat16)
    copies[2].wait()


def prep(ids, gw, tokens):
    tok, width = tokens.shape
    vmem = pl.BlockSpec(memory_space=pltpu.VMEM)
    hbm = pl.BlockSpec(memory_space=pl.ANY)
    return pl.pallas_call(
        prep_kernel,
        in_specs=[hbm, hbm, hbm],
        out_specs=[vmem, vmem],
        out_shape=[
            pltpu.VMEM((META, 4 * tok), jnp.bfloat16),
            pltpu.VMEM((tok + META, width), jnp.bfloat16),
        ],
        scratch_shapes=[
            pltpu.VMEM(ids.shape, ids.dtype),
            pltpu.VMEM(gw.shape, gw.dtype),
            pltpu.SemaphoreType.DMA((3,)),
        ],
        compiler_params=pltpu.CompilerParams(vmem_limit_bytes=4 * 1024 * 1024),
        cost_estimate=pl.CostEstimate(flops=2 * EXPERTS * tok**2, bytes_accessed=4 * tok * width, transcendentals=0),
        name="prep",
    )(*[pltpu.with_memory_space_constraint(v, pltpu.HBM) for v in (ids, gw, tokens)])


def select(q, meta, at, tok):
    half = EXPERTS // 2
    return jnp.dot(
        q[:, :half], meta[:, at : at + tok], preferred_element_type=jnp.float32
    ) + jnp.dot(q[:, half:], meta[:, at + tok : at + 2 * tok], preferred_element_type=jnp.float32)


def tables(metas, blocks):
    m0, m1, m3 = metas
    tok = blocks[0].shape[0] - META
    return m0[...], m1[...], blocks[1][tok:, : 4 * tok], m3[...]


def pack_kernel(which, q_ref, *refs):
    metas, blocks, outs = refs[:3], refs[3:7], refs[-len(which) :]
    tok, width = blocks[1].shape
    metas = tables(metas, blocks[::2])
    q = q_ref[...]
    span = 2 * CAP
    r = lax.broadcasted_iota(jnp.int32, (span, 2 * tok), 0)
    t = lax.broadcasted_iota(jnp.int32, (span, 2 * tok), 1)
    second = r >= CAP
    target = jnp.where(second, r - CAP, r)
    target = jnp.where(second == (t >= tok), target, -5).astype(jnp.float32)
    cols = 512
    for p in range(2):
        pair = metas[2 * p : 2 * p + 2]
        slots = jnp.concatenate([select(q, m, 0, tok) for m in pair], axis=1)
        pick = jnp.concatenate(
            [
                jnp.where(slots[NC * k + f : NC * k + f + 1, :] == target, 1.0, 0.0).astype(jnp.bfloat16)
                for k in which
                for f in range(NC)
            ],
            axis=0,
        )
        for at in range(0, width, cols):
            block = jnp.concatenate([b[:tok, at : at + cols] for b in blocks[2 * p : 2 * p + 2]], axis=0)
            got = jnp.dot(pick, block, preferred_element_type=jnp.float32).astype(jnp.bfloat16)
            for n, o in enumerate(outs):
                for f in range(NC):
                    to, of = span * (2 * f + p), span * (NC * n + f)
                    o[to : to + span, at : at + cols] = got[of : of + span, :]


def pack(which, q, metas, blocks, after=()):
    tok, width = blocks[1].shape
    count = len(which)
    rows = NC * 4 * CAP
    vmem = pl.BlockSpec(memory_space=pltpu.VMEM)
    return pl.pallas_call(
        functools.partial(pack_kernel, which),
        in_specs=[vmem] * 8 + [pl.BlockSpec(memory_space=pl.ANY)] * len(after),
        out_specs=[vmem] * count,
        out_shape=[jax.ShapeDtypeStruct((rows, width), jnp.bfloat16)] * count,
        compiler_params=pltpu.CompilerParams(vmem_limit_bytes=16 * 1024 * 1024),
        cost_estimate=pl.CostEstimate(
            flops=2 * rows * count * 2 * tok * width,
            bytes_accessed=2 * (4 * tok + rows * count) * width,
            transcendentals=0,
        ),
        name="pack",
    )(q, *metas, *blocks, *after)


def combine_kernel(q_ref, *refs):
    metas, blocks, backs, outs = refs[:3], refs[3:5], refs[5:9], refs[9:]
    metas = tables(metas, blocks)
    tok, width = outs[0].shape
    q = q_ref[...]
    half = 2 * CAP
    span = half * KF
    lane = lax.broadcasted_iota(jnp.int32, (2 * tok, span), 1)
    part = jnp.zeros((2 * tok, span), jnp.int32)
    er = lax.broadcasted_iota(jnp.int32, (16, span), 0)
    el = lax.broadcasted_iota(jnp.int32, (16, span), 1)
    ep = jnp.zeros((16, span), jnp.int32)
    for n in range(1, KF):
        part = jnp.where(lane >= half * n, half * n, part)
        ep = jnp.where(el >= half * n, n, ep)
    r = lane - part
    t = lax.broadcasted_iota(jnp.int32, (2 * tok, span), 0)
    second = r >= CAP
    target = jnp.where(second, r - CAP, r)
    target = jnp.where(second == (t >= tok), target, -5).astype(jnp.float32)
    expand = jnp.where(er == ep, 1.0, 0.0).astype(jnp.bfloat16)

    def widen(v):
        return lax.dot_general(
            v.astype(jnp.bfloat16), expand, (((0,), (0,)), ((), ())), preferred_element_type=jnp.float32
        )

    cols = 512
    for p in range(2):
        pair = metas[2 * p : 2 * p + 2]
        slots = jnp.concatenate([select(q, m, 0, tok) for m in pair], axis=1)
        weights = jnp.concatenate([select(q, m, 2 * tok, tok) for m in pair], axis=1)
        mix = jnp.where(widen(slots) == target, widen(weights), 0.0).astype(jnp.bfloat16)
        for at in range(0, width, cols):
            rows = jnp.concatenate(
                [b[half * (2 * f + p) : half * (2 * f + p + 1), at : at + cols] for b in backs for f in range(NC)],
                axis=0,
            )
            got = jnp.dot(mix, rows, preferred_element_type=jnp.float32)
            for n, o in enumerate(outs[2 * p : 2 * p + 2]):
                o[:, at : at + cols] = got[n * tok : (n + 1) * tok].astype(o.dtype)


def combine(q, metas, blocks, backs):
    rows, width = backs[0].shape
    tok = blocks[1].shape[0]
    vmem = pl.BlockSpec(memory_space=pltpu.VMEM)
    return pl.pallas_call(
        combine_kernel,
        in_specs=[vmem] * 10,
        out_specs=[vmem] * 4,
        out_shape=[jax.ShapeDtypeStruct((tok, width), jnp.float32)]
        + [jax.ShapeDtypeStruct((tok, width), jnp.bfloat16)] * 3,
        compiler_params=pltpu.CompilerParams(vmem_limit_bytes=16 * 1024 * 1024),
        cost_estimate=pl.CostEstimate(
            flops=2 * 4 * rows * 2 * tok * width,
            bytes_accessed=2 * (5 * tok + 4 * rows) * width,
            transcendentals=0,
        ),
        name="combine",
    )(q, *metas, *blocks[::2], *backs)


def expert_kernel(count, *refs):
    slabs, weights, outs = refs[:count], refs[count : count + 6], refs[count + 6 :]
    width = slabs[0].shape[1]
    rows = slabs[0].shape[0] // NC
    for f in range(NC):
        wg, wu, wd = weights[3 * f : 3 * f + 3]
        ff = wg.shape[-1]
        lines = jnp.concatenate([s[f * rows : (f + 1) * rows, :] for s in slabs], axis=0)
        hidden = []
        for at in range(0, ff, 256):
            gate = jnp.dot(lines, wg[0, :, at : at + 256], preferred_element_type=jnp.float32)
            up = jnp.dot(lines, wu[0, :, at : at + 256], preferred_element_type=jnp.float32)
            hidden.append((gate / (1.0 + jnp.exp(-gate)) * up).astype(jnp.bfloat16))
        hidden = jnp.concatenate(hidden, axis=1)
        for at in range(0, width, 512):
            got = jnp.dot(hidden, wd[0, :, at : at + 512], preferred_element_type=jnp.float32)
            for n, o in enumerate(outs):
                o[f * rows : (f + 1) * rows, at : at + 512] = got[n * rows : (n + 1) * rows].astype(jnp.bfloat16)


def expert(slabs, weights):
    count = len(slabs)
    rows, width = slabs[0].shape
    ff = weights[0].shape[-1]
    vmem = pl.BlockSpec(memory_space=pltpu.VMEM)
    return pl.pallas_call(
        functools.partial(expert_kernel, count),
        in_specs=[vmem] * (count + 6),
        out_specs=[vmem] * count,
        out_shape=[jax.ShapeDtypeStruct((rows, width), jnp.bfloat16)] * count,
        compiler_params=pltpu.CompilerParams(vmem_limit_bytes=16 * 1024 * 1024),
        cost_estimate=pl.CostEstimate(
            flops=6 * count * rows * width * ff,
            bytes_accessed=4 * count * rows * width,
            transcendentals=count * rows * ff,
        ),
        name="expert",
    )(*slabs, *[pltpu.with_memory_space_constraint(w, pltpu.VMEM) for w in weights])


def hold_kernel(*refs):
    ins, outs, sems = refs[:3], refs[3:6], refs[6]
    copies = [pltpu.make_async_copy(a, b, sems.at[n]) for n, (a, b) in enumerate(zip(ins, outs))]
    for copy in copies:
        copy.start()
    for copy in copies:
        copy.wait()


def hold(*weights):
    return pl.pallas_call(
        hold_kernel,
        in_specs=[pl.BlockSpec(memory_space=pl.ANY)] * 3,
        out_specs=[pl.BlockSpec(memory_space=pltpu.VMEM)] * 3,
        out_shape=[pltpu.VMEM(w.shape, w.dtype) for w in weights],
        scratch_shapes=[pltpu.SemaphoreType.DMA((3,))],
        compiler_params=pltpu.CompilerParams(vmem_limit_bytes=4 * 1024 * 1024),
        cost_estimate=pl.CostEstimate(flops=0, bytes_accessed=4 * weights[0].size * 3, transcendentals=0),
        name="hold",
    )(*[pltpu.with_memory_space_constraint(w, pltpu.HBM) for w in weights])


def per_device(tokens, expert_ids, gate_weights, w_gate, w_up, w_down):
    me = lax.axis_index("expert")
    x, y, c = me // (NY * NC), (me // NC) % NY, me % NC
    n = jnp.arange(16, dtype=jnp.int32)
    k, f = n // NC, n % NC
    along_y = x * (NY * NC) + ((y + k) % NY) * NC + (c ^ f)
    along_x = ((x + k) % NX) * (NY * NC) + y * NC + (c ^ f)
    mine = jnp.where(n < KF, jnp.where(c == 0, along_y, along_x), -1)
    q = (mine[:, None] == jnp.arange(EXPERTS, dtype=jnp.int32)[None, :]).astype(jnp.bfloat16)

    send = lambda v, pairs: lax.ppermute(v, "expert", pairs)
    moved = {j: send(tokens, spread_pairs(j)) for j in (1, 3)}
    meta, load = prep(expert_ids.T, gate_weights.T, tokens)
    moved[2] = send(load, spread_pairs(2))
    blocks = [load, moved[1], moved[2], moved[3]]
    metas = [meta] + [send(meta, spread_pairs(j)) for j in (1, 3)]
    first = lax.optimization_barrier((w_gate, w_up, moved[1]))[:2]
    weights = list(hold(w_gate, w_up, w_down)) + [send(w, swap_pairs()) for w in first]

    slabs = dict(zip((1, 3, 0), pack((1, 3, 0), q, metas, blocks)))
    last = lax.optimization_barrier((w_down, slabs[0]))[0]
    weights.append(send(last, swap_pairs()))
    arrived = {k: send(slabs[k], deliver_pairs(k)) for k in (1, 3)}
    backs = {}
    (backs[0],) = expert([slabs[0]], weights)
    (far,) = pack((2,), q, metas, blocks, (backs[0],))
    arrived[2] = send(far, deliver_pairs(2))
    for ks in ((1, 3), (2,)):
        for k, slab in zip(ks, expert([arrived[k] for k in ks], weights)):
            backs[k] = send(slab, back(deliver_pairs(k)))
    parts = combine(q, metas, blocks, [backs[k] for k in range(4)])
    mixed = parts[0]
    for j in (1, 2, 3):
        mixed = mixed + send(parts[j], back(spread_pairs(j))).astype(jnp.float32)
    return mixed.astype(jnp.bfloat16)


def solution(mesh):
    return jax.shard_map(
        per_device,
        mesh=mesh,
        in_specs=(
            P(("dp", "expert"), None),
            P(("dp", "expert"), None),
            P(("dp", "expert"), None),
            P("expert", None, None),
            P("expert", None, None),
            P("expert", None, None),
        ),
        out_specs=P(("dp", "expert"), None),
        check_vma=False,
    )
```

```python
import functools

import jax
import jax.numpy as jnp
from jax import lax
from jax.experimental import pallas as pl
from jax.experimental.pallas import tpu as pltpu
from jax.sharding import PartitionSpec as P

NX, NY, NC = 4, 4, 2
EXPERTS = NX * NY * NC
CAP = 40
EXTRA = 128
KF = 8


def index_of(x, y, c):
    return ((x % NX) * NY + (y % NY)) * NC + c


def spread_pairs(j):
    pairs = []
    for x in range(NX):
        for y in range(NY):
            pairs.append((index_of(x, y, 0), index_of(x + j, y, 0)))
            pairs.append((index_of(x, y, 1), index_of(x, y + j, 1)))
    return pairs


def deliver_pairs(k):
    pairs = []
    for x in range(NX):
        for y in range(NY):
            pairs.append((index_of(x, y, 0), index_of(x, y + k, 0)))
            pairs.append((index_of(x, y, 1), index_of(x + k, y, 1)))
    return pairs


def swap_pairs():
    return [(i, i ^ 1) for i in range(EXPERTS)]


def back(pairs):
    return [(b, a) for a, b in pairs]


def prep_kernel(ids_hbm, gw_hbm, tok_hbm, out_ref, ids_ref, gw_ref, sems):
    top, tok = ids_ref.shape
    width = tok_hbm.shape[1]
    copies = [
        pltpu.make_async_copy(ids_hbm, ids_ref, sems.at[0]),
        pltpu.make_async_copy(gw_hbm, gw_ref, sems.at[1]),
        pltpu.make_async_copy(tok_hbm, out_ref.at[:, pl.ds(0, width)], sems.at[2]),
    ]
    for copy in copies:
        copy.start()
    row = lax.broadcasted_iota(jnp.int32, (tok, tok), 0)
    col = lax.broadcasted_iota(jnp.int32, (tok, tok), 1)
    earlier = jnp.where(row < col, 1.0, 0.0).astype(jnp.bfloat16)
    name = lax.broadcasted_iota(jnp.int32, (EXPERTS, tok), 0)
    chosen = jnp.zeros((EXPERTS, tok), jnp.float32)
    weight = jnp.zeros((EXPERTS, tok), jnp.float32)
    copies[0].wait()
    copies[1].wait()
    ids = ids_ref[...]
    gw = gw_ref[...]
    for k in range(top):
        hit = ids[k : k + 1, :] == name
        chosen = jnp.where(hit, 1.0, chosen)
        weight = jnp.where(hit, gw[k : k + 1, :], weight)
    count = jnp.dot(chosen.astype(jnp.bfloat16), earlier, preferred_element_type=jnp.float32)
    slot = jnp.where(chosen > 0.5, count, -1.0)
    blank = jnp.zeros((EXTRA - 2 * EXPERTS, tok), jnp.float32)
    table = jnp.concatenate([slot, weight, blank], axis=0)
    out_ref[:, width:] = table.T.astype(jnp.bfloat16)
    copies[2].wait()


def prep(ids, gw, tokens):
    tok, width = tokens.shape
    hbm = pl.BlockSpec(memory_space=pl.ANY)
    return pl.pallas_call(
        prep_kernel,
        in_specs=[hbm, hbm, hbm],
        out_specs=pl.BlockSpec(memory_space=pltpu.VMEM),
        out_shape=pltpu.VMEM((tok, width + EXTRA), jnp.bfloat16),
        scratch_shapes=[
            pltpu.VMEM(ids.shape, ids.dtype),
            pltpu.VMEM(gw.shape, gw.dtype),
            pltpu.SemaphoreType.DMA((3,)),
        ],
        compiler_params=pltpu.CompilerParams(vmem_limit_bytes=4 * 1024 * 1024),
        cost_estimate=pl.CostEstimate(flops=2 * EXPERTS * tok**2, bytes_accessed=4 * tok * width, transcendentals=0),
        name="prep",
    )(*[pltpu.with_memory_space_constraint(v, pltpu.HBM) for v in (ids, gw, tokens)])


def select(q, blocks):
    width = blocks[0].shape[1] - EXTRA
    return jnp.concatenate(
        [
            lax.dot_general(q, b[:, width:], (((1,), (1,)), ((), ())), preferred_element_type=jnp.float32)
            for b in blocks
        ],
        axis=1,
    )


def pack_kernel(which, q_ref, *refs):
    blocks, outs = refs[:4], refs[4:]
    tok = blocks[0].shape[0]
    width = outs[0].shape[1]
    q = q_ref[0]
    half = 2 * CAP
    r = lax.broadcasted_iota(jnp.int32, (half, 2 * tok), 0)
    t = lax.broadcasted_iota(jnp.int32, (half, 2 * tok), 1)
    second = r >= CAP
    target = jnp.where(second, r - CAP, r)
    target = jnp.where(second == (t >= tok), target, -5).astype(jnp.float32)
    cols = 512
    for p in range(2):
        pair = blocks[2 * p : 2 * p + 2]
        slots = select(q, pair)
        pick = jnp.concatenate(
            [
                jnp.where(slots[NC * k + f : NC * k + f + 1, :] == target, 1.0, 0.0).astype(jnp.bfloat16)
                for k in which
                for f in range(NC)
            ],
            axis=0,
        )
        for at in range(0, width, cols):
            block = jnp.concatenate([b[:, at : at + cols] for b in pair], axis=0)
            got = jnp.dot(pick, block, preferred_element_type=jnp.float32).astype(jnp.bfloat16)
            for n, o in enumerate(outs):
                o[2 * half * p : 2 * half * (p + 1), at : at + cols] = got[2 * half * n : 2 * half * (n + 1), :]


def pack(which, q, blocks):
    tok = blocks[0].shape[0]
    width = blocks[0].shape[1] - EXTRA
    count = len(which)
    rows = NC * 4 * CAP
    vmem = pl.BlockSpec(memory_space=pltpu.VMEM)
    return pl.pallas_call(
        functools.partial(pack_kernel, which),
        in_specs=[vmem] * 5,
        out_specs=[vmem] * count,
        out_shape=[jax.ShapeDtypeStruct((rows, width), jnp.bfloat16)] * count,
        compiler_params=pltpu.CompilerParams(vmem_limit_bytes=16 * 1024 * 1024),
        cost_estimate=pl.CostEstimate(
            flops=2 * rows * count * 2 * tok * width,
            bytes_accessed=2 * (4 * tok + rows * count) * width,
            transcendentals=0,
        ),
        name="pack",
    )(q, *blocks)


def combine_kernel(spots, q_ref, *refs):
    pair, backs, outs = refs[:2], refs[2:6], refs[6:]
    tok, width = outs[0].shape
    half = 2 * CAP
    span = half * KF
    lane = lax.broadcasted_iota(jnp.int32, (2 * tok, span), 1)
    part = jnp.zeros((2 * tok, span), jnp.int32)
    er = lax.broadcasted_iota(jnp.int32, (16, span), 0)
    el = lax.broadcasted_iota(jnp.int32, (16, span), 1)
    ep = jnp.zeros((16, span), jnp.int32)
    for n in range(1, KF):
        part = jnp.where(lane >= half * n, half * n, part)
        ep = jnp.where(el >= half * n, n, ep)
    r = lane - part
    t = lax.broadcasted_iota(jnp.int32, (2 * tok, span), 0)
    second = r >= CAP
    target = jnp.where(second, r - CAP, r)
    target = jnp.where(second == (t >= tok), target, -5).astype(jnp.float32)
    expand = jnp.where(er == ep, 1.0, 0.0).astype(jnp.bfloat16)

    def widen(v):
        return lax.dot_general(
            v.astype(jnp.bfloat16), expand, (((0,), (0,)), ((), ())), preferred_element_type=jnp.float32
        )

    mix = jnp.where(widen(select(q_ref[0], pair)) == target, widen(select(q_ref[1], pair)), 0.0)
    mix = mix.astype(jnp.bfloat16)
    cols = 512
    for at in range(0, width, cols):
        rows = jnp.concatenate(
            [b[2 * half * p : 2 * half * (p + 1), at : at + cols] for b, p in zip(backs, spots)], axis=0
        )
        got = jnp.dot(mix, rows, preferred_element_type=jnp.float32)
        for n, o in enumerate(outs):
            o[:, at : at + cols] = got[n * tok : (n + 1) * tok].astype(o.dtype)


def combine(q, pair, backs, spots, dtypes):
    tok = pair[0].shape[0]
    width = backs[0].shape[1]
    rows = NC * 4 * CAP
    vmem = pl.BlockSpec(memory_space=pltpu.VMEM)
    return pl.pallas_call(
        functools.partial(combine_kernel, spots),
        in_specs=[vmem] * 7,
        out_specs=[vmem] * 2,
        out_shape=[jax.ShapeDtypeStruct((tok, width), d) for d in dtypes],
        compiler_params=pltpu.CompilerParams(vmem_limit_bytes=16 * 1024 * 1024),
        cost_estimate=pl.CostEstimate(
            flops=2 * 2 * rows * 2 * tok * width,
            bytes_accessed=2 * (3 * tok + 2 * rows) * width,
            transcendentals=0,
        ),
        name="combine",
    )(q, *pair, *backs)


def expert_kernel(count, *refs):
    slabs, weights, outs = refs[:count], refs[count : count + 6], refs[count + 6 :]
    width = slabs[0].shape[1]
    half = 2 * CAP
    for f in range(NC):
        wg, wu, wd = weights[3 * f : 3 * f + 3]
        ff = wg.shape[-1]
        spots = [half * (2 * p + f) for p in range(2)]
        lines = jnp.concatenate([s[at : at + half, :] for s in slabs for at in spots], axis=0)
        hidden = []
        for at in range(0, ff, 256):
            gate = jnp.dot(lines, wg[0, :, at : at + 256], preferred_element_type=jnp.float32)
            up = jnp.dot(lines, wu[0, :, at : at + 256], preferred_element_type=jnp.float32)
            hidden.append((gate / (1.0 + jnp.exp(-gate)) * up).astype(jnp.bfloat16))
        hidden = jnp.concatenate(hidden, axis=1)
        for at in range(0, width, 512):
            got = jnp.dot(hidden, wd[0, :, at : at + 512], preferred_element_type=jnp.float32)
            got = got.astype(jnp.bfloat16)
            if len(outs) == count:
                places = [(o, spot) for o in outs for spot in spots]
            else:
                places = [(o, half * f) for o in outs]
            for n, (o, spot) in enumerate(places):
                o[spot : spot + half, at : at + 512] = got[n * half : (n + 1) * half]


def expert(slabs, weights, split=False):
    count = len(slabs)
    rows, width = slabs[0].shape
    ff = weights[0].shape[-1]
    outs = 2 * count if split else count
    vmem = pl.BlockSpec(memory_space=pltpu.VMEM)
    return pl.pallas_call(
        functools.partial(expert_kernel, count),
        in_specs=[vmem] * (count + 6),
        out_specs=[vmem] * outs,
        out_shape=[jax.ShapeDtypeStruct((rows * count // outs, width), jnp.bfloat16)] * outs,
        compiler_params=pltpu.CompilerParams(vmem_limit_bytes=16 * 1024 * 1024),
        cost_estimate=pl.CostEstimate(
            flops=6 * count * rows * width * ff,
            bytes_accessed=4 * count * rows * width,
            transcendentals=count * rows * ff,
        ),
        name="expert",
    )(*slabs, *[pltpu.with_memory_space_constraint(w, pltpu.VMEM) for w in weights])


def hold_kernel(*refs):
    ins, outs, sems = refs[:3], refs[3:6], refs[6]
    copies = [pltpu.make_async_copy(a, b, sems.at[n]) for n, (a, b) in enumerate(zip(ins, outs))]
    for copy in copies:
        copy.start()
    for copy in copies:
        copy.wait()


def hold(*weights):
    return pl.pallas_call(
        hold_kernel,
        in_specs=[pl.BlockSpec(memory_space=pl.ANY)] * 3,
        out_specs=[pl.BlockSpec(memory_space=pltpu.VMEM)] * 3,
        out_shape=[pltpu.VMEM(w.shape, w.dtype) for w in weights],
        scratch_shapes=[pltpu.SemaphoreType.DMA((3,))],
        compiler_params=pltpu.CompilerParams(vmem_limit_bytes=4 * 1024 * 1024),
        cost_estimate=pl.CostEstimate(flops=0, bytes_accessed=4 * weights[0].size * 3, transcendentals=0),
        name="hold",
    )(*[pltpu.with_memory_space_constraint(w, pltpu.HBM) for w in weights])


def per_device(tokens, expert_ids, gate_weights, w_gate, w_up, w_down):
    me = lax.axis_index("expert")
    x, y, c = me // (NY * NC), (me // NC) % NY, me % NC
    n = jnp.arange(16, dtype=jnp.int32)
    k, f = n // NC, n % NC
    along_y = x * (NY * NC) + ((y + k) % NY) * NC + (c ^ f)
    along_x = ((x + k) % NX) * (NY * NC) + y * NC + (c ^ f)
    mine = jnp.where(n < KF, jnp.where(c == 0, along_y, along_x), -1)
    spot = jnp.arange(EXTRA, dtype=jnp.int32)[None, :]
    q = jnp.stack([mine[:, None] == spot, (mine[:, None] + EXPERTS == spot) & (n < KF)[:, None]])
    q = q.astype(jnp.bfloat16)

    send = lambda v, pairs: lax.ppermute(v, "expert", pairs)
    after = lambda v, other: lax.optimization_barrier((v, other))[0]
    home = prep(expert_ids.T, gate_weights.T, tokens)
    blocks = [home] + [send(home, spread_pairs(j)) for j in (1, 2, 3)]
    weights = list(hold(w_gate, w_up, w_down)) + [send(after(w, home), swap_pairs()) for w in (w_gate, w_up)]

    near = pack((1, 3), q, blocks)
    weights.append(send(after(w_down, near[0]), swap_pairs()))
    arrived = {k: send(slab, deliver_pairs(k)) for k, slab in zip((1, 3), near)}
    stay, far = pack((0, 2), q, blocks)
    backs = {}
    (backs[0],) = expert([stay], weights)
    arrived[2] = send(after(far, backs[0]), deliver_pairs(2))
    for k, slab in zip((1, 3), expert([arrived[1], arrived[3]], weights)):
        backs[k] = send(slab, back(deliver_pairs(k)))
    early, late = expert([arrived[2]], weights, split=True)[::-1]
    early = send(early, back(deliver_pairs(2)))
    late = send(after(late, (backs[1], backs[3])), back(deliver_pairs(2)))

    whole = [backs[k] for k in (0, 1)]
    part2, part3 = combine(
        q, blocks[2:], [*whole, early, backs[3]], (1, 1, 0, 1), (jnp.bfloat16, jnp.bfloat16)
    )
    part0, part1 = combine(q, blocks[:2], [*whole, late, backs[3]], (0, 0, 0, 0), (jnp.float32, jnp.bfloat16))
    mixed = part0
    for j, part in ((2, part2), (3, part3), (1, part1)):
        mixed = mixed + send(part, back(spread_pairs(j))).astype(jnp.float32)
    return mixed.astype(jnp.bfloat16)


def solution(mesh):
    return jax.shard_map(
        per_device,
        mesh=mesh,
        in_specs=(
            P(("dp", "expert"), None),
            P(("dp", "expert"), None),
            P(("dp", "expert"), None),
            P("expert", None, None),
            P("expert", None, None),
            P("expert", None, None),
        ),
        out_specs=P(("dp", "expert"), None),
        check_vma=False,
    )
```

```python
import functools

import jax
import jax.numpy as jnp
from jax import lax
from jax.experimental import pallas as pl
from jax.experimental.pallas import tpu as pltpu
from jax.sharding import PartitionSpec as P

NX, NY, NC = 4, 4, 2
EXPERTS = NX * NY * NC
CAP = 40
EXTRA = 128
KF = 8


def index_of(x, y, c):
    return ((x % NX) * NY + (y % NY)) * NC + c


def spread_pairs(j):
    pairs = []
    for x in range(NX):
        for y in range(NY):
            pairs.append((index_of(x, y, 0), index_of(x + j, y, 0)))
            pairs.append((index_of(x, y, 1), index_of(x, y + j, 1)))
    return pairs


def deliver_pairs(k):
    pairs = []
    for x in range(NX):
        for y in range(NY):
            pairs.append((index_of(x, y, 0), index_of(x, y + k, 0)))
            pairs.append((index_of(x, y, 1), index_of(x + k, y, 1)))
    return pairs


def swap_pairs():
    return [(i, i ^ 1) for i in range(EXPERTS)]


def back(pairs):
    return [(b, a) for a, b in pairs]


def prep_kernel(ids_hbm, gw_hbm, tok_hbm, out_ref, q_ref, ids_ref, gw_ref, sems):
    top, tok = ids_ref.shape
    width = tok_hbm.shape[1]
    copies = [
        pltpu.make_async_copy(ids_hbm, ids_ref, sems.at[0]),
        pltpu.make_async_copy(gw_hbm, gw_ref, sems.at[1]),
        pltpu.make_async_copy(tok_hbm, out_ref.at[:, pl.ds(0, width)], sems.at[2]),
    ]
    for copy in copies:
        copy.start()
    row = lax.broadcasted_iota(jnp.int32, (tok, tok), 0)
    col = lax.broadcasted_iota(jnp.int32, (tok, tok), 1)
    earlier = jnp.where(row < col, 1.0, 0.0).astype(jnp.bfloat16)
    name = lax.broadcasted_iota(jnp.int32, (EXPERTS, tok), 0)
    chosen = jnp.zeros((EXPERTS, tok), jnp.float32)
    weight = jnp.zeros((EXPERTS, tok), jnp.float32)
    copies[0].wait()
    copies[1].wait()
    ids = ids_ref[...]
    gw = gw_ref[...]
    for k in range(top):
        hit = ids[k : k + 1, :] == name
        chosen = jnp.where(hit, 1.0, chosen)
        weight = jnp.where(hit, gw[k : k + 1, :], weight)
    count = jnp.dot(chosen.astype(jnp.bfloat16), earlier, preferred_element_type=jnp.float32)
    slot = jnp.where(chosen > 0.5, count, -1.0)
    blank = jnp.zeros((EXTRA - 2 * EXPERTS, tok), jnp.float32)
    table = jnp.concatenate([slot, weight, blank], axis=0)
    out_ref[:, width:] = table.T.astype(jnp.bfloat16)
    me = lax.axis_index("expert")
    x, y, c = me >> 3, (me >> 1) & 3, me & 1
    n = lax.broadcasted_iota(jnp.int32, (16, EXTRA), 0)
    spot = lax.broadcasted_iota(jnp.int32, (16, EXTRA), 1)
    k, f = n >> 1, n & 1
    along_y = x * (NY * NC) + ((y + k) & 3) * NC + ((c + f) & 1)
    along_x = ((x + k) & 3) * (NY * NC) + y * NC + ((c + f) & 1)
    mine = jnp.where(n < KF, jnp.where(c == 0, along_y, along_x), -EXTRA)
    q_ref[0] = jnp.where(mine == spot, 1.0, 0.0).astype(jnp.bfloat16)
    q_ref[1] = jnp.where(mine + EXPERTS == spot, 1.0, 0.0).astype(jnp.bfloat16)
    copies[2].wait()


def prep(ids, gw, tokens):
    tok, width = tokens.shape
    hbm = pl.BlockSpec(memory_space=pl.ANY)
    return pl.pallas_call(
        prep_kernel,
        in_specs=[hbm, hbm, hbm],
        out_specs=[pl.BlockSpec(memory_space=pltpu.VMEM)] * 2,
        out_shape=[
            pltpu.VMEM((tok, width + EXTRA), jnp.bfloat16),
            pltpu.VMEM((2, 16, EXTRA), jnp.bfloat16),
        ],
        scratch_shapes=[
            pltpu.VMEM(ids.shape, ids.dtype),
            pltpu.VMEM(gw.shape, gw.dtype),
            pltpu.SemaphoreType.DMA((3,)),
        ],
        compiler_params=pltpu.CompilerParams(vmem_limit_bytes=4 * 1024 * 1024),
        cost_estimate=pl.CostEstimate(flops=2 * EXPERTS * tok**2, bytes_accessed=4 * tok * width, transcendentals=0),
        name="prep",
    )(*[pltpu.with_memory_space_constraint(v, pltpu.HBM) for v in (ids, gw, tokens)])


def select(q, blocks):
    width = blocks[0].shape[1] - EXTRA
    return jnp.concatenate(
        [
            lax.dot_general(q, b[:, width:], (((1,), (1,)), ((), ())), preferred_element_type=jnp.float32)
            for b in blocks
        ],
        axis=1,
    )


def pack_kernel(which, q_ref, *refs):
    blocks, outs = refs[:4], refs[4:]
    tok = blocks[0].shape[0]
    width = outs[0].shape[1]
    q = q_ref[0]
    half = 2 * CAP
    r = lax.broadcasted_iota(jnp.int32, (half, 2 * tok), 0)
    t = lax.broadcasted_iota(jnp.int32, (half, 2 * tok), 1)
    second = r >= CAP
    target = jnp.where(second, r - CAP, r)
    target = jnp.where(second == (t >= tok), target, -5).astype(jnp.float32)
    cols = 512
    for p in range(2):
        pair = blocks[2 * p : 2 * p + 2]
        slots = select(q, pair)
        pick = jnp.concatenate(
            [
                jnp.where(slots[NC * k + f : NC * k + f + 1, :] == target, 1.0, 0.0).astype(jnp.bfloat16)
                for k in which
                for f in range(NC)
            ],
            axis=0,
        )
        for at in range(0, width, cols):
            block = jnp.concatenate([b[:, at : at + cols] for b in pair], axis=0)
            got = jnp.dot(pick, block, preferred_element_type=jnp.float32).astype(jnp.bfloat16)
            for n, o in enumerate(outs):
                o[2 * half * p : 2 * half * (p + 1), at : at + cols] = got[2 * half * n : 2 * half * (n + 1), :]


def pack(which, q, blocks):
    tok = blocks[0].shape[0]
    width = blocks[0].shape[1] - EXTRA
    count = len(which)
    rows = NC * 4 * CAP
    vmem = pl.BlockSpec(memory_space=pltpu.VMEM)
    return pl.pallas_call(
        functools.partial(pack_kernel, which),
        in_specs=[vmem] * 5,
        out_specs=[vmem] * count,
        out_shape=[jax.ShapeDtypeStruct((rows, width), jnp.bfloat16)] * count,
        compiler_params=pltpu.CompilerParams(vmem_limit_bytes=16 * 1024 * 1024),
        cost_estimate=pl.CostEstimate(
            flops=2 * rows * count * 2 * tok * width,
            bytes_accessed=2 * (4 * tok + rows * count) * width,
            transcendentals=0,
        ),
        name="pack",
    )(q, *blocks)


def combine_kernel(spots, q_ref, *refs):
    pair, backs, outs = refs[:2], refs[2:6], refs[6:]
    tok, width = outs[0].shape
    half = 2 * CAP
    span = half * KF
    lane = lax.broadcasted_iota(jnp.int32, (2 * tok, span), 1)
    part = jnp.zeros((2 * tok, span), jnp.int32)
    er = lax.broadcasted_iota(jnp.int32, (16, span), 0)
    el = lax.broadcasted_iota(jnp.int32, (16, span), 1)
    ep = jnp.zeros((16, span), jnp.int32)
    for n in range(1, KF):
        part = jnp.where(lane >= half * n, half * n, part)
        ep = jnp.where(el >= half * n, n, ep)
    r = lane - part
    t = lax.broadcasted_iota(jnp.int32, (2 * tok, span), 0)
    second = r >= CAP
    target = jnp.where(second, r - CAP, r)
    target = jnp.where(second == (t >= tok), target, -5).astype(jnp.float32)
    expand = jnp.where(er == ep, 1.0, 0.0).astype(jnp.bfloat16)

    def widen(v):
        return lax.dot_general(
            v.astype(jnp.bfloat16), expand, (((0,), (0,)), ((), ())), preferred_element_type=jnp.float32
        )

    mix = jnp.where(widen(select(q_ref[0], pair)) == target, widen(select(q_ref[1], pair)), 0.0)
    mix = mix.astype(jnp.bfloat16)
    cols = 512
    for at in range(0, width, cols):
        rows = jnp.concatenate(
            [b[2 * half * p : 2 * half * (p + 1), at : at + cols] for b, p in zip(backs, spots)], axis=0
        )
        got = jnp.dot(mix, rows, preferred_element_type=jnp.float32)
        for n, o in enumerate(outs):
            o[:, at : at + cols] = got[n * tok : (n + 1) * tok].astype(o.dtype)


def combine(q, pair, backs, spots, dtypes):
    tok = pair[0].shape[0]
    width = backs[0].shape[1]
    rows = NC * 4 * CAP
    vmem = pl.BlockSpec(memory_space=pltpu.VMEM)
    return pl.pallas_call(
        functools.partial(combine_kernel, spots),
        in_specs=[vmem] * 7,
        out_specs=[vmem] * 2,
        out_shape=[jax.ShapeDtypeStruct((tok, width), d) for d in dtypes],
        compiler_params=pltpu.CompilerParams(vmem_limit_bytes=16 * 1024 * 1024),
        cost_estimate=pl.CostEstimate(
            flops=2 * 2 * rows * 2 * tok * width,
            bytes_accessed=2 * (3 * tok + 2 * rows) * width,
            transcendentals=0,
        ),
        name="combine",
    )(q, *pair, *backs)


def expert_kernel(count, *refs):
    slabs, weights, outs = refs[:count], refs[count : count + 6], refs[count + 6 :]
    width = slabs[0].shape[1]
    half = 2 * CAP
    for f in range(NC):
        wg, wu, wd = weights[3 * f : 3 * f + 3]
        ff = wg.shape[-1]
        spots = [half * (2 * p + f) for p in range(2)]
        lines = jnp.concatenate([s[at : at + half, :] for s in slabs for at in spots], axis=0)
        hidden = []
        for at in range(0, ff, 256):
            gate = jnp.dot(lines, wg[0, :, at : at + 256], preferred_element_type=jnp.float32)
            up = jnp.dot(lines, wu[0, :, at : at + 256], preferred_element_type=jnp.float32)
            hidden.append((gate / (1.0 + jnp.exp(-gate)) * up).astype(jnp.bfloat16))
        hidden = jnp.concatenate(hidden, axis=1)
        for at in range(0, width, 512):
            got = jnp.dot(hidden, wd[0, :, at : at + 512], preferred_element_type=jnp.float32)
            got = got.astype(jnp.bfloat16)
            if len(outs) == count:
                places = [(o, spot) for o in outs for spot in spots]
            else:
                places = [(o, half * f) for o in outs]
            for n, (o, spot) in enumerate(places):
                o[spot : spot + half, at : at + 512] = got[n * half : (n + 1) * half]


def expert(slabs, weights, split=False):
    count = len(slabs)
    rows, width = slabs[0].shape
    ff = weights[0].shape[-1]
    outs = 2 * count if split else count
    vmem = pl.BlockSpec(memory_space=pltpu.VMEM)
    return pl.pallas_call(
        functools.partial(expert_kernel, count),
        in_specs=[vmem] * (count + 6),
        out_specs=[vmem] * outs,
        out_shape=[jax.ShapeDtypeStruct((rows * count // outs, width), jnp.bfloat16)] * outs,
        compiler_params=pltpu.CompilerParams(vmem_limit_bytes=16 * 1024 * 1024),
        cost_estimate=pl.CostEstimate(
            flops=6 * count * rows * width * ff,
            bytes_accessed=4 * count * rows * width,
            transcendentals=count * rows * ff,
        ),
        name="expert",
    )(*slabs, *[pltpu.with_memory_space_constraint(w, pltpu.VMEM) for w in weights])


def hold_kernel(*refs):
    ins, outs, sems = refs[:3], refs[3:6], refs[6]
    copies = [pltpu.make_async_copy(a, b, sems.at[n]) for n, (a, b) in enumerate(zip(ins, outs))]
    for copy in copies:
        copy.start()
    for copy in copies:
        copy.wait()


def hold(*weights):
    return pl.pallas_call(
        hold_kernel,
        in_specs=[pl.BlockSpec(memory_space=pl.ANY)] * 3,
        out_specs=[pl.BlockSpec(memory_space=pltpu.VMEM)] * 3,
        out_shape=[pltpu.VMEM(w.shape, w.dtype) for w in weights],
        scratch_shapes=[pltpu.SemaphoreType.DMA((3,))],
        compiler_params=pltpu.CompilerParams(vmem_limit_bytes=4 * 1024 * 1024),
        cost_estimate=pl.CostEstimate(flops=0, bytes_accessed=4 * weights[0].size * 3, transcendentals=0),
        name="hold",
    )(*[pltpu.with_memory_space_constraint(w, pltpu.HBM) for w in weights])


def per_device(tokens, expert_ids, gate_weights, w_gate, w_up, w_down):
    send = lambda v, pairs: lax.ppermute(v, "expert", pairs)
    after = lambda v, other: lax.optimization_barrier((v, other))[0]
    home, q = prep(expert_ids.T, gate_weights.T, tokens)
    blocks = [home] + [send(home, spread_pairs(j)) for j in (1, 2, 3)]
    weights = list(hold(w_gate, w_up, w_down)) + [send(w, swap_pairs()) for w in (w_gate, w_up)]

    near = pack((1, 3), q, blocks)
    weights.append(send(after(w_down, near[0]), swap_pairs()))
    arrived = {k: send(slab, deliver_pairs(k)) for k, slab in zip((1, 3), near)}
    stay, far = pack((0, 2), q, blocks)
    backs = {}
    (backs[0],) = expert([stay], weights)
    arrived[2] = send(after(far, (arrived[1], arrived[3])), deliver_pairs(2))
    for k, slab in zip((1, 3), expert([arrived[1], arrived[3]], weights)):
        backs[k] = send(slab, back(deliver_pairs(k)))
    early, late = expert([arrived[2]], weights, split=True)[::-1]
    early = send(early, back(deliver_pairs(2)))
    late = send(after(late, (backs[1], backs[3])), back(deliver_pairs(2)))

    whole = [backs[k] for k in (0, 1)]
    part2, part3 = combine(
        q, blocks[2:], [*whole, early, backs[3]], (1, 1, 0, 1), (jnp.bfloat16, jnp.bfloat16)
    )
    part0, part1 = combine(q, blocks[:2], [*whole, late, backs[3]], (0, 0, 0, 0), (jnp.float32, jnp.bfloat16))
    mixed = part0
    for j, part in ((2, part2), (3, part3), (1, part1)):
        mixed = mixed + send(part, back(spread_pairs(j))).astype(jnp.float32)
    return mixed.astype(jnp.bfloat16)


def solution(mesh):
    return jax.shard_map(
        per_device,
        mesh=mesh,
        in_specs=(
            P(("dp", "expert"), None),
            P(("dp", "expert"), None),
            P(("dp", "expert"), None),
            P("expert", None, None),
            P("expert", None, None),
            P("expert", None, None),
        ),
        out_specs=P(("dp", "expert"), None),
        check_vma=False,
    )
```

```python
import functools

import jax
import jax.numpy as jnp
from jax import lax
from jax.experimental import pallas as pl
from jax.experimental.pallas import tpu as pltpu
from jax.sharding import PartitionSpec as P

NX, NY, NC = 4, 4, 2
EXPERTS = NX * NY * NC
CAP = 40
EXTRA = 128
KF = 8


def index_of(x, y, c):
    return ((x % NX) * NY + (y % NY)) * NC + c


def spread_pairs(j):
    pairs = []
    for x in range(NX):
        for y in range(NY):
            pairs.append((index_of(x, y, 0), index_of(x + j, y, 0)))
            pairs.append((index_of(x, y, 1), index_of(x, y + j, 1)))
    return pairs


def deliver_pairs(k):
    pairs = []
    for x in range(NX):
        for y in range(NY):
            pairs.append((index_of(x, y, 0), index_of(x, y + k, 0)))
            pairs.append((index_of(x, y, 1), index_of(x + k, y, 1)))
    return pairs


def swap_pairs():
    return [(i, i ^ 1) for i in range(EXPERTS)]


def back(pairs):
    return [(b, a) for a, b in pairs]


def prep_kernel(ids_hbm, gw_hbm, tok_hbm, out_ref, q_ref, ids_ref, gw_ref, sems):
    top, tok = ids_ref.shape
    width = tok_hbm.shape[1]
    copies = [
        pltpu.make_async_copy(ids_hbm, ids_ref, sems.at[0]),
        pltpu.make_async_copy(gw_hbm, gw_ref, sems.at[1]),
        pltpu.make_async_copy(tok_hbm, out_ref.at[:, pl.ds(0, width)], sems.at[2]),
    ]
    for copy in copies:
        copy.start()
    row = lax.broadcasted_iota(jnp.int32, (tok, tok), 0)
    col = lax.broadcasted_iota(jnp.int32, (tok, tok), 1)
    earlier = jnp.where(row < col, 1.0, 0.0).astype(jnp.bfloat16)
    name = lax.broadcasted_iota(jnp.int32, (EXPERTS, tok), 0)
    chosen = jnp.zeros((EXPERTS, tok), jnp.float32)
    weight = jnp.zeros((EXPERTS, tok), jnp.float32)
    copies[0].wait()
    copies[1].wait()
    ids = ids_ref[...]
    gw = gw_ref[...]
    for k in range(top):
        hit = ids[k : k + 1, :] == name
        chosen = jnp.where(hit, 1.0, chosen)
        weight = jnp.where(hit, gw[k : k + 1, :], weight)
    count = jnp.dot(chosen.astype(jnp.bfloat16), earlier, preferred_element_type=jnp.float32)
    slot = jnp.where(chosen > 0.5, count, -1.0)
    blank = jnp.zeros((EXTRA - 2 * EXPERTS, tok), jnp.float32)
    table = jnp.concatenate([slot, weight, blank], axis=0)
    out_ref[:, width:] = table.T.astype(jnp.bfloat16)
    me = lax.axis_index("expert")
    x, y, c = me >> 3, (me >> 1) & 3, me & 1
    n = lax.broadcasted_iota(jnp.int32, (16, EXTRA), 0)
    spot = lax.broadcasted_iota(jnp.int32, (16, EXTRA), 1)
    k, f = n >> 1, n & 1
    along_y = x * (NY * NC) + ((y + k) & 3) * NC + ((c + f) & 1)
    along_x = ((x + k) & 3) * (NY * NC) + y * NC + ((c + f) & 1)
    mine = jnp.where(n < KF, jnp.where(c == 0, along_y, along_x), -EXTRA)
    q_ref[0] = jnp.where(mine == spot, 1.0, 0.0).astype(jnp.bfloat16)
    q_ref[1] = jnp.where(mine + EXPERTS == spot, 1.0, 0.0).astype(jnp.bfloat16)
    copies[2].wait()


def prep(ids, gw, tokens):
    tok, width = tokens.shape
    hbm = pl.BlockSpec(memory_space=pl.ANY)
    return pl.pallas_call(
        prep_kernel,
        in_specs=[hbm, hbm, hbm],
        out_specs=[pl.BlockSpec(memory_space=pltpu.VMEM)] * 2,
        out_shape=[
            pltpu.VMEM((tok, width + EXTRA), jnp.bfloat16),
            pltpu.VMEM((2, 16, EXTRA), jnp.bfloat16),
        ],
        scratch_shapes=[
            pltpu.VMEM(ids.shape, ids.dtype),
            pltpu.VMEM(gw.shape, gw.dtype),
            pltpu.SemaphoreType.DMA((3,)),
        ],
        compiler_params=pltpu.CompilerParams(vmem_limit_bytes=4 * 1024 * 1024),
        cost_estimate=pl.CostEstimate(flops=2 * EXPERTS * tok**2, bytes_accessed=4 * tok * width, transcendentals=0),
        name="prep",
    )(*[pltpu.with_memory_space_constraint(v, pltpu.HBM) for v in (ids, gw, tokens)])


def select(q, blocks):
    width = blocks[0].shape[1] - EXTRA
    return jnp.concatenate(
        [
            lax.dot_general(q, b[:, width:], (((1,), (1,)), ((), ())), preferred_element_type=jnp.float32)
            for b in blocks
        ],
        axis=1,
    )


def pack_kernel(which, q_ref, *refs):
    outs = refs[len(refs) - len(which) :]
    blocks = refs[: len(refs) - len(which)]
    tok = blocks[0].shape[0]
    width = outs[0].shape[1]
    q = q_ref[0]
    half = 2 * CAP
    r = lax.broadcasted_iota(jnp.int32, (half, 2 * tok), 0)
    t = lax.broadcasted_iota(jnp.int32, (half, 2 * tok), 1)
    second = r >= CAP
    target = jnp.where(second, r - CAP, r)
    target = jnp.where(second == (t >= tok), target, -5).astype(jnp.float32)
    cols = 512
    for p in range(len(blocks) // 2):
        pair = blocks[2 * p : 2 * p + 2]
        slots = select(q, pair)
        pick = jnp.concatenate(
            [
                jnp.where(slots[NC * k + f : NC * k + f + 1, :] == target, 1.0, 0.0).astype(jnp.bfloat16)
                for k in which
                for f in range(NC)
            ],
            axis=0,
        )
        for at in range(0, width, cols):
            block = jnp.concatenate([b[:, at : at + cols] for b in pair], axis=0)
            got = jnp.dot(pick, block, preferred_element_type=jnp.float32).astype(jnp.bfloat16)
            for n, o in enumerate(outs):
                o[2 * half * p : 2 * half * (p + 1), at : at + cols] = got[2 * half * n : 2 * half * (n + 1), :]


def pack(which, q, blocks):
    tok = blocks[0].shape[0]
    width = blocks[0].shape[1] - EXTRA
    count = len(which)
    rows = NC * len(blocks) * CAP
    vmem = pl.BlockSpec(memory_space=pltpu.VMEM)
    return pl.pallas_call(
        functools.partial(pack_kernel, which),
        in_specs=[vmem] * (1 + len(blocks)),
        out_specs=[vmem] * count,
        out_shape=[jax.ShapeDtypeStruct((rows, width), jnp.bfloat16)] * count,
        compiler_params=pltpu.CompilerParams(vmem_limit_bytes=16 * 1024 * 1024),
        cost_estimate=pl.CostEstimate(
            flops=2 * rows * count * 2 * tok * width,
            bytes_accessed=2 * (len(blocks) * tok + rows * count) * width,
            transcendentals=0,
        ),
        name="pack",
    )(q, *blocks)


def combine_kernel(spots, q_ref, *refs):
    pair, backs, outs = refs[:2], refs[2:6], refs[6:]
    tok, width = outs[0].shape
    half = 2 * CAP
    span = half * KF
    lane = lax.broadcasted_iota(jnp.int32, (2 * tok, span), 1)
    part = jnp.zeros((2 * tok, span), jnp.int32)
    er = lax.broadcasted_iota(jnp.int32, (16, span), 0)
    el = lax.broadcasted_iota(jnp.int32, (16, span), 1)
    ep = jnp.zeros((16, span), jnp.int32)
    for n in range(1, KF):
        part = jnp.where(lane >= half * n, half * n, part)
        ep = jnp.where(el >= half * n, n, ep)
    r = lane - part
    t = lax.broadcasted_iota(jnp.int32, (2 * tok, span), 0)
    second = r >= CAP
    target = jnp.where(second, r - CAP, r)
    target = jnp.where(second == (t >= tok), target, -5).astype(jnp.float32)
    expand = jnp.where(er == ep, 1.0, 0.0).astype(jnp.bfloat16)

    def widen(v):
        return lax.dot_general(
            v.astype(jnp.bfloat16), expand, (((0,), (0,)), ((), ())), preferred_element_type=jnp.float32
        )

    mix = jnp.where(widen(select(q_ref[0], pair)) == target, widen(select(q_ref[1], pair)), 0.0)
    mix = mix.astype(jnp.bfloat16)
    cols = 512
    for at in range(0, width, cols):
        rows = jnp.concatenate(
            [b[2 * half * p : 2 * half * (p + 1), at : at + cols] for b, p in zip(backs, spots)], axis=0
        )
        got = jnp.dot(mix, rows, preferred_element_type=jnp.float32)
        for n, o in enumerate(outs):
            o[:, at : at + cols] = got[n * tok : (n + 1) * tok].astype(o.dtype)


def combine(q, pair, backs, spots, dtypes):
    tok = pair[0].shape[0]
    width = backs[0].shape[1]
    rows = NC * 4 * CAP
    vmem = pl.BlockSpec(memory_space=pltpu.VMEM)
    return pl.pallas_call(
        functools.partial(combine_kernel, spots),
        in_specs=[vmem] * 7,
        out_specs=[vmem] * 2,
        out_shape=[jax.ShapeDtypeStruct((tok, width), d) for d in dtypes],
        compiler_params=pltpu.CompilerParams(vmem_limit_bytes=16 * 1024 * 1024),
        cost_estimate=pl.CostEstimate(
            flops=2 * 2 * rows * 2 * tok * width,
            bytes_accessed=2 * (3 * tok + 2 * rows) * width,
            transcendentals=0,
        ),
        name="combine",
    )(q, *pair, *backs)


def halves(refs):
    size = 2 * NC * CAP
    return [(ref, at) for ref in refs for at in range(0, ref.shape[0], size)]


def expert_kernel(count, ff, *refs):
    slabs, bundles, outs = refs[:count], refs[count : count + 2], refs[count + 2 :]
    width = slabs[0].shape[1]
    half = 2 * CAP
    for f, w in enumerate(bundles):
        lines = jnp.concatenate([s[at + half * f : at + half * (f + 1), :] for s, at in halves(slabs)], axis=0)
        hidden = []
        for at in range(0, ff, 256):
            gate = jnp.dot(lines, w[:width, at : at + 256], preferred_element_type=jnp.float32)
            up = jnp.dot(lines, w[:width, ff + at : ff + at + 256], preferred_element_type=jnp.float32)
            hidden.append((gate / (1.0 + jnp.exp(-gate)) * up).astype(jnp.bfloat16))
        whole = jnp.concatenate(hidden, axis=1)
        for at in range(0, width, 512):
            if at < 2 * ff:
                down = w[width : width + ff, at : at + 512]
            else:
                down = jnp.concatenate([w[width + ff :, 512 * i : 512 * (i + 1)] for i in range(ff // 256)], axis=0)
            got = jnp.dot(whole, down, preferred_element_type=jnp.float32)
            got = got.astype(jnp.bfloat16)
            for n, (o, to) in enumerate(halves(outs)):
                o[to + half * f : to + half * (f + 1), at : at + 512] = got[n * half : (n + 1) * half]


def expert(slabs, bundles, outs):
    count = len(slabs)
    rows = sum(s.shape[0] for s in slabs)
    width = slabs[0].shape[1]
    ff = bundles[0].shape[1] // 2
    vmem = pl.BlockSpec(memory_space=pltpu.VMEM)
    return pl.pallas_call(
        functools.partial(expert_kernel, count, ff),
        in_specs=[vmem] * (count + 2),
        out_specs=[vmem] * outs,
        out_shape=[jax.ShapeDtypeStruct((rows // outs, width), jnp.bfloat16)] * outs,
        compiler_params=pltpu.CompilerParams(vmem_limit_bytes=16 * 1024 * 1024),
        cost_estimate=pl.CostEstimate(
            flops=6 * rows * width * ff,
            bytes_accessed=4 * rows * width,
            transcendentals=rows * ff,
        ),
        name="expert",
    )(*slabs, *[pltpu.with_memory_space_constraint(w, pltpu.VMEM) for w in bundles])


def hold_kernel(wg, wu, wd, out_ref, mark_ref, sems):
    width, ff = wg.shape[1:]
    moves = [
        (wg.at[0], out_ref.at[pl.ds(0, width), pl.ds(0, ff)]),
        (wu.at[0], out_ref.at[pl.ds(0, width), pl.ds(ff, ff)]),
        (wd.at[0, :, pl.ds(0, 2 * ff)], out_ref.at[pl.ds(width, ff)]),
    ]
    for i in range(ff // 256):
        moves.append(
            (
                wd.at[0, pl.ds(256 * i, 256), pl.ds(2 * ff, 512)],
                out_ref.at[pl.ds(width + ff, 256), pl.ds(512 * i, 512)],
            )
        )
    copies = [pltpu.make_async_copy(a, b, sems.at[n]) for n, (a, b) in enumerate(moves)]
    for copy in copies:
        copy.start()
    mark_ref[...] = jnp.zeros_like(mark_ref)
    for copy in copies:
        copy.wait()


def hold(*weights):
    width, ff = weights[0].shape[1:]
    return pl.pallas_call(
        hold_kernel,
        in_specs=[pl.BlockSpec(memory_space=pl.ANY)] * 3,
        out_specs=[pl.BlockSpec(memory_space=pltpu.VMEM)] * 2,
        out_shape=[
            pltpu.VMEM((width + ff + 256, 2 * ff), weights[0].dtype),
            pltpu.VMEM((8, 128), jnp.float32),
        ],
        scratch_shapes=[pltpu.SemaphoreType.DMA((6,))],
        compiler_params=pltpu.CompilerParams(vmem_limit_bytes=4 * 1024 * 1024),
        cost_estimate=pl.CostEstimate(flops=0, bytes_accessed=4 * weights[0].size * 3, transcendentals=0),
        name="hold",
    )(*[pltpu.with_memory_space_constraint(w, pltpu.HBM) for w in weights])[0]


def per_device(tokens, expert_ids, gate_weights, w_gate, w_up, w_down):
    send = lambda v, pairs: lax.ppermute(v, "expert", pairs)
    after = lambda v, other: lax.optimization_barrier((v, other))[0]
    home, q = prep(expert_ids.T, gate_weights.T, tokens)
    moved = {j: send(home, spread_pairs(j)) for j in (1, 3, 2)}
    pairs = [[home, moved[2]], [moved[1], moved[3]]]
    near = [pack((1, 3), q, pair) for pair in pairs]
    bundle = hold(w_gate, w_up, w_down)
    weights = [bundle, send(after(bundle, moved[2]), swap_pairs())]

    arrived = {k: [send(slabs[n], deliver_pairs(k)) for slabs in near] for n, k in enumerate((1, 3))}
    stay, far = pack((0, 2), q, pairs[0] + pairs[1])
    backs = {}
    (backs[0],) = expert([stay], weights, 1)
    arrived[2] = [send(after(far, (arrived[1], arrived[3])), deliver_pairs(2))]
    for k, slab in zip((1, 3), expert(arrived[1] + arrived[3], weights, 2)):
        backs[k] = send(slab, back(deliver_pairs(k)))
    early, late = expert(arrived[2], weights, 2)
    early = send(early, back(deliver_pairs(2)))
    late = send(after(late, (backs[1], backs[3])), back(deliver_pairs(2)))

    whole = [backs[k] for k in (0, 1)]
    part0, part2 = combine(q, pairs[0], [*whole, early, backs[3]], (0, 0, 0, 0), (jnp.float32, jnp.bfloat16))
    part1, part3 = combine(q, pairs[1], [*whole, late, backs[3]], (1, 1, 0, 1), (jnp.bfloat16, jnp.bfloat16))
    mixed = part0
    for j, part in ((2, part2), (1, part1), (3, part3)):
        mixed = mixed + send(part, back(spread_pairs(j))).astype(jnp.float32)
    return mixed.astype(jnp.bfloat16)


def solution(mesh):
    return jax.shard_map(
        per_device,
        mesh=mesh,
        in_specs=(
            P(("dp", "expert"), None),
            P(("dp", "expert"), None),
            P(("dp", "expert"), None),
            P("expert", None, None),
            P("expert", None, None),
            P("expert", None, None),
        ),
        out_specs=P(("dp", "expert"), None),
        check_vma=False,
    )
```

```python
import functools

import jax
import jax.numpy as jnp
from jax import lax
from jax.experimental import pallas as pl
from jax.experimental.pallas import tpu as pltpu
from jax.sharding import PartitionSpec as P

NX, NY, NC = 4, 4, 2
EXPERTS = NX * NY * NC
CAP = 40
EXTRA = 128
KF = 8


def index_of(x, y, c):
    return ((x % NX) * NY + (y % NY)) * NC + c


def spread_pairs(j):
    pairs = []
    for x in range(NX):
        for y in range(NY):
            pairs.append((index_of(x, y, 0), index_of(x + j, y, 0)))
            pairs.append((index_of(x, y, 1), index_of(x, y + j, 1)))
    return pairs


def deliver_pairs(k):
    pairs = []
    for x in range(NX):
        for y in range(NY):
            pairs.append((index_of(x, y, 0), index_of(x, y + k, 0)))
            pairs.append((index_of(x, y, 1), index_of(x + k, y, 1)))
    return pairs


def swap_pairs():
    return [(i, i ^ 1) for i in range(EXPERTS)]


def back(pairs):
    return [(b, a) for a, b in pairs]


def prep_kernel(ids_hbm, gw_hbm, tok_hbm, out_ref, q_ref, ids_ref, gw_ref, sems):
    top, tok = ids_ref.shape
    width = tok_hbm.shape[1]
    copies = [
        pltpu.make_async_copy(ids_hbm, ids_ref, sems.at[0]),
        pltpu.make_async_copy(gw_hbm, gw_ref, sems.at[1]),
        pltpu.make_async_copy(tok_hbm, out_ref.at[:, pl.ds(0, width)], sems.at[2]),
    ]
    for copy in copies:
        copy.start()
    row = lax.broadcasted_iota(jnp.int32, (tok, tok), 0)
    col = lax.broadcasted_iota(jnp.int32, (tok, tok), 1)
    earlier = jnp.where(row < col, 1.0, 0.0).astype(jnp.bfloat16)
    name = lax.broadcasted_iota(jnp.int32, (EXPERTS, tok), 0)
    chosen = jnp.zeros((EXPERTS, tok), jnp.float32)
    weight = jnp.zeros((EXPERTS, tok), jnp.float32)
    copies[0].wait()
    copies[1].wait()
    ids = ids_ref[...]
    gw = gw_ref[...]
    for k in range(top):
        hit = ids[k : k + 1, :] == name
        chosen = jnp.where(hit, 1.0, chosen)
        weight = jnp.where(hit, gw[k : k + 1, :], weight)
    count = jnp.dot(chosen.astype(jnp.bfloat16), earlier, preferred_element_type=jnp.float32)
    slot = jnp.where(chosen > 0.5, count, -1.0)
    blank = jnp.zeros((EXTRA - 2 * EXPERTS, tok), jnp.float32)
    table = jnp.concatenate([slot, weight, blank], axis=0)
    out_ref[:, width:] = table.T.astype(jnp.bfloat16)
    me = lax.axis_index("expert")
    x, y, c = me >> 3, (me >> 1) & 3, me & 1
    n = lax.broadcasted_iota(jnp.int32, (16, EXTRA), 0)
    spot = lax.broadcasted_iota(jnp.int32, (16, EXTRA), 1)
    k, f = n >> 1, n & 1
    along_y = x * (NY * NC) + ((y + k) & 3) * NC + ((c + f) & 1)
    along_x = ((x + k) & 3) * (NY * NC) + y * NC + ((c + f) & 1)
    mine = jnp.where(n < KF, jnp.where(c == 0, along_y, along_x), -EXTRA)
    q_ref[0] = jnp.where(mine == spot, 1.0, 0.0).astype(jnp.bfloat16)
    q_ref[1] = jnp.where(mine + EXPERTS == spot, 1.0, 0.0).astype(jnp.bfloat16)
    copies[2].wait()


def prep(ids, gw, tokens):
    tok, width = tokens.shape
    hbm = pl.BlockSpec(memory_space=pl.ANY)
    return pl.pallas_call(
        prep_kernel,
        in_specs=[hbm, hbm, hbm],
        out_specs=[pl.BlockSpec(memory_space=pltpu.VMEM)] * 2,
        out_shape=[
            pltpu.VMEM((tok, width + EXTRA), jnp.bfloat16),
            pltpu.VMEM((2, 16, EXTRA), jnp.bfloat16),
        ],
        scratch_shapes=[
            pltpu.VMEM(ids.shape, ids.dtype),
            pltpu.VMEM(gw.shape, gw.dtype),
            pltpu.SemaphoreType.DMA((3,)),
        ],
        compiler_params=pltpu.CompilerParams(vmem_limit_bytes=4 * 1024 * 1024),
        cost_estimate=pl.CostEstimate(flops=2 * EXPERTS * tok**2, bytes_accessed=4 * tok * width, transcendentals=0),
        name="prep",
    )(*[pltpu.with_memory_space_constraint(v, pltpu.HBM) for v in (ids, gw, tokens)])


def select(q, blocks):
    width = blocks[0].shape[1] - EXTRA
    return jnp.concatenate(
        [
            lax.dot_general(q, b[:, width:], (((1,), (1,)), ((), ())), preferred_element_type=jnp.float32)
            for b in blocks
        ],
        axis=1,
    )


def pack_kernel(which, q_ref, *refs):
    outs = refs[len(refs) - len(which) :]
    blocks = refs[: len(refs) - len(which)]
    tok = blocks[0].shape[0]
    width = outs[0].shape[1]
    q = q_ref[0]
    half = 2 * CAP
    r = lax.broadcasted_iota(jnp.int32, (half, 2 * tok), 0)
    t = lax.broadcasted_iota(jnp.int32, (half, 2 * tok), 1)
    second = r >= CAP
    target = jnp.where(second, r - CAP, r)
    target = jnp.where(second == (t >= tok), target, -5).astype(jnp.float32)
    cols = 512
    for p in range(len(blocks) // 2):
        pair = blocks[2 * p : 2 * p + 2]
        slots = select(q, pair)
        pick = jnp.concatenate(
            [
                jnp.where(slots[NC * k + f : NC * k + f + 1, :] == target, 1.0, 0.0).astype(jnp.bfloat16)
                for k in which
                for f in range(NC)
            ],
            axis=0,
        )
        for at in range(0, width, cols):
            block = jnp.concatenate([b[:, at : at + cols] for b in pair], axis=0)
            got = jnp.dot(pick, block, preferred_element_type=jnp.float32).astype(jnp.bfloat16)
            for n, o in enumerate(outs):
                o[2 * half * p : 2 * half * (p + 1), at : at + cols] = got[2 * half * n : 2 * half * (n + 1), :]


def pack(which, q, blocks):
    tok = blocks[0].shape[0]
    width = blocks[0].shape[1] - EXTRA
    count = len(which)
    rows = NC * len(blocks) * CAP
    vmem = pl.BlockSpec(memory_space=pltpu.VMEM)
    return pl.pallas_call(
        functools.partial(pack_kernel, which),
        in_specs=[vmem] * (1 + len(blocks)),
        out_specs=[vmem] * count,
        out_shape=[jax.ShapeDtypeStruct((rows, width), jnp.bfloat16)] * count,
        compiler_params=pltpu.CompilerParams(vmem_limit_bytes=16 * 1024 * 1024),
        cost_estimate=pl.CostEstimate(
            flops=2 * rows * count * 2 * tok * width,
            bytes_accessed=2 * (len(blocks) * tok + rows * count) * width,
            transcendentals=0,
        ),
        name="pack",
    )(q, *blocks)


def combine_kernel(spots, q_ref, *refs):
    pair, backs, outs = refs[:2], refs[2:6], refs[6:]
    tok, width = outs[0].shape
    half = 2 * CAP
    span = half * KF
    lane = lax.broadcasted_iota(jnp.int32, (2 * tok, span), 1)
    part = jnp.zeros((2 * tok, span), jnp.int32)
    er = lax.broadcasted_iota(jnp.int32, (16, span), 0)
    el = lax.broadcasted_iota(jnp.int32, (16, span), 1)
    ep = jnp.zeros((16, span), jnp.int32)
    for n in range(1, KF):
        part = jnp.where(lane >= half * n, half * n, part)
        ep = jnp.where(el >= half * n, n, ep)
    r = lane - part
    t = lax.broadcasted_iota(jnp.int32, (2 * tok, span), 0)
    second = r >= CAP
    target = jnp.where(second, r - CAP, r)
    target = jnp.where(second == (t >= tok), target, -5).astype(jnp.float32)
    expand = jnp.where(er == ep, 1.0, 0.0).astype(jnp.bfloat16)

    def widen(v):
        return lax.dot_general(
            v.astype(jnp.bfloat16), expand, (((0,), (0,)), ((), ())), preferred_element_type=jnp.float32
        )

    mix = jnp.where(widen(select(q_ref[0], pair)) == target, widen(select(q_ref[1], pair)), 0.0)
    mix = mix.astype(jnp.bfloat16)
    cols = 512
    for at in range(0, width, cols):
        rows = jnp.concatenate(
            [b[2 * half * p : 2 * half * (p + 1), at : at + cols] for b, p in zip(backs, spots)], axis=0
        )
        got = jnp.dot(mix, rows, preferred_element_type=jnp.float32)
        for n, o in enumerate(outs):
            o[:, at : at + cols] = got[n * tok : (n + 1) * tok].astype(o.dtype)


def combine(q, pair, backs, spots, dtypes):
    tok = pair[0].shape[0]
    width = backs[0].shape[1]
    rows = NC * 4 * CAP
    vmem = pl.BlockSpec(memory_space=pltpu.VMEM)
    return pl.pallas_call(
        functools.partial(combine_kernel, spots),
        in_specs=[vmem] * 7,
        out_specs=[vmem] * 2,
        out_shape=[jax.ShapeDtypeStruct((tok, width), d) for d in dtypes],
        compiler_params=pltpu.CompilerParams(vmem_limit_bytes=16 * 1024 * 1024),
        cost_estimate=pl.CostEstimate(
            flops=2 * 2 * rows * 2 * tok * width,
            bytes_accessed=2 * (3 * tok + 2 * rows) * width,
            transcendentals=0,
        ),
        name="combine",
    )(q, *pair, *backs)


def halves(refs):
    size = 2 * NC * CAP
    return [(ref, at) for ref in refs for at in range(0, ref.shape[0], size)]


def expert_kernel(count, ff, *refs):
    slabs, bundles, outs = refs[:count], refs[count : count + 2], refs[count + 2 :]
    width = slabs[0].shape[1]
    half = 2 * CAP
    for f, w in enumerate(bundles):
        lines = jnp.concatenate([s[at + half * f : at + half * (f + 1), :] for s, at in halves(slabs)], axis=0)
        hidden = []
        for at in range(0, ff, 256):
            gate = jnp.dot(lines, w[:width, at : at + 256], preferred_element_type=jnp.float32)
            up = jnp.dot(lines, w[:width, ff + at : ff + at + 256], preferred_element_type=jnp.float32)
            hidden.append((gate / (1.0 + jnp.exp(-gate)) * up).astype(jnp.bfloat16))
        whole = jnp.concatenate(hidden, axis=1)
        for at in range(0, width, 512):
            if at < 2 * ff:
                down = w[width : width + ff, at : at + 512]
            else:
                down = jnp.concatenate([w[width + ff :, 512 * i : 512 * (i + 1)] for i in range(ff // 256)], axis=0)
            got = jnp.dot(whole, down, preferred_element_type=jnp.float32)
            got = got.astype(jnp.bfloat16)
            for n, (o, to) in enumerate(halves(outs)):
                o[to + half * f : to + half * (f + 1), at : at + 512] = got[n * half : (n + 1) * half]


def expert(slabs, bundles, outs):
    count = len(slabs)
    rows = sum(s.shape[0] for s in slabs)
    width = slabs[0].shape[1]
    ff = bundles[0].shape[1] // 2
    vmem = pl.BlockSpec(memory_space=pltpu.VMEM)
    return pl.pallas_call(
        functools.partial(expert_kernel, count, ff),
        in_specs=[vmem] * (count + 2),
        out_specs=[vmem] * outs,
        out_shape=[jax.ShapeDtypeStruct((rows // outs, width), jnp.bfloat16)] * outs,
        compiler_params=pltpu.CompilerParams(vmem_limit_bytes=16 * 1024 * 1024),
        cost_estimate=pl.CostEstimate(
            flops=6 * rows * width * ff,
            bytes_accessed=4 * rows * width,
            transcendentals=rows * ff,
        ),
        name="expert",
    )(*slabs, *[pltpu.with_memory_space_constraint(w, pltpu.VMEM) for w in bundles])


def hold_kernel(wg, wu, wd, out_ref, mark_ref, sems):
    width, ff = wg.shape[1:]
    moves = [
        (wg.at[0], out_ref.at[pl.ds(0, width), pl.ds(0, ff)]),
        (wu.at[0], out_ref.at[pl.ds(0, width), pl.ds(ff, ff)]),
        (wd.at[0, :, pl.ds(0, 2 * ff)], out_ref.at[pl.ds(width, ff)]),
    ]
    for i in range(ff // 256):
        moves.append(
            (
                wd.at[0, pl.ds(256 * i, 256), pl.ds(2 * ff, 512)],
                out_ref.at[pl.ds(width + ff, 256), pl.ds(512 * i, 512)],
            )
        )
    copies = [pltpu.make_async_copy(a, b, sems.at[n]) for n, (a, b) in enumerate(moves)]
    for copy in copies:
        copy.start()
    mark_ref[...] = jnp.zeros_like(mark_ref)
    for copy in copies:
        copy.wait()


def hold(*weights):
    width, ff = weights[0].shape[1:]
    return pl.pallas_call(
        hold_kernel,
        in_specs=[pl.BlockSpec(memory_space=pl.ANY)] * 3,
        out_specs=[pl.BlockSpec(memory_space=pltpu.VMEM)] * 2,
        out_shape=[
            pltpu.VMEM((width + ff + 256, 2 * ff), weights[0].dtype),
            pltpu.VMEM((8, 128), jnp.float32),
        ],
        scratch_shapes=[pltpu.SemaphoreType.DMA((6,))],
        compiler_params=pltpu.CompilerParams(vmem_limit_bytes=4 * 1024 * 1024),
        cost_estimate=pl.CostEstimate(flops=0, bytes_accessed=4 * weights[0].size * 3, transcendentals=0),
        name="hold",
    )(*[pltpu.with_memory_space_constraint(w, pltpu.HBM) for w in weights])[0]


def per_device(tokens, expert_ids, gate_weights, w_gate, w_up, w_down):
    send = lambda v, pairs: lax.ppermute(v, "expert", pairs)
    after = lambda v, other: lax.optimization_barrier((v, other))[0]
    home, q = prep(expert_ids.T, gate_weights.T, tokens)
    moved = {j: send(home, spread_pairs(j)) for j in (1, 2, 3)}
    pairs = [[home, moved[2]], [moved[1], moved[3]]]
    bundle = hold(w_gate, w_up, w_down)

    near = pack((1, 3), q, pairs[0] + pairs[1])
    weights = [bundle, send(after(bundle, near[0]), swap_pairs())]
    arrived = {k: send(slab, deliver_pairs(k)) for k, slab in zip((1, 3), near)}
    stay, far = pack((0, 2), q, pairs[0] + pairs[1])
    backs = {}
    (backs[0],) = expert([stay], weights, 1)
    arrived[2] = send(after(far, (arrived[1], arrived[3])), deliver_pairs(2))
    for k, slab in zip((1, 3), expert([arrived[1], arrived[3]], weights, 2)):
        backs[k] = send(slab, back(deliver_pairs(k)))
    late, early = expert([arrived[2]], weights, 2)
    early = send(early, back(deliver_pairs(2)))
    late = send(after(late, (backs[1], backs[3])), back(deliver_pairs(2)))

    whole = [backs[k] for k in (0, 1)]
    part1, part3 = combine(q, pairs[1], [*whole, early, backs[3]], (1, 1, 0, 1), (jnp.bfloat16, jnp.bfloat16))
    part0, part2 = combine(q, pairs[0], [*whole, late, backs[3]], (0, 0, 0, 0), (jnp.float32, jnp.bfloat16))
    mixed = part0
    for j, part in ((1, part1), (3, part3), (2, part2)):
        mixed = mixed + send(part, back(spread_pairs(j))).astype(jnp.float32)
    return mixed.astype(jnp.bfloat16)


def solution(mesh):
    return jax.shard_map(
        per_device,
        mesh=mesh,
        in_specs=(
            P(("dp", "expert"), None),
            P(("dp", "expert"), None),
            P(("dp", "expert"), None),
            P("expert", None, None),
            P("expert", None, None),
            P("expert", None, None),
        ),
        out_specs=P(("dp", "expert"), None),
        check_vma=False,
    )
```

```python
import functools

import jax
import jax.numpy as jnp
from jax import lax
from jax.experimental import pallas as pl
from jax.experimental.pallas import tpu as pltpu
from jax.sharding import PartitionSpec as P

NX, NY, NC = 4, 4, 2
EXPERTS = NX * NY * NC
CAP = 40
EXTRA = 128
KF = 8


def index_of(x, y, c):
    return ((x % NX) * NY + (y % NY)) * NC + c


def spread_pairs(j):
    pairs = []
    for x in range(NX):
        for y in range(NY):
            pairs.append((index_of(x, y, 0), index_of(x + j, y, 0)))
            pairs.append((index_of(x, y, 1), index_of(x, y + j, 1)))
    return pairs


def deliver_pairs(k):
    pairs = []
    for x in range(NX):
        for y in range(NY):
            pairs.append((index_of(x, y, 0), index_of(x, y + k, 0)))
            pairs.append((index_of(x, y, 1), index_of(x + k, y, 1)))
    return pairs


def swap_pairs():
    return [(i, i ^ 1) for i in range(EXPERTS)]


def back(pairs):
    return [(b, a) for a, b in pairs]


def prep_kernel(ids_hbm, gw_hbm, tok_hbm, out_ref, q_ref, ids_ref, gw_ref, sems):
    top, tok = ids_ref.shape
    width = tok_hbm.shape[1]
    copies = [
        pltpu.make_async_copy(ids_hbm, ids_ref, sems.at[0]),
        pltpu.make_async_copy(gw_hbm, gw_ref, sems.at[1]),
        pltpu.make_async_copy(tok_hbm, out_ref.at[:, pl.ds(0, width)], sems.at[2]),
    ]
    for copy in copies:
        copy.start()
    row = lax.broadcasted_iota(jnp.int32, (tok, tok), 0)
    col = lax.broadcasted_iota(jnp.int32, (tok, tok), 1)
    earlier = jnp.where(row < col, 1.0, 0.0).astype(jnp.bfloat16)
    name = lax.broadcasted_iota(jnp.int32, (EXPERTS, tok), 0)
    chosen = jnp.zeros((EXPERTS, tok), jnp.float32)
    weight = jnp.zeros((EXPERTS, tok), jnp.float32)
    copies[0].wait()
    copies[1].wait()
    ids = ids_ref[...]
    gw = gw_ref[...]
    for k in range(top):
        hit = ids[k : k + 1, :] == name
        chosen = jnp.where(hit, 1.0, chosen)
        weight = jnp.where(hit, gw[k : k + 1, :], weight)
    count = jnp.dot(chosen.astype(jnp.bfloat16), earlier, preferred_element_type=jnp.float32)
    slot = jnp.where(chosen > 0.5, count, -1.0)
    blank = jnp.zeros((EXTRA - 2 * EXPERTS, tok), jnp.float32)
    table = jnp.concatenate([slot, weight, blank], axis=0)
    out_ref[:, width:] = table.T.astype(jnp.bfloat16)
    me = lax.axis_index("expert")
    x, y, c = me >> 3, (me >> 1) & 3, me & 1
    n = lax.broadcasted_iota(jnp.int32, (16, EXTRA), 0)
    spot = lax.broadcasted_iota(jnp.int32, (16, EXTRA), 1)
    k, f = n >> 1, n & 1
    along_y = x * (NY * NC) + ((y + k) & 3) * NC + ((c + f) & 1)
    along_x = ((x + k) & 3) * (NY * NC) + y * NC + ((c + f) & 1)
    mine = jnp.where(n < KF, jnp.where(c == 0, along_y, along_x), -EXTRA)
    q_ref[0] = jnp.where(mine == spot, 1.0, 0.0).astype(jnp.bfloat16)
    q_ref[1] = jnp.where(mine + EXPERTS == spot, 1.0, 0.0).astype(jnp.bfloat16)
    copies[2].wait()


def prep(ids, gw, tokens):
    tok, width = tokens.shape
    hbm = pl.BlockSpec(memory_space=pl.ANY)
    return pl.pallas_call(
        prep_kernel,
        in_specs=[hbm, hbm, hbm],
        out_specs=[pl.BlockSpec(memory_space=pltpu.VMEM)] * 2,
        out_shape=[
            pltpu.VMEM((tok, width + EXTRA), jnp.bfloat16),
            pltpu.VMEM((2, 16, EXTRA), jnp.bfloat16),
        ],
        scratch_shapes=[
            pltpu.VMEM(ids.shape, ids.dtype),
            pltpu.VMEM(gw.shape, gw.dtype),
            pltpu.SemaphoreType.DMA((3,)),
        ],
        compiler_params=pltpu.CompilerParams(vmem_limit_bytes=4 * 1024 * 1024),
        cost_estimate=pl.CostEstimate(flops=2 * EXPERTS * tok**2, bytes_accessed=4 * tok * width, transcendentals=0),
        name="prep",
    )(*[pltpu.with_memory_space_constraint(v, pltpu.HBM) for v in (ids, gw, tokens)])


def select(q, blocks):
    width = blocks[0].shape[1] - EXTRA
    return jnp.concatenate(
        [
            lax.dot_general(q, b[:, width:], (((1,), (1,)), ((), ())), preferred_element_type=jnp.float32)
            for b in blocks
        ],
        axis=1,
    )


def pack_kernel(which, q_ref, *refs):
    outs = refs[len(refs) - len(which) :]
    blocks = [refs[n] for n in (0, 3, 2, 1)]
    tok = blocks[0].shape[0]
    width = outs[0].shape[1]
    q = q_ref[0]
    half = 2 * CAP
    r = lax.broadcasted_iota(jnp.int32, (half, 2 * tok), 0)
    t = lax.broadcasted_iota(jnp.int32, (half, 2 * tok), 1)
    second = r >= CAP
    target = jnp.where(second, r - CAP, r)
    target = jnp.where(second == (t >= tok), target, -5).astype(jnp.float32)
    cols = 512
    for p in range(len(blocks) // 2):
        pair = blocks[2 * p : 2 * p + 2]
        slots = select(q, pair)
        pick = jnp.concatenate(
            [
                jnp.where(slots[NC * k + f : NC * k + f + 1, :] == target, 1.0, 0.0).astype(jnp.bfloat16)
                for k in which
                for f in range(NC)
            ],
            axis=0,
        )
        for at in range(0, width, cols):
            block = jnp.concatenate([b[:, at : at + cols] for b in pair], axis=0)
            got = jnp.dot(pick, block, preferred_element_type=jnp.float32).astype(jnp.bfloat16)
            for n, o in enumerate(outs):
                o[2 * half * p : 2 * half * (p + 1), at : at + cols] = got[2 * half * n : 2 * half * (n + 1), :]


def pack(which, q, blocks):
    tok = blocks[0].shape[0]
    width = blocks[0].shape[1] - EXTRA
    count = len(which)
    rows = NC * len(blocks) * CAP
    vmem = pl.BlockSpec(memory_space=pltpu.VMEM)
    return pl.pallas_call(
        functools.partial(pack_kernel, which),
        in_specs=[vmem] * (1 + len(blocks)),
        out_specs=[vmem] * count,
        out_shape=[jax.ShapeDtypeStruct((rows, width), jnp.bfloat16)] * count,
        compiler_params=pltpu.CompilerParams(vmem_limit_bytes=16 * 1024 * 1024),
        cost_estimate=pl.CostEstimate(
            flops=2 * rows * count * 2 * tok * width,
            bytes_accessed=2 * (len(blocks) * tok + rows * count) * width,
            transcendentals=0,
        ),
        name="pack",
    )(q, *[blocks[n] for n in (0, 3, 2, 1)])


def combine_kernel(which, q_ref, *refs):
    count = len(which)
    blocks, backs, sums, outs = refs[:4], refs[4 : 4 + count], refs[4 + count : -4], refs[-4:]
    blocks = [blocks[n] for n in (0, 3, 2, 1)]
    tok, width = outs[0].shape
    half = 2 * CAP
    places = [NC * k + f for k in which for f in range(NC)]
    span = half * len(places)
    lane = lax.broadcasted_iota(jnp.int32, (2 * tok, span), 1)
    part = jnp.zeros((2 * tok, span), jnp.int32)
    er = lax.broadcasted_iota(jnp.int32, (16, span), 0)
    el = lax.broadcasted_iota(jnp.int32, (16, span), 1)
    ep = jnp.full((16, span), places[0], jnp.int32)
    for n in range(1, len(places)):
        part = jnp.where(lane >= half * n, half * n, part)
        ep = jnp.where(el >= half * n, places[n], ep)
    r = lane - part
    t = lax.broadcasted_iota(jnp.int32, (2 * tok, span), 0)
    second = r >= CAP
    target = jnp.where(second, r - CAP, r)
    target = jnp.where(second == (t >= tok), target, -5).astype(jnp.float32)
    expand = jnp.where(er == ep, 1.0, 0.0).astype(jnp.bfloat16)

    def widen(v):
        return lax.dot_general(
            v.astype(jnp.bfloat16), expand, (((0,), (0,)), ((), ())), preferred_element_type=jnp.float32
        )

    cols = 512
    for p in range(2):
        pair = blocks[2 * p : 2 * p + 2]
        mix = jnp.where(widen(select(q_ref[0], pair)) == target, widen(select(q_ref[1], pair)), 0.0)
        mix = mix.astype(jnp.bfloat16)
        for at in range(0, width, cols):
            rows = jnp.concatenate([b[2 * half * p : 2 * half * (p + 1), at : at + cols] for b in backs], axis=0)
            got = jnp.dot(mix, rows, preferred_element_type=jnp.float32)
            for n in range(2):
                new = got[n * tok : (n + 1) * tok]
                if sums:
                    new = new + sums[2 * p + n][:, at : at + cols]
                outs[2 * p + n][:, at : at + cols] = new.astype(outs[2 * p + n].dtype)


def combine(which, q, blocks, backs, sums, dtypes):
    tok = blocks[0].shape[0]
    rows, width = backs[0].shape
    vmem = pl.BlockSpec(memory_space=pltpu.VMEM)
    return pl.pallas_call(
        functools.partial(combine_kernel, which),
        in_specs=[vmem] * (5 + len(backs) + len(sums)),
        out_specs=[vmem] * 4,
        out_shape=[jax.ShapeDtypeStruct((tok, width), d) for d in dtypes],
        compiler_params=pltpu.CompilerParams(vmem_limit_bytes=16 * 1024 * 1024),
        cost_estimate=pl.CostEstimate(
            flops=2 * len(which) * rows * 2 * tok * width,
            bytes_accessed=2 * (6 * tok + len(which) * rows) * width,
            transcendentals=0,
        ),
        name="combine",
    )(q, *[blocks[n] for n in (0, 3, 2, 1)], *backs, *sums)


def finish_kernel(q_ref, *refs):
    pair, back_ref, sums, outs = refs[:2], refs[2], refs[3:5], refs[5:]
    tok, width = outs[0].shape
    half = 2 * CAP
    span = half * NC
    lane = lax.broadcasted_iota(jnp.int32, (2 * tok, span), 1)
    er = lax.broadcasted_iota(jnp.int32, (16, span), 0)
    el = lax.broadcasted_iota(jnp.int32, (16, span), 1)
    r = jnp.where(lane >= half, lane - half, lane)
    t = lax.broadcasted_iota(jnp.int32, (2 * tok, span), 0)
    second = r >= CAP
    target = jnp.where(second, r - CAP, r)
    target = jnp.where(second == (t >= tok), target, -5).astype(jnp.float32)
    expand = jnp.where(er == jnp.where(el >= half, 2 * NC + 1, 2 * NC), 1.0, 0.0).astype(jnp.bfloat16)

    def widen(v):
        return lax.dot_general(
            v.astype(jnp.bfloat16), expand, (((0,), (0,)), ((), ())), preferred_element_type=jnp.float32
        )

    mix = jnp.where(widen(select(q_ref[0], pair)) == target, widen(select(q_ref[1], pair)), 0.0)
    mix = mix.astype(jnp.bfloat16)
    cols = 512
    for at in range(0, width, cols):
        got = jnp.dot(mix, back_ref[:, at : at + cols], preferred_element_type=jnp.float32)
        for n in range(2):
            new = got[n * tok : (n + 1) * tok] + sums[n][:, at : at + cols]
            outs[n][:, at : at + cols] = new.astype(outs[n].dtype)


def finish(q, pair, slab, sums, dtypes):
    tok = pair[0].shape[0]
    rows, width = slab.shape
    vmem = pl.BlockSpec(memory_space=pltpu.VMEM)
    return pl.pallas_call(
        finish_kernel,
        in_specs=[vmem] * 6,
        out_specs=[vmem] * 2,
        out_shape=[jax.ShapeDtypeStruct((tok, width), d) for d in dtypes],
        compiler_params=pltpu.CompilerParams(vmem_limit_bytes=16 * 1024 * 1024),
        cost_estimate=pl.CostEstimate(
            flops=2 * rows * 2 * tok * width,
            bytes_accessed=2 * (6 * tok + rows) * width,
            transcendentals=0,
        ),
        name="finish",
    )(q, *pair, slab, *sums)


def halves(refs):
    size = 2 * NC * CAP
    return [(ref, at) for ref in refs for at in range(0, ref.shape[0], size)]


def expert_kernel(count, ff, *refs):
    slabs, bundles, outs = refs[:count], refs[count : count + 2], refs[count + 2 :]
    width = slabs[0].shape[1]
    half = 2 * CAP
    for f, w in enumerate(bundles):
        lines = jnp.concatenate([s[at + half * f : at + half * (f + 1), :] for s, at in halves(slabs)], axis=0)
        hidden = []
        for at in range(0, ff, 256):
            gate = jnp.dot(lines, w[:width, at : at + 256], preferred_element_type=jnp.float32)
            up = jnp.dot(lines, w[:width, ff + at : ff + at + 256], preferred_element_type=jnp.float32)
            hidden.append((gate / (1.0 + jnp.exp(-gate)) * up).astype(jnp.bfloat16))
        whole = jnp.concatenate(hidden, axis=1)
        for at in range(0, width, 512):
            if at < 2 * ff:
                down = w[width : width + ff, at : at + 512]
            else:
                down = jnp.concatenate([w[width + ff :, 512 * i : 512 * (i + 1)] for i in range(ff // 256)], axis=0)
            got = jnp.dot(whole, down, preferred_element_type=jnp.float32)
            got = got.astype(jnp.bfloat16)
            for n, (o, to) in enumerate(halves(outs)):
                o[to + half * f : to + half * (f + 1), at : at + 512] = got[n * half : (n + 1) * half]


def expert(slabs, bundles, outs):
    count = len(slabs)
    rows = sum(s.shape[0] for s in slabs)
    width = slabs[0].shape[1]
    ff = bundles[0].shape[1] // 2
    vmem = pl.BlockSpec(memory_space=pltpu.VMEM)
    return pl.pallas_call(
        functools.partial(expert_kernel, count, ff),
        in_specs=[vmem] * (count + 2),
        out_specs=[vmem] * outs,
        out_shape=[jax.ShapeDtypeStruct((rows // outs, width), jnp.bfloat16)] * outs,
        compiler_params=pltpu.CompilerParams(vmem_limit_bytes=16 * 1024 * 1024),
        cost_estimate=pl.CostEstimate(
            flops=6 * rows * width * ff,
            bytes_accessed=4 * rows * width,
            transcendentals=rows * ff,
        ),
        name="expert",
    )(*slabs, *[pltpu.with_memory_space_constraint(w, pltpu.VMEM) for w in bundles])


def hold_kernel(wg, wu, wd, out_ref, mark_ref, sems):
    width, ff = wg.shape[1:]
    moves = [
        (wg.at[0], out_ref.at[pl.ds(0, width), pl.ds(0, ff)]),
        (wu.at[0], out_ref.at[pl.ds(0, width), pl.ds(ff, ff)]),
        (wd.at[0, :, pl.ds(0, 2 * ff)], out_ref.at[pl.ds(width, ff)]),
    ]
    for i in range(ff // 256):
        moves.append(
            (
                wd.at[0, pl.ds(256 * i, 256), pl.ds(2 * ff, 512)],
                out_ref.at[pl.ds(width + ff, 256), pl.ds(512 * i, 512)],
            )
        )
    copies = [pltpu.make_async_copy(a, b, sems.at[n]) for n, (a, b) in enumerate(moves)]
    for copy in copies:
        copy.start()
    mark_ref[...] = jnp.zeros_like(mark_ref)
    for copy in copies:
        copy.wait()


def hold(*weights):
    width, ff = weights[0].shape[1:]
    return pl.pallas_call(
        hold_kernel,
        in_specs=[pl.BlockSpec(memory_space=pl.ANY)] * 3,
        out_specs=[pl.BlockSpec(memory_space=pltpu.VMEM)] * 2,
        out_shape=[
            pltpu.VMEM((width + ff + 256, 2 * ff), weights[0].dtype),
            pltpu.VMEM((8, 128), jnp.float32),
        ],
        scratch_shapes=[pltpu.SemaphoreType.DMA((6,))],
        compiler_params=pltpu.CompilerParams(vmem_limit_bytes=4 * 1024 * 1024),
        cost_estimate=pl.CostEstimate(flops=0, bytes_accessed=4 * weights[0].size * 3, transcendentals=0),
        name="hold",
    )(*[pltpu.with_memory_space_constraint(w, pltpu.HBM) for w in weights])[0]


def per_device(tokens, expert_ids, gate_weights, w_gate, w_up, w_down):
    send = lambda v, pairs: lax.ppermute(v, "expert", pairs)
    after = lambda v, other: lax.optimization_barrier((v, other))[0]
    home, q = prep(expert_ids.T, gate_weights.T, tokens)
    moved = {j: send(home, spread_pairs(j)) for j in (1, 3, 2)}
    pairs = [[home, moved[2]], [moved[1], moved[3]]]
    bundle = hold(w_gate, w_up, w_down)

    near = pack((1, 3), q, pairs[0] + pairs[1])
    weights = [bundle, send(after(bundle, near[0]), swap_pairs())]
    arrived = {k: send(slab, deliver_pairs(k)) for k, slab in zip((1, 3), near)}
    stay, far = pack((0, 2), q, pairs[0] + pairs[1])
    backs = {}
    (backs[0],) = expert([stay], weights, 1)
    arrived[2] = send(after(far, arrived[3]), deliver_pairs(2))
    for k, slab in zip((1, 3), expert([arrived[1], arrived[3]], weights, 2)):
        backs[k] = send(slab, back(deliver_pairs(k)))
    halves2 = expert([arrived[2]], weights, 2)
    early = send(halves2[0], back(deliver_pairs(2)))
    late = send(after(halves2[1], (backs[1], backs[3])), back(deliver_pairs(2)))

    f32, bf16 = jnp.float32, jnp.bfloat16
    sums = combine((0, 1, 3), q, pairs[0] + pairs[1], [backs[k] for k in (0, 1, 3)], [], [f32] * 4)
    parts = {}
    for p, slab in ((0, early), (1, late)):
        kinds = (f32, bf16) if p == 0 else (bf16, bf16)
        parts[p] = finish(q, pairs[p], slab, sums[2 * p : 2 * p + 2], kinds)
    part0, part2 = parts[0]
    part1, part3 = parts[1]
    mixed = part0 + send(part2, back(spread_pairs(2))).astype(f32)
    mixed = lax.optimization_barrier(mixed)
    for j, part in ((1, part1), (3, part3)):
        mixed = mixed + send(part, back(spread_pairs(j))).astype(f32)
    return mixed.astype(bf16)


def solution(mesh):
    return jax.shard_map(
        per_device,
        mesh=mesh,
        in_specs=(
            P(("dp", "expert"), None),
            P(("dp", "expert"), None),
            P(("dp", "expert"), None),
            P("expert", None, None),
            P("expert", None, None),
            P("expert", None, None),
        ),
        out_specs=P(("dp", "expert"), None),
        check_vma=False,
    )
```

```python
import functools

import jax
import jax.numpy as jnp
from jax import lax
from jax.experimental import pallas as pl
from jax.experimental.pallas import tpu as pltpu
from jax.sharding import PartitionSpec as P

NX, NY, NC = 4, 4, 2
EXPERTS = NX * NY * NC
CAP = 40
EXTRA = 128
KF = 8


def index_of(x, y, c):
    return ((x % NX) * NY + (y % NY)) * NC + c


def spread_pairs(j):
    pairs = []
    for x in range(NX):
        for y in range(NY):
            pairs.append((index_of(x, y, 0), index_of(x + j, y, 0)))
            pairs.append((index_of(x, y, 1), index_of(x, y + j, 1)))
    return pairs


def deliver_pairs(k):
    pairs = []
    for x in range(NX):
        for y in range(NY):
            pairs.append((index_of(x, y, 0), index_of(x, y + k, 0)))
            pairs.append((index_of(x, y, 1), index_of(x + k, y, 1)))
    return pairs


def swap_pairs():
    return [(i, i ^ 1) for i in range(EXPERTS)]


def back(pairs):
    return [(b, a) for a, b in pairs]


def prep_kernel(ids_hbm, gw_hbm, tok_hbm, out_ref, q_ref, ids_ref, gw_ref, sems):
    top, tok = ids_ref.shape
    width = tok_hbm.shape[1]
    copies = [
        pltpu.make_async_copy(ids_hbm, ids_ref, sems.at[0]),
        pltpu.make_async_copy(gw_hbm, gw_ref, sems.at[1]),
        pltpu.make_async_copy(tok_hbm, out_ref.at[:, pl.ds(0, width)], sems.at[2]),
    ]
    for copy in copies:
        copy.start()
    row = lax.broadcasted_iota(jnp.int32, (tok, tok), 0)
    col = lax.broadcasted_iota(jnp.int32, (tok, tok), 1)
    earlier = jnp.where(row < col, 1.0, 0.0).astype(jnp.bfloat16)
    name = lax.broadcasted_iota(jnp.int32, (EXPERTS, tok), 0)
    chosen = jnp.zeros((EXPERTS, tok), jnp.float32)
    weight = jnp.zeros((EXPERTS, tok), jnp.float32)
    copies[0].wait()
    copies[1].wait()
    ids = ids_ref[...]
    gw = gw_ref[...]
    for k in range(top):
        hit = ids[k : k + 1, :] == name
        chosen = jnp.where(hit, 1.0, chosen)
        weight = jnp.where(hit, gw[k : k + 1, :], weight)
    count = jnp.dot(chosen.astype(jnp.bfloat16), earlier, preferred_element_type=jnp.float32)
    slot = jnp.where(chosen > 0.5, count, -1.0)
    blank = jnp.zeros((EXTRA - 2 * EXPERTS, tok), jnp.float32)
    table = jnp.concatenate([slot, weight, blank], axis=0)
    out_ref[:, width:] = table.T.astype(jnp.bfloat16)
    me = lax.axis_index("expert")
    x, y, c = me >> 3, (me >> 1) & 3, me & 1
    n = lax.broadcasted_iota(jnp.int32, (16, EXTRA), 0)
    spot = lax.broadcasted_iota(jnp.int32, (16, EXTRA), 1)
    k, f = n >> 1, n & 1
    along_y = x * (NY * NC) + ((y + k) & 3) * NC + ((c + f) & 1)
    along_x = ((x + k) & 3) * (NY * NC) + y * NC + ((c + f) & 1)
    mine = jnp.where(n < KF, jnp.where(c == 0, along_y, along_x), -EXTRA)
    q_ref[0] = jnp.where(mine == spot, 1.0, 0.0).astype(jnp.bfloat16)
    q_ref[1] = jnp.where(mine + EXPERTS == spot, 1.0, 0.0).astype(jnp.bfloat16)
    copies[2].wait()


def prep(ids, gw, tokens):
    tok, width = tokens.shape
    hbm = pl.BlockSpec(memory_space=pl.ANY)
    return pl.pallas_call(
        prep_kernel,
        in_specs=[hbm, hbm, hbm],
        out_specs=[pl.BlockSpec(memory_space=pltpu.VMEM)] * 2,
        out_shape=[
            pltpu.VMEM((tok, width + EXTRA), jnp.bfloat16),
            pltpu.VMEM((2, 16, EXTRA), jnp.bfloat16),
        ],
        scratch_shapes=[
            pltpu.VMEM(ids.shape, ids.dtype),
            pltpu.VMEM(gw.shape, gw.dtype),
            pltpu.SemaphoreType.DMA((3,)),
        ],
        compiler_params=pltpu.CompilerParams(vmem_limit_bytes=4 * 1024 * 1024),
        cost_estimate=pl.CostEstimate(flops=2 * EXPERTS * tok**2, bytes_accessed=4 * tok * width, transcendentals=0),
        name="prep",
    )(*[pltpu.with_memory_space_constraint(v, pltpu.HBM) for v in (ids, gw, tokens)])


def select(q, blocks):
    width = blocks[0].shape[1] - EXTRA
    return jnp.concatenate(
        [
            lax.dot_general(q, b[:, width:], (((1,), (1,)), ((), ())), preferred_element_type=jnp.float32)
            for b in blocks
        ],
        axis=1,
    )


def pack_kernel(which, q_ref, *refs):
    outs = refs[len(refs) - len(which) :]
    blocks = [refs[n] for n in (0, 3, 2, 1)]
    tok = blocks[0].shape[0]
    width = outs[0].shape[1]
    q = q_ref[0]
    half = 2 * CAP
    r = lax.broadcasted_iota(jnp.int32, (half, 2 * tok), 0)
    t = lax.broadcasted_iota(jnp.int32, (half, 2 * tok), 1)
    second = r >= CAP
    target = jnp.where(second, r - CAP, r)
    target = jnp.where(second == (t >= tok), target, -5).astype(jnp.float32)
    cols = 512
    for p in range(len(blocks) // 2):
        pair = blocks[2 * p : 2 * p + 2]
        slots = select(q, pair)
        pick = jnp.concatenate(
            [
                jnp.where(slots[NC * k + f : NC * k + f + 1, :] == target, 1.0, 0.0).astype(jnp.bfloat16)
                for k in which
                for f in range(NC)
            ],
            axis=0,
        )
        for at in range(0, width, cols):
            block = jnp.concatenate([b[:, at : at + cols] for b in pair], axis=0)
            got = jnp.dot(pick, block, preferred_element_type=jnp.float32).astype(jnp.bfloat16)
            for n, o in enumerate(outs):
                o[2 * half * p : 2 * half * (p + 1), at : at + cols] = got[2 * half * n : 2 * half * (n + 1), :]


def pack(which, q, blocks):
    tok = blocks[0].shape[0]
    width = blocks[0].shape[1] - EXTRA
    count = len(which)
    rows = NC * len(blocks) * CAP
    vmem = pl.BlockSpec(memory_space=pltpu.VMEM)
    return pl.pallas_call(
        functools.partial(pack_kernel, which),
        in_specs=[vmem] * (1 + len(blocks)),
        out_specs=[vmem] * count,
        out_shape=[jax.ShapeDtypeStruct((rows, width), jnp.bfloat16)] * count,
        compiler_params=pltpu.CompilerParams(vmem_limit_bytes=16 * 1024 * 1024),
        cost_estimate=pl.CostEstimate(
            flops=2 * rows * count * 2 * tok * width,
            bytes_accessed=2 * (len(blocks) * tok + rows * count) * width,
            transcendentals=0,
        ),
        name="pack",
    )(q, *[blocks[n] for n in (0, 3, 2, 1)])


def combine_kernel(which, q_ref, *refs):
    count = len(which)
    blocks, backs, sums, outs = refs[:4], refs[4 : 4 + count], refs[4 + count : -4], refs[-4:]
    blocks = [blocks[n] for n in (0, 3, 2, 1)]
    tok, width = outs[0].shape
    half = 2 * CAP
    places = [NC * k + f for k in which for f in range(NC)]
    span = half * len(places)
    lane = lax.broadcasted_iota(jnp.int32, (2 * tok, span), 1)
    part = jnp.zeros((2 * tok, span), jnp.int32)
    er = lax.broadcasted_iota(jnp.int32, (16, span), 0)
    el = lax.broadcasted_iota(jnp.int32, (16, span), 1)
    ep = jnp.full((16, span), places[0], jnp.int32)
    for n in range(1, len(places)):
        part = jnp.where(lane >= half * n, half * n, part)
        ep = jnp.where(el >= half * n, places[n], ep)
    r = lane - part
    t = lax.broadcasted_iota(jnp.int32, (2 * tok, span), 0)
    second = r >= CAP
    target = jnp.where(second, r - CAP, r)
    target = jnp.where(second == (t >= tok), target, -5).astype(jnp.float32)
    expand = jnp.where(er == ep, 1.0, 0.0).astype(jnp.bfloat16)

    def widen(v):
        return lax.dot_general(
            v.astype(jnp.bfloat16), expand, (((0,), (0,)), ((), ())), preferred_element_type=jnp.float32
        )

    cols = 512
    for p in range(2):
        pair = blocks[2 * p : 2 * p + 2]
        mix = jnp.where(widen(select(q_ref[0], pair)) == target, widen(select(q_ref[1], pair)), 0.0)
        mix = mix.astype(jnp.bfloat16)
        for at in range(0, width, cols):
            rows = jnp.concatenate([b[2 * half * p : 2 * half * (p + 1), at : at + cols] for b in backs], axis=0)
            got = jnp.dot(mix, rows, preferred_element_type=jnp.float32)
            for n in range(2):
                new = got[n * tok : (n + 1) * tok]
                if sums:
                    new = new + sums[2 * p + n][:, at : at + cols]
                outs[2 * p + n][:, at : at + cols] = new.astype(outs[2 * p + n].dtype)


def combine(which, q, blocks, backs, sums, dtypes):
    tok = blocks[0].shape[0]
    rows, width = backs[0].shape
    vmem = pl.BlockSpec(memory_space=pltpu.VMEM)
    return pl.pallas_call(
        functools.partial(combine_kernel, which),
        in_specs=[vmem] * (5 + len(backs) + len(sums)),
        out_specs=[vmem] * 4,
        out_shape=[jax.ShapeDtypeStruct((tok, width), d) for d in dtypes],
        compiler_params=pltpu.CompilerParams(vmem_limit_bytes=16 * 1024 * 1024),
        cost_estimate=pl.CostEstimate(
            flops=2 * len(which) * rows * 2 * tok * width,
            bytes_accessed=2 * (6 * tok + len(which) * rows) * width,
            transcendentals=0,
        ),
        name="combine",
    )(q, *[blocks[n] for n in (0, 3, 2, 1)], *backs, *sums)


def finish_kernel(back_ref, *refs):
    sums, q_ref, pair, outs = refs[:2], refs[2], refs[3:5], refs[5:]
    tok, width = outs[0].shape
    half = 2 * CAP
    span = half * NC
    lane = lax.broadcasted_iota(jnp.int32, (2 * tok, span), 1)
    er = lax.broadcasted_iota(jnp.int32, (16, span), 0)
    el = lax.broadcasted_iota(jnp.int32, (16, span), 1)
    r = jnp.where(lane >= half, lane - half, lane)
    t = lax.broadcasted_iota(jnp.int32, (2 * tok, span), 0)
    second = r >= CAP
    target = jnp.where(second, r - CAP, r)
    target = jnp.where(second == (t >= tok), target, -5).astype(jnp.float32)
    expand = jnp.where(er == jnp.where(el >= half, 2 * NC + 1, 2 * NC), 1.0, 0.0).astype(jnp.bfloat16)

    def widen(v):
        return lax.dot_general(
            v.astype(jnp.bfloat16), expand, (((0,), (0,)), ((), ())), preferred_element_type=jnp.float32
        )

    mix = jnp.where(widen(select(q_ref[0], pair)) == target, widen(select(q_ref[1], pair)), 0.0)
    mix = mix.astype(jnp.bfloat16)
    cols = 512
    for at in range(0, width, cols):
        got = jnp.dot(mix, back_ref[:, at : at + cols], preferred_element_type=jnp.float32)
        for n in range(2):
            new = got[n * tok : (n + 1) * tok] + sums[n][:, at : at + cols]
            outs[n][:, at : at + cols] = new.astype(outs[n].dtype)


def finish(q, pair, slab, sums, dtypes):
    tok = pair[0].shape[0]
    rows, width = slab.shape
    vmem = pl.BlockSpec(memory_space=pltpu.VMEM)
    return pl.pallas_call(
        finish_kernel,
        in_specs=[vmem] * 6,
        out_specs=[vmem] * 2,
        out_shape=[jax.ShapeDtypeStruct((tok, width), d) for d in dtypes],
        compiler_params=pltpu.CompilerParams(vmem_limit_bytes=16 * 1024 * 1024),
        cost_estimate=pl.CostEstimate(
            flops=2 * rows * 2 * tok * width,
            bytes_accessed=2 * (6 * tok + rows) * width,
            transcendentals=0,
        ),
        name="finish",
    )(slab, *sums, q, *pair)


def halves(refs):
    size = 2 * NC * CAP
    return [(ref, at) for ref in refs for at in range(0, ref.shape[0], size)]


def expert_kernel(count, ff, *refs):
    slabs, bundles, outs = refs[:count], refs[count : count + 2], refs[count + 2 :]
    width = slabs[0].shape[1]
    half = 2 * CAP
    for f, w in enumerate(bundles):
        lines = jnp.concatenate([s[at + half * f : at + half * (f + 1), :] for s, at in halves(slabs)], axis=0)
        hidden = []
        for at in range(0, ff, 256):
            gate = jnp.dot(lines, w[:width, at : at + 256], preferred_element_type=jnp.float32)
            up = jnp.dot(lines, w[:width, ff + at : ff + at + 256], preferred_element_type=jnp.float32)
            hidden.append((gate / (1.0 + jnp.exp(-gate)) * up).astype(jnp.bfloat16))
        whole = jnp.concatenate(hidden, axis=1)
        for at in range(0, width, 512):
            if at < 2 * ff:
                down = w[width : width + ff, at : at + 512]
            else:
                down = jnp.concatenate([w[width + ff :, 512 * i : 512 * (i + 1)] for i in range(ff // 256)], axis=0)
            got = jnp.dot(whole, down, preferred_element_type=jnp.float32)
            got = got.astype(jnp.bfloat16)
            for n, (o, to) in enumerate(halves(outs)):
                o[to + half * f : to + half * (f + 1), at : at + 512] = got[n * half : (n + 1) * half]


def expert(slabs, bundles, outs):
    count = len(slabs)
    rows = sum(s.shape[0] for s in slabs)
    width = slabs[0].shape[1]
    ff = bundles[0].shape[1] // 2
    vmem = pl.BlockSpec(memory_space=pltpu.VMEM)
    return pl.pallas_call(
        functools.partial(expert_kernel, count, ff),
        in_specs=[vmem] * (count + 2),
        out_specs=[vmem] * outs,
        out_shape=[jax.ShapeDtypeStruct((rows // outs, width), jnp.bfloat16)] * outs,
        compiler_params=pltpu.CompilerParams(vmem_limit_bytes=16 * 1024 * 1024),
        cost_estimate=pl.CostEstimate(
            flops=6 * rows * width * ff,
            bytes_accessed=4 * rows * width,
            transcendentals=rows * ff,
        ),
        name="expert",
    )(*slabs, *[pltpu.with_memory_space_constraint(w, pltpu.VMEM) for w in bundles])


def hold_kernel(wg, wu, wd, out_ref, mark_ref, sems):
    width, ff = wg.shape[1:]
    moves = [
        (wg.at[0], out_ref.at[pl.ds(0, width), pl.ds(0, ff)]),
        (wu.at[0], out_ref.at[pl.ds(0, width), pl.ds(ff, ff)]),
        (wd.at[0, :, pl.ds(0, 2 * ff)], out_ref.at[pl.ds(width, ff)]),
    ]
    for i in range(ff // 256):
        moves.append(
            (
                wd.at[0, pl.ds(256 * i, 256), pl.ds(2 * ff, 512)],
                out_ref.at[pl.ds(width + ff, 256), pl.ds(512 * i, 512)],
            )
        )
    copies = [pltpu.make_async_copy(a, b, sems.at[n]) for n, (a, b) in enumerate(moves)]
    for copy in copies:
        copy.start()
    mark_ref[...] = jnp.zeros_like(mark_ref)
    for copy in copies:
        copy.wait()


def hold(*weights):
    width, ff = weights[0].shape[1:]
    return pl.pallas_call(
        hold_kernel,
        in_specs=[pl.BlockSpec(memory_space=pl.ANY)] * 3,
        out_specs=[pl.BlockSpec(memory_space=pltpu.VMEM)] * 2,
        out_shape=[
            pltpu.VMEM((width + ff + 256, 2 * ff), weights[0].dtype),
            pltpu.VMEM((8, 128), jnp.float32),
        ],
        scratch_shapes=[pltpu.SemaphoreType.DMA((6,))],
        compiler_params=pltpu.CompilerParams(vmem_limit_bytes=4 * 1024 * 1024),
        cost_estimate=pl.CostEstimate(flops=0, bytes_accessed=4 * weights[0].size * 3, transcendentals=0),
        name="hold",
    )(*[pltpu.with_memory_space_constraint(w, pltpu.HBM) for w in weights])[0]


def per_device(tokens, expert_ids, gate_weights, w_gate, w_up, w_down):
    send = lambda v, pairs: lax.ppermute(v, "expert", pairs)
    after = lambda v, other: lax.optimization_barrier((v, other))[0]
    home, q = prep(expert_ids.T, gate_weights.T, tokens)
    moved = {j: send(home, spread_pairs(j)) for j in (1, 3, 2)}
    pairs = [[home, moved[2]], [moved[1], moved[3]]]
    bundle = hold(w_gate, w_up, w_down)

    near = pack((1, 3), q, pairs[0] + pairs[1])
    weights = [bundle, send(after(bundle, near[0]), swap_pairs())]
    arrived = {k: send(slab, deliver_pairs(k)) for k, slab in zip((1, 3), near)}
    stay, far = pack((0, 2), q, pairs[0] + pairs[1])
    backs = {}
    (backs[0],) = expert([stay], weights, 1)
    arrived[2] = send(after(far, arrived[3]), deliver_pairs(2))
    for k, slab in zip((1, 3), expert([arrived[1], arrived[3]], weights, 2)):
        backs[k] = send(slab, back(deliver_pairs(k)))
    halves2 = expert([arrived[2]], weights, 2)
    early = send(halves2[0], back(deliver_pairs(2)))
    late = send(after(halves2[1], (backs[1], backs[3])), back(deliver_pairs(2)))

    f32, bf16 = jnp.float32, jnp.bfloat16
    sums = combine((0, 1, 3), q, pairs[0] + pairs[1], [backs[k] for k in (0, 1, 3)], [], [f32] * 4)
    parts = {}
    for p, slab in ((0, early), (1, late)):
        kinds = (f32, bf16) if p == 0 else (bf16, bf16)
        parts[p] = finish(q, pairs[p], slab, sums[2 * p : 2 * p + 2], kinds)
    part0, part2 = parts[0]
    part1, part3 = parts[1]
    mixed = part0 + send(after(part2, late), back(spread_pairs(2))).astype(f32)
    mixed = lax.optimization_barrier(mixed)
    for j, part in ((1, part1), (3, part3)):
        mixed = mixed + send(part, back(spread_pairs(j))).astype(f32)
    return mixed.astype(bf16)


def solution(mesh):
    return jax.shard_map(
        per_device,
        mesh=mesh,
        in_specs=(
            P(("dp", "expert"), None),
            P(("dp", "expert"), None),
            P(("dp", "expert"), None),
            P("expert", None, None),
            P("expert", None, None),
            P("expert", None, None),
        ),
        out_specs=P(("dp", "expert"), None),
        check_vma=False,
    )
```

```python
import functools

import jax
import jax.numpy as jnp
from jax import lax
from jax.experimental import pallas as pl
from jax.experimental.pallas import tpu as pltpu
from jax.sharding import PartitionSpec as P

NX, NY, NC = 4, 4, 2
EXPERTS = NX * NY * NC
CAP = 40
EXTRA = 128
KF = 8


def index_of(x, y, c):
    return ((x % NX) * NY + (y % NY)) * NC + c


def spread_pairs(j):
    pairs = []
    for x in range(NX):
        for y in range(NY):
            pairs.append((index_of(x, y, 0), index_of(x + j, y, 0)))
            pairs.append((index_of(x, y, 1), index_of(x, y + j, 1)))
    return pairs


def deliver_pairs(k):
    pairs = []
    for x in range(NX):
        for y in range(NY):
            pairs.append((index_of(x, y, 0), index_of(x, y + k, 0)))
            pairs.append((index_of(x, y, 1), index_of(x + k, y, 1)))
    return pairs


def swap_pairs():
    return [(i, i ^ 1) for i in range(EXPERTS)]


def back(pairs):
    return [(b, a) for a, b in pairs]


def prep_kernel(ids_hbm, gw_hbm, tok_hbm, out_ref, q_ref, ids_ref, gw_ref, sems):
    top, tok = ids_ref.shape
    width = tok_hbm.shape[1]
    copies = [
        pltpu.make_async_copy(ids_hbm, ids_ref, sems.at[0]),
        pltpu.make_async_copy(gw_hbm, gw_ref, sems.at[1]),
        pltpu.make_async_copy(tok_hbm, out_ref.at[:, pl.ds(0, width)], sems.at[2]),
    ]
    for copy in copies:
        copy.start()
    row = lax.broadcasted_iota(jnp.int32, (tok, tok), 0)
    col = lax.broadcasted_iota(jnp.int32, (tok, tok), 1)
    earlier = jnp.where(row < col, 1.0, 0.0).astype(jnp.bfloat16)
    name = lax.broadcasted_iota(jnp.int32, (EXPERTS, tok), 0)
    chosen = jnp.zeros((EXPERTS, tok), jnp.float32)
    weight = jnp.zeros((EXPERTS, tok), jnp.float32)
    copies[0].wait()
    copies[1].wait()
    ids = ids_ref[...]
    gw = gw_ref[...]
    for k in range(top):
        hit = ids[k : k + 1, :] == name
        chosen = jnp.where(hit, 1.0, chosen)
        weight = jnp.where(hit, gw[k : k + 1, :], weight)
    count = jnp.dot(chosen.astype(jnp.bfloat16), earlier, preferred_element_type=jnp.float32)
    slot = jnp.where(chosen > 0.5, count, -1.0)
    blank = jnp.zeros((EXTRA - 2 * EXPERTS, tok), jnp.float32)
    table = jnp.concatenate([slot, weight, blank], axis=0)
    out_ref[:, width:] = table.T.astype(jnp.bfloat16)
    me = lax.axis_index("expert")
    x, y, c = me >> 3, (me >> 1) & 3, me & 1
    n = lax.broadcasted_iota(jnp.int32, (16, EXTRA), 0)
    spot = lax.broadcasted_iota(jnp.int32, (16, EXTRA), 1)
    k, f = n >> 1, n & 1
    along_y = x * (NY * NC) + ((y + k) & 3) * NC + ((c + f) & 1)
    along_x = ((x + k) & 3) * (NY * NC) + y * NC + ((c + f) & 1)
    mine = jnp.where(n < KF, jnp.where(c == 0, along_y, along_x), -EXTRA)
    q_ref[0] = jnp.where(mine == spot, 1.0, 0.0).astype(jnp.bfloat16)
    q_ref[1] = jnp.where(mine + EXPERTS == spot, 1.0, 0.0).astype(jnp.bfloat16)
    copies[2].wait()


def prep(ids, gw, tokens):
    tok, width = tokens.shape
    hbm = pl.BlockSpec(memory_space=pl.ANY)
    return pl.pallas_call(
        prep_kernel,
        in_specs=[hbm, hbm, hbm],
        out_specs=[pl.BlockSpec(memory_space=pltpu.VMEM)] * 2,
        out_shape=[
            pltpu.VMEM((tok, width + EXTRA), jnp.bfloat16),
            pltpu.VMEM((2, 16, EXTRA), jnp.bfloat16),
        ],
        scratch_shapes=[
            pltpu.VMEM(ids.shape, ids.dtype),
            pltpu.VMEM(gw.shape, gw.dtype),
            pltpu.SemaphoreType.DMA((3,)),
        ],
        compiler_params=pltpu.CompilerParams(vmem_limit_bytes=4 * 1024 * 1024),
        cost_estimate=pl.CostEstimate(flops=2 * EXPERTS * tok**2, bytes_accessed=4 * tok * width, transcendentals=0),
        name="prep",
    )(*[pltpu.with_memory_space_constraint(v, pltpu.HBM) for v in (ids, gw, tokens)])


def select(q, blocks):
    width = blocks[0].shape[1] - EXTRA
    return jnp.concatenate(
        [
            lax.dot_general(q, b[:, width:], (((1,), (1,)), ((), ())), preferred_element_type=jnp.float32)
            for b in blocks
        ],
        axis=1,
    )


def pack_kernel(which, q_ref, *refs):
    outs = refs[len(refs) - len(which) :]
    blocks = [refs[n] for n in (0, 3, 2, 1)]
    tok = blocks[0].shape[0]
    width = outs[0].shape[1]
    q = q_ref[0]
    half = 2 * CAP
    r = lax.broadcasted_iota(jnp.int32, (half, 2 * tok), 0)
    t = lax.broadcasted_iota(jnp.int32, (half, 2 * tok), 1)
    second = r >= CAP
    target = jnp.where(second, r - CAP, r)
    target = jnp.where(second == (t >= tok), target, -5).astype(jnp.float32)
    cols = 512
    for p in range(len(blocks) // 2):
        pair = blocks[2 * p : 2 * p + 2]
        slots = select(q, pair)
        pick = jnp.concatenate(
            [
                jnp.where(slots[NC * k + f : NC * k + f + 1, :] == target, 1.0, 0.0).astype(jnp.bfloat16)
                for k in which
                for f in range(NC)
            ],
            axis=0,
        )
        for at in range(0, width, cols):
            block = jnp.concatenate([b[:, at : at + cols] for b in pair], axis=0)
            got = jnp.dot(pick, block, preferred_element_type=jnp.float32).astype(jnp.bfloat16)
            for n, o in enumerate(outs):
                o[2 * half * p : 2 * half * (p + 1), at : at + cols] = got[2 * half * n : 2 * half * (n + 1), :]


def pack(which, q, blocks):
    tok = blocks[0].shape[0]
    width = blocks[0].shape[1] - EXTRA
    count = len(which)
    rows = NC * len(blocks) * CAP
    vmem = pl.BlockSpec(memory_space=pltpu.VMEM)
    return pl.pallas_call(
        functools.partial(pack_kernel, which),
        in_specs=[vmem] * (1 + len(blocks)),
        out_specs=[vmem] * count,
        out_shape=[jax.ShapeDtypeStruct((rows, width), jnp.bfloat16)] * count,
        compiler_params=pltpu.CompilerParams(vmem_limit_bytes=16 * 1024 * 1024),
        cost_estimate=pl.CostEstimate(
            flops=2 * rows * count * 2 * tok * width,
            bytes_accessed=2 * (len(blocks) * tok + rows * count) * width,
            transcendentals=0,
        ),
        name="pack",
    )(q, *[blocks[n] for n in (0, 3, 2, 1)])


def combine_kernel(which, q_ref, *refs):
    count = len(which)
    blocks, backs, sums, outs = refs[:4], refs[4 : 4 + count], refs[4 + count : -4], refs[-4:]
    blocks = [blocks[n] for n in (0, 3, 2, 1)]
    tok, width = outs[0].shape
    half = 2 * CAP
    places = [NC * k + f for k in which for f in range(NC)]
    span = half * len(places)
    lane = lax.broadcasted_iota(jnp.int32, (2 * tok, span), 1)
    part = jnp.zeros((2 * tok, span), jnp.int32)
    er = lax.broadcasted_iota(jnp.int32, (16, span), 0)
    el = lax.broadcasted_iota(jnp.int32, (16, span), 1)
    ep = jnp.full((16, span), places[0], jnp.int32)
    for n in range(1, len(places)):
        part = jnp.where(lane >= half * n, half * n, part)
        ep = jnp.where(el >= half * n, places[n], ep)
    r = lane - part
    t = lax.broadcasted_iota(jnp.int32, (2 * tok, span), 0)
    second = r >= CAP
    target = jnp.where(second, r - CAP, r)
    target = jnp.where(second == (t >= tok), target, -5).astype(jnp.float32)
    expand = jnp.where(er == ep, 1.0, 0.0).astype(jnp.bfloat16)

    def widen(v):
        return lax.dot_general(
            v.astype(jnp.bfloat16), expand, (((0,), (0,)), ((), ())), preferred_element_type=jnp.float32
        )

    cols = 512
    for p in range(2):
        pair = blocks[2 * p : 2 * p + 2]
        mix = jnp.where(widen(select(q_ref[0], pair)) == target, widen(select(q_ref[1], pair)), 0.0)
        mix = mix.astype(jnp.bfloat16)
        for at in range(0, width, cols):
            rows = jnp.concatenate([b[2 * half * p : 2 * half * (p + 1), at : at + cols] for b in backs], axis=0)
            got = jnp.dot(mix, rows, preferred_element_type=jnp.float32)
            for n in range(2):
                new = got[n * tok : (n + 1) * tok]
                if sums:
                    new = new + sums[2 * p + n][:, at : at + cols]
                outs[2 * p + n][:, at : at + cols] = new.astype(outs[2 * p + n].dtype)


def combine(which, q, blocks, backs, sums, dtypes):
    tok = blocks[0].shape[0]
    rows, width = backs[0].shape
    vmem = pl.BlockSpec(memory_space=pltpu.VMEM)
    return pl.pallas_call(
        functools.partial(combine_kernel, which),
        in_specs=[vmem] * (5 + len(backs) + len(sums)),
        out_specs=[vmem] * 4,
        out_shape=[jax.ShapeDtypeStruct((tok, width), d) for d in dtypes],
        compiler_params=pltpu.CompilerParams(vmem_limit_bytes=16 * 1024 * 1024),
        cost_estimate=pl.CostEstimate(
            flops=2 * len(which) * rows * 2 * tok * width,
            bytes_accessed=2 * (6 * tok + len(which) * rows) * width,
            transcendentals=0,
        ),
        name="combine",
    )(q, *[blocks[n] for n in (0, 3, 2, 1)], *backs, *sums)


def finish_kernel(back_ref, *refs):
    sums, q_ref, pair, outs = refs[:2], refs[2], refs[3:5], refs[5:]
    tok, width = outs[0].shape
    half = 2 * CAP
    span = half * NC
    lane = lax.broadcasted_iota(jnp.int32, (2 * tok, span), 1)
    er = lax.broadcasted_iota(jnp.int32, (16, span), 0)
    el = lax.broadcasted_iota(jnp.int32, (16, span), 1)
    r = jnp.where(lane >= half, lane - half, lane)
    t = lax.broadcasted_iota(jnp.int32, (2 * tok, span), 0)
    second = r >= CAP
    target = jnp.where(second, r - CAP, r)
    target = jnp.where(second == (t >= tok), target, -5).astype(jnp.float32)
    expand = jnp.where(er == jnp.where(el >= half, 2 * NC + 1, 2 * NC), 1.0, 0.0).astype(jnp.bfloat16)

    def widen(v):
        return lax.dot_general(
            v.astype(jnp.bfloat16), expand, (((0,), (0,)), ((), ())), preferred_element_type=jnp.float32
        )

    mix = jnp.where(widen(select(q_ref[0], pair)) == target, widen(select(q_ref[1], pair)), 0.0)
    mix = mix.astype(jnp.bfloat16)
    cols = 512
    for at in range(0, width, cols):
        got = jnp.dot(mix, back_ref[:, at : at + cols], preferred_element_type=jnp.float32)
        for n in range(2):
            new = got[n * tok : (n + 1) * tok] + sums[n][:, at : at + cols]
            outs[n][:, at : at + cols] = new.astype(outs[n].dtype)


def finish(q, pair, slab, sums, dtypes):
    tok = pair[0].shape[0]
    rows, width = slab.shape
    vmem = pl.BlockSpec(memory_space=pltpu.VMEM)
    return pl.pallas_call(
        finish_kernel,
        in_specs=[vmem] * 6,
        out_specs=[vmem] * 2,
        out_shape=[jax.ShapeDtypeStruct((tok, width), d) for d in dtypes],
        compiler_params=pltpu.CompilerParams(vmem_limit_bytes=16 * 1024 * 1024),
        cost_estimate=pl.CostEstimate(
            flops=2 * rows * 2 * tok * width,
            bytes_accessed=2 * (6 * tok + rows) * width,
            transcendentals=0,
        ),
        name="finish",
    )(slab, *sums, q, *pair)


def halves(refs):
    size = 2 * NC * CAP
    return [(ref, at) for ref in refs for at in range(0, ref.shape[0], size)]


def expert_kernel(count, ff, *refs):
    slabs, bundles, outs = refs[:count], refs[count : count + 2], refs[count + 2 :]
    width = slabs[0].shape[1]
    half = 2 * CAP
    for f, w in enumerate(bundles):
        lines = jnp.concatenate([s[at + half * f : at + half * (f + 1), :] for s, at in halves(slabs)], axis=0)
        hidden = []
        for at in range(0, ff, 256):
            gate = jnp.dot(lines, w[:width, at : at + 256], preferred_element_type=jnp.float32)
            up = jnp.dot(lines, w[:width, ff + at : ff + at + 256], preferred_element_type=jnp.float32)
            hidden.append((gate / (1.0 + jnp.exp(-gate)) * up).astype(jnp.bfloat16))
        whole = jnp.concatenate(hidden, axis=1)
        for at in range(0, width, 512):
            if at < 2 * ff:
                down = w[width : width + ff, at : at + 512]
            else:
                down = jnp.concatenate([w[width + ff :, 512 * i : 512 * (i + 1)] for i in range(ff // 256)], axis=0)
            got = jnp.dot(whole, down, preferred_element_type=jnp.float32)
            got = got.astype(jnp.bfloat16)
            for n, (o, to) in enumerate(halves(outs)):
                o[to + half * f : to + half * (f + 1), at : at + 512] = got[n * half : (n + 1) * half]


def expert(slabs, bundles, outs):
    count = len(slabs)
    rows = sum(s.shape[0] for s in slabs)
    width = slabs[0].shape[1]
    ff = bundles[0].shape[1] // 2
    vmem = pl.BlockSpec(memory_space=pltpu.VMEM)
    return pl.pallas_call(
        functools.partial(expert_kernel, count, ff),
        in_specs=[vmem] * (count + 2),
        out_specs=[vmem] * outs,
        out_shape=[jax.ShapeDtypeStruct((rows // outs, width), jnp.bfloat16)] * outs,
        compiler_params=pltpu.CompilerParams(vmem_limit_bytes=16 * 1024 * 1024),
        cost_estimate=pl.CostEstimate(
            flops=6 * rows * width * ff,
            bytes_accessed=4 * rows * width,
            transcendentals=rows * ff,
        ),
        name="expert",
    )(*slabs, *[pltpu.with_memory_space_constraint(w, pltpu.VMEM) for w in bundles])


def hold_kernel(wg, wu, wd, out_ref, mark_ref, sems):
    width, ff = wg.shape[1:]
    moves = [
        (wg.at[0], out_ref.at[pl.ds(0, width), pl.ds(0, ff)]),
        (wu.at[0], out_ref.at[pl.ds(0, width), pl.ds(ff, ff)]),
        (wd.at[0, :, pl.ds(0, 2 * ff)], out_ref.at[pl.ds(width, ff)]),
    ]
    for i in range(ff // 256):
        moves.append(
            (
                wd.at[0, pl.ds(256 * i, 256), pl.ds(2 * ff, 512)],
                out_ref.at[pl.ds(width + ff, 256), pl.ds(512 * i, 512)],
            )
        )
    copies = [pltpu.make_async_copy(a, b, sems.at[n]) for n, (a, b) in enumerate(moves)]
    for copy in copies:
        copy.start()
    mark_ref[...] = jnp.zeros_like(mark_ref)
    for copy in copies:
        copy.wait()


def hold(*weights):
    width, ff = weights[0].shape[1:]
    return pl.pallas_call(
        hold_kernel,
        in_specs=[pl.BlockSpec(memory_space=pl.ANY)] * 3,
        out_specs=[pl.BlockSpec(memory_space=pltpu.VMEM)] * 2,
        out_shape=[
            pltpu.VMEM((width + ff + 256, 2 * ff), weights[0].dtype),
            pltpu.VMEM((8, 128), jnp.float32),
        ],
        scratch_shapes=[pltpu.SemaphoreType.DMA((6,))],
        compiler_params=pltpu.CompilerParams(vmem_limit_bytes=4 * 1024 * 1024),
        cost_estimate=pl.CostEstimate(flops=0, bytes_accessed=4 * weights[0].size * 3, transcendentals=0),
        name="hold",
    )(*[pltpu.with_memory_space_constraint(w, pltpu.HBM) for w in weights])[0]


def per_device(tokens, expert_ids, gate_weights, w_gate, w_up, w_down):
    send = lambda v, pairs: lax.ppermute(v, "expert", pairs)
    after = lambda v, other: lax.optimization_barrier((v, other))[0]
    home, q = prep(expert_ids.T, gate_weights.T, tokens)
    moved = {j: send(home, spread_pairs(j)) for j in (1, 3, 2)}
    pairs = [[home, moved[2]], [moved[1], moved[3]]]
    bundle = hold(w_gate, w_up, w_down)

    near = pack((1, 3), q, pairs[0] + pairs[1])
    weights = [bundle, send(after(bundle, near[0]), swap_pairs())]
    arrived = {k: send(slab, deliver_pairs(k)) for k, slab in zip((1, 3), near)}
    stay, far = pack((0, 2), q, pairs[0] + pairs[1])
    backs = {}
    (backs[0],) = expert([stay], weights, 1)
    arrived[2] = send(after(far, arrived[3]), deliver_pairs(2))
    for k, slab in zip((1, 3), expert([arrived[1], arrived[3]], weights, 2)):
        backs[k] = send(slab, back(deliver_pairs(k)))
    halves2 = expert([arrived[2]], weights, 2)
    early = send(halves2[0], back(deliver_pairs(2)))
    late = send(after(halves2[1], (backs[1], backs[3])), back(deliver_pairs(2)))

    f32, bf16 = jnp.float32, jnp.bfloat16
    sums = combine((0, 1, 3), after(q, early), pairs[0] + pairs[1], [backs[k] for k in (0, 1, 3)], [], [f32] * 4)
    parts = {}
    for p, slab in ((0, early), (1, late)):
        kinds = (f32, bf16) if p == 0 else (bf16, bf16)
        parts[p] = finish(q, pairs[p], slab, sums[2 * p : 2 * p + 2], kinds)
    part0, part2 = parts[0]
    part1, part3 = parts[1]
    mixed = part0 + send(part2, back(spread_pairs(2))).astype(f32)
    mixed = lax.optimization_barrier(mixed)
    for j, part in ((3, part3), (1, part1)):
        mixed = mixed + send(part, back(spread_pairs(j))).astype(f32)
    return mixed.astype(bf16)


def solution(mesh):
    return jax.shard_map(
        per_device,
        mesh=mesh,
        in_specs=(
            P(("dp", "expert"), None),
            P(("dp", "expert"), None),
            P(("dp", "expert"), None),
            P("expert", None, None),
            P("expert", None, None),
            P("expert", None, None),
        ),
        out_specs=P(("dp", "expert"), None),
        check_vma=False,
    )
```

```python
import functools

import jax
import jax.numpy as jnp
from jax import lax
from jax.experimental import pallas as pl
from jax.experimental.pallas import tpu as pltpu
from jax.sharding import PartitionSpec as P

NX, NY, NC = 4, 4, 2
EXPERTS = NX * NY * NC
CAP = 40
EXTRA = 128
KF = 8


def index_of(x, y, c):
    return ((x % NX) * NY + (y % NY)) * NC + c


def spread_pairs(j):
    pairs = []
    for x in range(NX):
        for y in range(NY):
            pairs.append((index_of(x, y, 0), index_of(x + j, y, 0)))
            pairs.append((index_of(x, y, 1), index_of(x, y + j, 1)))
    return pairs


def deliver_pairs(k):
    pairs = []
    for x in range(NX):
        for y in range(NY):
            pairs.append((index_of(x, y, 0), index_of(x, y + k, 0)))
            pairs.append((index_of(x, y, 1), index_of(x + k, y, 1)))
    return pairs


def swap_pairs():
    return [(i, i ^ 1) for i in range(EXPERTS)]


def back(pairs):
    return [(b, a) for a, b in pairs]


def prep_kernel(ids_hbm, gw_hbm, tok_hbm, out_ref, q_ref, ids_ref, gw_ref, sems):
    top, tok = ids_ref.shape
    width = tok_hbm.shape[1]
    copies = [
        pltpu.make_async_copy(ids_hbm, ids_ref, sems.at[0]),
        pltpu.make_async_copy(gw_hbm, gw_ref, sems.at[1]),
        pltpu.make_async_copy(tok_hbm, out_ref.at[:, pl.ds(0, width)], sems.at[2]),
    ]
    for copy in copies:
        copy.start()
    row = lax.broadcasted_iota(jnp.int32, (tok, tok), 0)
    col = lax.broadcasted_iota(jnp.int32, (tok, tok), 1)
    earlier = jnp.where(row < col, 1.0, 0.0).astype(jnp.bfloat16)
    name = lax.broadcasted_iota(jnp.int32, (EXPERTS, tok), 0)
    chosen = jnp.zeros((EXPERTS, tok), jnp.float32)
    weight = jnp.zeros((EXPERTS, tok), jnp.float32)
    copies[0].wait()
    copies[1].wait()
    ids = ids_ref[...]
    gw = gw_ref[...]
    for k in range(top):
        hit = ids[k : k + 1, :] == name
        chosen = jnp.where(hit, 1.0, chosen)
        weight = jnp.where(hit, gw[k : k + 1, :], weight)
    count = jnp.dot(chosen.astype(jnp.bfloat16), earlier, preferred_element_type=jnp.float32)
    slot = jnp.where(chosen > 0.5, count, -1.0)
    blank = jnp.zeros((EXTRA - 2 * EXPERTS, tok), jnp.float32)
    table = jnp.concatenate([slot, weight, blank], axis=0)
    out_ref[:, width:] = table.T.astype(jnp.bfloat16)
    me = lax.axis_index("expert")
    x, y, c = me >> 3, (me >> 1) & 3, me & 1
    n = lax.broadcasted_iota(jnp.int32, (16, EXTRA), 0)
    spot = lax.broadcasted_iota(jnp.int32, (16, EXTRA), 1)
    k, f = n >> 1, n & 1
    along_y = x * (NY * NC) + ((y + k) & 3) * NC + ((c + f) & 1)
    along_x = ((x + k) & 3) * (NY * NC) + y * NC + ((c + f) & 1)
    mine = jnp.where(n < KF, jnp.where(c == 0, along_y, along_x), -EXTRA)
    q_ref[0] = jnp.where(mine == spot, 1.0, 0.0).astype(jnp.bfloat16)
    q_ref[1] = jnp.where(mine + EXPERTS == spot, 1.0, 0.0).astype(jnp.bfloat16)
    copies[2].wait()


def prep(ids, gw, tokens):
    tok, width = tokens.shape
    hbm = pl.BlockSpec(memory_space=pl.ANY)
    return pl.pallas_call(
        prep_kernel,
        in_specs=[hbm, hbm, hbm],
        out_specs=[pl.BlockSpec(memory_space=pltpu.VMEM)] * 2,
        out_shape=[
            pltpu.VMEM((tok, width + EXTRA), jnp.bfloat16),
            pltpu.VMEM((2, 16, EXTRA), jnp.bfloat16),
        ],
        scratch_shapes=[
            pltpu.VMEM(ids.shape, ids.dtype),
            pltpu.VMEM(gw.shape, gw.dtype),
            pltpu.SemaphoreType.DMA((3,)),
        ],
        compiler_params=pltpu.CompilerParams(vmem_limit_bytes=4 * 1024 * 1024),
        cost_estimate=pl.CostEstimate(flops=2 * EXPERTS * tok**2, bytes_accessed=4 * tok * width, transcendentals=0),
        name="prep",
    )(*[pltpu.with_memory_space_constraint(v, pltpu.HBM) for v in (ids, gw, tokens)])


def select(q, blocks):
    width = blocks[0].shape[1] - EXTRA
    return jnp.concatenate(
        [
            lax.dot_general(q, b[:, width:], (((1,), (1,)), ((), ())), preferred_element_type=jnp.float32)
            for b in blocks
        ],
        axis=1,
    )


def pack_kernel(which, q_ref, *refs):
    outs = refs[len(refs) - len(which) :]
    blocks = [refs[n] for n in (0, 3, 2, 1)]
    tok = blocks[0].shape[0]
    width = outs[0].shape[1]
    q = q_ref[0]
    half = 2 * CAP
    r = lax.broadcasted_iota(jnp.int32, (half, 2 * tok), 0)
    t = lax.broadcasted_iota(jnp.int32, (half, 2 * tok), 1)
    second = r >= CAP
    target = jnp.where(second, r - CAP, r)
    target = jnp.where(second == (t >= tok), target, -5).astype(jnp.float32)
    cols = 512
    for p in range(len(blocks) // 2):
        pair = blocks[2 * p : 2 * p + 2]
        slots = select(q, pair)
        pick = jnp.concatenate(
            [
                jnp.where(slots[NC * k + f : NC * k + f + 1, :] == target, 1.0, 0.0).astype(jnp.bfloat16)
                for k in which
                for f in range(NC)
            ],
            axis=0,
        )
        for at in range(0, width, cols):
            block = jnp.concatenate([b[:, at : at + cols] for b in pair], axis=0)
            got = jnp.dot(pick, block, preferred_element_type=jnp.float32).astype(jnp.bfloat16)
            for n, o in enumerate(outs):
                o[2 * half * p : 2 * half * (p + 1), at : at + cols] = got[2 * half * n : 2 * half * (n + 1), :]


def pack(which, q, blocks):
    tok = blocks[0].shape[0]
    width = blocks[0].shape[1] - EXTRA
    count = len(which)
    rows = NC * len(blocks) * CAP
    vmem = pl.BlockSpec(memory_space=pltpu.VMEM)
    return pl.pallas_call(
        functools.partial(pack_kernel, which),
        in_specs=[vmem] * (1 + len(blocks)),
        out_specs=[vmem] * count,
        out_shape=[jax.ShapeDtypeStruct((rows, width), jnp.bfloat16)] * count,
        compiler_params=pltpu.CompilerParams(vmem_limit_bytes=16 * 1024 * 1024),
        cost_estimate=pl.CostEstimate(
            flops=2 * rows * count * 2 * tok * width,
            bytes_accessed=2 * (len(blocks) * tok + rows * count) * width,
            transcendentals=0,
        ),
        name="pack",
    )(q, *[blocks[n] for n in (0, 3, 2, 1)])


def combine_kernel(which, q_ref, *refs):
    count = len(which)
    blocks, backs, sums, outs = refs[:4], refs[4 : 4 + count], refs[4 + count : -4], refs[-4:]
    blocks = [blocks[n] for n in (0, 3, 2, 1)]
    tok, width = outs[0].shape
    half = 2 * CAP
    places = [NC * k + f for k in which for f in range(NC)]
    span = half * len(places)
    lane = lax.broadcasted_iota(jnp.int32, (2 * tok, span), 1)
    part = jnp.zeros((2 * tok, span), jnp.int32)
    er = lax.broadcasted_iota(jnp.int32, (16, span), 0)
    el = lax.broadcasted_iota(jnp.int32, (16, span), 1)
    ep = jnp.full((16, span), places[0], jnp.int32)
    for n in range(1, len(places)):
        part = jnp.where(lane >= half * n, half * n, part)
        ep = jnp.where(el >= half * n, places[n], ep)
    r = lane - part
    t = lax.broadcasted_iota(jnp.int32, (2 * tok, span), 0)
    second = r >= CAP
    target = jnp.where(second, r - CAP, r)
    target = jnp.where(second == (t >= tok), target, -5).astype(jnp.float32)
    expand = jnp.where(er == ep, 1.0, 0.0).astype(jnp.bfloat16)

    def widen(v):
        return lax.dot_general(
            v.astype(jnp.bfloat16), expand, (((0,), (0,)), ((), ())), preferred_element_type=jnp.float32
        )

    cols = 512
    for p in range(2):
        pair = blocks[2 * p : 2 * p + 2]
        mix = jnp.where(widen(select(q_ref[0], pair)) == target, widen(select(q_ref[1], pair)), 0.0)
        mix = mix.astype(jnp.bfloat16)
        for at in range(0, width, cols):
            rows = jnp.concatenate([b[2 * half * p : 2 * half * (p + 1), at : at + cols] for b in backs], axis=0)
            got = jnp.dot(mix, rows, preferred_element_type=jnp.float32)
            for n in range(2):
                new = got[n * tok : (n + 1) * tok]
                if sums:
                    new = new + sums[2 * p + n][:, at : at + cols]
                outs[2 * p + n][:, at : at + cols] = new.astype(outs[2 * p + n].dtype)


def combine(which, q, blocks, backs, sums, dtypes):
    tok = blocks[0].shape[0]
    rows, width = backs[0].shape
    vmem = pl.BlockSpec(memory_space=pltpu.VMEM)
    return pl.pallas_call(
        functools.partial(combine_kernel, which),
        in_specs=[vmem] * (5 + len(backs) + len(sums)),
        out_specs=[vmem] * 4,
        out_shape=[jax.ShapeDtypeStruct((tok, width), d) for d in dtypes],
        compiler_params=pltpu.CompilerParams(vmem_limit_bytes=16 * 1024 * 1024),
        cost_estimate=pl.CostEstimate(
            flops=2 * len(which) * rows * 2 * tok * width,
            bytes_accessed=2 * (6 * tok + len(which) * rows) * width,
            transcendentals=0,
        ),
        name="combine",
    )(q, *[blocks[n] for n in (0, 3, 2, 1)], *backs, *sums)


def finish_kernel(back_ref, *refs):
    sums, q_ref, pair, outs = refs[:2], refs[2], refs[3:5], refs[5:]
    tok, width = outs[0].shape
    half = 2 * CAP
    span = half * NC
    lane = lax.broadcasted_iota(jnp.int32, (2 * tok, span), 1)
    er = lax.broadcasted_iota(jnp.int32, (16, span), 0)
    el = lax.broadcasted_iota(jnp.int32, (16, span), 1)
    r = jnp.where(lane >= half, lane - half, lane)
    t = lax.broadcasted_iota(jnp.int32, (2 * tok, span), 0)
    second = r >= CAP
    target = jnp.where(second, r - CAP, r)
    target = jnp.where(second == (t >= tok), target, -5).astype(jnp.float32)
    expand = jnp.where(er == jnp.where(el >= half, 2 * NC + 1, 2 * NC), 1.0, 0.0).astype(jnp.bfloat16)

    def widen(v):
        return lax.dot_general(
            v.astype(jnp.bfloat16), expand, (((0,), (0,)), ((), ())), preferred_element_type=jnp.float32
        )

    mix = jnp.where(widen(select(q_ref[0], pair)) == target, widen(select(q_ref[1], pair)), 0.0)
    mix = mix.astype(jnp.bfloat16)
    cols = 512
    for at in range(0, width, cols):
        got = jnp.dot(mix, back_ref[:, at : at + cols], preferred_element_type=jnp.float32)
        for n in range(2):
            new = got[n * tok : (n + 1) * tok] + sums[n][:, at : at + cols]
            outs[n][:, at : at + cols] = new.astype(outs[n].dtype)


def finish(q, pair, slab, sums, dtypes):
    tok = pair[0].shape[0]
    rows, width = slab.shape
    vmem = pl.BlockSpec(memory_space=pltpu.VMEM)
    return pl.pallas_call(
        finish_kernel,
        in_specs=[vmem] * 6,
        out_specs=[vmem] * 2,
        out_shape=[jax.ShapeDtypeStruct((tok, width), d) for d in dtypes],
        compiler_params=pltpu.CompilerParams(vmem_limit_bytes=16 * 1024 * 1024),
        cost_estimate=pl.CostEstimate(
            flops=2 * rows * 2 * tok * width,
            bytes_accessed=2 * (6 * tok + rows) * width,
            transcendentals=0,
        ),
        name="finish",
    )(slab, *sums, q, *pair)


def halves(refs):
    size = 2 * NC * CAP
    return [(ref, at) for ref in refs for at in range(0, ref.shape[0], size)]


def expert_kernel(count, ff, *refs):
    slabs, bundles, outs = refs[:count], refs[count : count + 2], refs[count + 2 :]
    width = slabs[0].shape[1]
    half = 2 * CAP
    for f, w in enumerate(bundles):
        lines = jnp.concatenate([s[at + half * f : at + half * (f + 1), :] for s, at in halves(slabs)], axis=0)
        hidden = []
        for at in range(0, ff, 256):
            gate = jnp.dot(lines, w[:width, at : at + 256], preferred_element_type=jnp.float32)
            up = jnp.dot(lines, w[:width, ff + at : ff + at + 256], preferred_element_type=jnp.float32)
            hidden.append((gate / (1.0 + jnp.exp(-gate)) * up).astype(jnp.bfloat16))
        whole = jnp.concatenate(hidden, axis=1)
        for at in range(0, width, 512):
            if at < 2 * ff:
                down = w[width : width + ff, at : at + 512]
            else:
                down = jnp.concatenate([w[width + ff :, 512 * i : 512 * (i + 1)] for i in range(ff // 256)], axis=0)
            got = jnp.dot(whole, down, preferred_element_type=jnp.float32)
            got = got.astype(jnp.bfloat16)
            for n, (o, to) in enumerate(halves(outs)):
                o[to + half * f : to + half * (f + 1), at : at + 512] = got[n * half : (n + 1) * half]


def expert(slabs, bundles, outs):
    count = len(slabs)
    rows = sum(s.shape[0] for s in slabs)
    width = slabs[0].shape[1]
    ff = bundles[0].shape[1] // 2
    vmem = pl.BlockSpec(memory_space=pltpu.VMEM)
    return pl.pallas_call(
        functools.partial(expert_kernel, count, ff),
        in_specs=[vmem] * (count + 2),
        out_specs=[vmem] * outs,
        out_shape=[jax.ShapeDtypeStruct((rows // outs, width), jnp.bfloat16)] * outs,
        compiler_params=pltpu.CompilerParams(vmem_limit_bytes=16 * 1024 * 1024),
        cost_estimate=pl.CostEstimate(
            flops=6 * rows * width * ff,
            bytes_accessed=4 * rows * width,
            transcendentals=rows * ff,
        ),
        name="expert",
    )(*slabs, *[pltpu.with_memory_space_constraint(w, pltpu.VMEM) for w in bundles])


def hold_kernel(wg, wu, wd, out_ref, mark_ref, sems):
    width, ff = wg.shape[1:]
    moves = [
        (wg.at[0], out_ref.at[pl.ds(0, width), pl.ds(0, ff)]),
        (wu.at[0], out_ref.at[pl.ds(0, width), pl.ds(ff, ff)]),
        (wd.at[0, :, pl.ds(0, 2 * ff)], out_ref.at[pl.ds(width, ff)]),
    ]
    for i in range(ff // 256):
        moves.append(
            (
                wd.at[0, pl.ds(256 * i, 256), pl.ds(2 * ff, 512)],
                out_ref.at[pl.ds(width + ff, 256), pl.ds(512 * i, 512)],
            )
        )
    copies = [pltpu.make_async_copy(a, b, sems.at[n]) for n, (a, b) in enumerate(moves)]
    for copy in copies:
        copy.start()
    mark_ref[...] = jnp.zeros_like(mark_ref)
    for copy in copies:
        copy.wait()


def hold(*weights):
    width, ff = weights[0].shape[1:]
    return pl.pallas_call(
        hold_kernel,
        in_specs=[pl.BlockSpec(memory_space=pl.ANY)] * 3,
        out_specs=[pl.BlockSpec(memory_space=pltpu.VMEM)] * 2,
        out_shape=[
            pltpu.VMEM((width + ff + 256, 2 * ff), weights[0].dtype),
            pltpu.VMEM((8, 128), jnp.float32),
        ],
        scratch_shapes=[pltpu.SemaphoreType.DMA((6,))],
        compiler_params=pltpu.CompilerParams(vmem_limit_bytes=4 * 1024 * 1024),
        cost_estimate=pl.CostEstimate(flops=0, bytes_accessed=4 * weights[0].size * 3, transcendentals=0),
        name="hold",
    )(*[pltpu.with_memory_space_constraint(w, pltpu.HBM) for w in weights])[0]


def per_device(tokens, expert_ids, gate_weights, w_gate, w_up, w_down):
    send = lambda v, pairs: lax.ppermute(v, "expert", pairs)
    after = lambda v, other: lax.optimization_barrier((v, other))[0]
    home, q = prep(expert_ids.T, gate_weights.T, tokens)
    moved = {j: send(home, spread_pairs(j)) for j in (1, 3, 2)}
    pairs = [[home, moved[2]], [moved[1], moved[3]]]
    bundle = hold(w_gate, w_up, w_down)

    near = pack((1, 3), q, pairs[0] + pairs[1])
    weights = [bundle, send(after(bundle, near[0]), swap_pairs())]
    arrived = {k: send(slab, deliver_pairs(k)) for k, slab in zip((1, 3), near)}
    stay, far = pack((0, 2), q, pairs[0] + pairs[1])
    backs = {}
    (backs[0],) = expert([stay], weights, 1)
    arrived[2] = send(after(far, arrived[3]), deliver_pairs(2))
    for k, slab in zip((1, 3), expert([arrived[1], arrived[3]], weights, 2)):
        backs[k] = send(slab, back(deliver_pairs(k)))
    halves2 = expert([arrived[2]], weights, 2)
    early = send(halves2[0], back(deliver_pairs(2)))
    late = send(after(halves2[1], backs[0]), back(deliver_pairs(2)))

    f32, bf16 = jnp.float32, jnp.bfloat16
    sums = combine((0, 1, 3), after(q, early), pairs[0] + pairs[1], [backs[k] for k in (0, 1, 3)], [], [f32] * 4)
    parts = {}
    for p, slab in ((0, early), (1, late)):
        kinds = (f32, bf16) if p == 0 else (bf16, bf16)
        parts[p] = finish(q, pairs[p], slab, sums[2 * p : 2 * p + 2], kinds)
    part0, part2 = parts[0]
    part1, part3 = parts[1]
    mixed = part0 + send(part2, back(spread_pairs(2))).astype(f32)
    mixed = lax.optimization_barrier(mixed)
    for j, part in ((3, part3), (1, part1)):
        mixed = mixed + send(part, back(spread_pairs(j))).astype(f32)
    return mixed.astype(bf16)


def solution(mesh):
    return jax.shard_map(
        per_device,
        mesh=mesh,
        in_specs=(
            P(("dp", "expert"), None),
            P(("dp", "expert"), None),
            P(("dp", "expert"), None),
            P("expert", None, None),
            P("expert", None, None),
            P("expert", None, None),
        ),
        out_specs=P(("dp", "expert"), None),
        check_vma=False,
    )
```
